32 devices in a mesh: gx: 4 (over y, core), gy: 2 (over x), gz: 4 (over z).
Axes of the slice: x: 2, y: 2, z: 4, core: 2. Of those that a mesh axis runs over, the one named last changes fastest.
Arguments:
- displacement: float32 [3, 8, 16, 512], P(None, 'gx', 'gy', 'gz'), may hold values from -6 to 6
- displacement_old: float32 [3, 8, 16, 512], P(None, 'gx', 'gy', 'gz'), may hold values from -6 to 6
- visco_state: float32 [6, 6, 8, 16, 512], P(None, None, 'gx', 'gy', 'gz'), may hold values from -3 to 3
- energy_max: float32 [8, 16, 512], P('gx', 'gy', 'gz'), may hold values from 0.1 to 4
- region: int32 [8, 16, 512], P('gx', 'gy', 'gz'), may hold values from 0 to 3
- dirichlet: int32 [8, 16, 512], P('gx', 'gy', 'gz'), may hold values 0 or 1
- prony_moduli: float32 [4, 6], replicated, may hold values from 0.02 to 0.12
- prony_times: float32 [4, 6], replicated, may hold values from 0.05 to 50
- shear_modulus: float32 [4], replicated, may hold values from 0.5 to 2
- mullins_ratio: float32 [4], replicated, may hold values from 1.5 to 4
- mullins_scale: float32 [4], replicated, may hold values from 0.3 to 3
Outputs:
- stress: float32 [6, 8, 16, 512], P(None, 'gx', 'gy', 'gz')
- visco_next: float32 [6, 6, 8, 16, 512], P(None, None, 'gx', 'gy', 'gz')
- energy_next: float32 [8, 16, 512], P('gx', 'gy', 'gz')
- damage_field: float32 [8, 16, 512], P('gx', 'gy', 'gz')
- residual: float32 [8, 16, 512], P('gx', 'gy', 'gz')
The draws below stay inside these ranges and needn't reach their ends.
All inputs are finite; a program needn't handle non-finite values. No bound on the sum of `dirichlet` on one device may be relied on, other than what follows from the above.
Results may differ from the reference program's by a relative error of at most 0.0003.
Values sent between devices are 32-bit elements; how exact they have to be, the bound alone decides.
No kernel may reach another device: no remote copies, remote signals or barrier semaphores. Data moves between devices by JAX's collectives and lax.ppermute only.
A program may use at most 64 MiB of HBM per device.

```python
import math
import jax
import jax.numpy as jnp
from jax import lax

TERMS = 6
REGIONS = 4
ITERS = 4
NX = 8
NY = 16
NZ = 512


def with_ends(entries, stream_key, least, top_value):
    extent = entries.shape
    spot = [jax.random.randint(jax.random.fold_in(stream_key, axis), (), 0, extent[axis]) for axis in range(len(extent))]
    entries = entries.at[tuple(spot)].set(least)
    longest = extent.index(max(extent))
    spot[longest] = (spot[longest] + 1) % extent[longest]
    return entries.at[tuple(spot)].set(top_value)


def levels(own_key, dims, shards, smallest, high):
    gain, own = 1.0, jax.random.fold_in(own_key, 6)
    for axis_at, shards_of in shards:
        heights = jnp.exp(jax.random.uniform(jax.random.fold_in(own, axis_at), (shards_of,), jnp.float32, smallest / len(shards), high / len(shards)))
        gain = gain * jnp.repeat(heights, dims[axis_at] // shards_of).reshape([-1 if axis == axis_at else 1 for axis in range(len(dims))])
    return gain


def normal_values(stream_key, extent, spread, most, split=(), held_as=jnp.bfloat16):
    result = spread * jax.random.normal(stream_key, extent, jnp.float32)
    if split:
        result = result * levels(stream_key, extent, split, -0.22, 0.18)
    return jnp.clip(result, -most, most).astype(held_as)


def setup_inputs(seed: int = 0) -> dict:
    seeds = jax.random.split(jax.random.key(seed), 12)
    return {
        "displacement": normal_values(seeds[0], (3, NX, NY, NZ), 1.0, 6.0, ((1, 4), (2, 2), (3, 4)), jnp.float32),
        "displacement_old": normal_values(seeds[1], (3, NX, NY, NZ), 1.0, 6.0, ((1, 4), (2, 2), (3, 4)), jnp.float32),
        "visco_state": normal_values(seeds[2], (TERMS, 6, NX, NY, NZ), 0.3, 3.0, ((2, 4), (3, 2), (4, 4)), jnp.float32),
        "energy_max": jnp.clip(jnp.exp(math.log(4.0) - 3.6888794 * jax.random.uniform(seeds[3], (NX, NY, NZ), jnp.float32) ** levels(seeds[3], (NX, NY, NZ), ((0, 4), (1, 2), (2, 4)), -0.2, 0.2)), 0.1, 4.0),
        "region": with_ends(jax.random.randint(seeds[4], (NX, NY, NZ), 0, REGIONS), jax.random.fold_in(seeds[4], 1), 0, REGIONS - 1).astype(jnp.int32),
        "dirichlet": with_ends((jax.random.randint(seeds[5], (NX, NY, NZ), 0, 8) < 1).astype(jnp.int32), jax.random.fold_in(seeds[5], 1), 0, 1),
        "prony_moduli": jnp.clip(jax.random.uniform(seeds[6], (REGIONS, TERMS), jnp.float32, 0.02, 0.12), 0.02, 0.12),
        "prony_times": jnp.clip(jnp.exp(jax.random.uniform(seeds[7], (REGIONS, TERMS), jnp.float32, math.log(0.05), math.log(50.0))), 0.05, 50.0),
        "shear_modulus": jnp.clip(jnp.exp(jax.random.uniform(seeds[8], (REGIONS,), jnp.float32, math.log(0.5), math.log(2.0))), 0.5, 2.0),
        "mullins_ratio": jnp.clip(jax.random.uniform(seeds[9], (REGIONS,), jnp.float32, 1.5, 4.0), 1.5, 4.0),
        "mullins_scale": jnp.clip(jnp.exp(jax.random.uniform(seeds[10], (REGIONS,), jnp.float32, math.log(0.3), math.log(3.0))), 0.3, 3.0),
    }


LENGTH_SQUARED = 4.0


def neighbours(field):
    next_x = jnp.roll(field, -1, axis=-3)
    prev_x = jnp.roll(field, 1, axis=-3)
    padding = [(0, 0)] * (field.ndim - 2) + [(1, 1), (1, 1)]
    padded = jnp.pad(field, padding)
    next_y = padded[..., 2:, 1:-1]
    prev_y = padded[..., :-2, 1:-1]
    next_z = padded[..., 1:-1, 2:]
    prev_z = padded[..., 1:-1, :-2]
    return next_x, prev_x, next_y, prev_y, next_z, prev_z


def deviator(held):
    next_x, prev_x, next_y, prev_y, next_z, prev_z = neighbours(held)
    grad_x = 0.5 * (next_x - prev_x)
    grad_y = 0.5 * (next_y - prev_y)
    grad_z = 0.5 * (next_z - prev_z)
    strain_xx = grad_x[0]
    strain_yy = grad_y[1]
    strain_zz = grad_z[2]
    strain_yz = 0.5 * (grad_z[1] + grad_y[2])
    strain_xz = 0.5 * (grad_z[0] + grad_x[2])
    strain_xy = 0.5 * (grad_y[0] + grad_x[1])
    trace_third = (strain_xx + strain_yy + strain_zz) / 3.0
    return jnp.stack([strain_xx - trace_third, strain_yy - trace_third, strain_zz - trace_third, strain_yz, strain_xz, strain_xy])


def contract(dev):
    return dev[0] * dev[0] + dev[1] * dev[1] + dev[2] * dev[2] + 2.0 * (dev[3] * dev[3] + dev[4] * dev[4] + dev[5] * dev[5])


def operate(field):
    next_x, prev_x, next_y, prev_y, next_z, prev_z = neighbours(field)
    beside_all = next_x + prev_x + next_y + prev_y + next_z + prev_z
    return (1.0 + 6.0 * LENGTH_SQUARED) * field - LENGTH_SQUARED * beside_all


def reference(displacement, displacement_old, visco_state, energy_max, region, dirichlet, prony_moduli, prony_times, shear_modulus, mullins_ratio, mullins_scale):
    free_share = (1 - dirichlet).astype(jnp.float32)
    dev_new = deviator(displacement * free_share[None])
    dev_old = deviator(displacement_old * free_share[None])
    shear_cells = shear_modulus[region]
    energy = shear_cells * contract(dev_new)
    energy_next = jnp.maximum(energy_max, energy)
    softening = 1.0 - jax.scipy.special.erf((energy_next - energy) / mullins_scale[region]) / mullins_ratio[region]
    stress_jump = 2.0 * shear_cells * (dev_new - dev_old)

    def prony_term(term_index):
        relax_time = prony_times[:, term_index][region]
        modulus = prony_moduli[:, term_index][region]
        decays = jnp.exp(-1.0 / relax_time)
        weight = modulus * (1.0 - decays) * relax_time
        return decays * visco_state[term_index] + weight * stress_jump

    visco_next = lax.map(prony_term, jnp.arange(TERMS))
    long_term = 1.0 - jnp.sum(prony_moduli, axis=1)[region]
    stress = softening * (long_term * 2.0 * shear_cells * dev_new + jnp.sum(visco_next, axis=0))
    local_drive = softening * energy

    damage_field = jnp.zeros_like(local_drive)
    residual = local_drive
    direction = local_drive
    norm_now = jnp.sum(residual * residual)
    for iteration in range(ITERS):
        image = operate(direction)
        alpha_now = norm_now / jnp.sum(direction * image)
        damage_field = damage_field + alpha_now * direction
        residual = residual - alpha_now * image
        norm_next = jnp.sum(residual * residual)
        direction = residual + (norm_next / norm_now) * direction
        norm_now = norm_next
    return stress, visco_next, energy_next, damage_field, residual
```

```python
import functools
import typing

import jax
import jax.numpy as jnp
import numpy as np
from jax import lax
from jax.experimental import pallas as pl
from jax.experimental.pallas import tpu as pltpu
from jax.sharding import PartitionSpec as P

ITERS = 4
LENGTH_SQUARED = 4.0

SHIFTS = (0.0, 6.0, 1.5, 9.0)
PAIRS = [(i, j) for i in range(ITERS + 1) for j in range(i, ITERS + 1) if i < ITERS]

WIDE, NARROW = 5, 3
REACHES = (ITERS + 1,) * WIDE + (1,) * NARROW
FIELDS = WIDE + NARROW
MB = 1 << 20


class Geometry(typing.NamedTuple):
    lx: int
    ly: int
    lz: int
    gx: int
    gy: int
    gz: int
    hops_x: int
    hops_y: int
    full: bool

    @property
    def bx(self):
        return self.gx if self.full else 2 * self.hops_x + 1

    @property
    def by(self):
        return self.gy if self.full else 2 * self.hops_y + 1


def geometry(block):
    lx, ly, lz = block
    gx, gy, gz = (lax.axis_size(name) for name in ("gx", "gy", "gz"))
    hops_x, hops_y = -(-(ITERS + 1) // lx), -(-(ITERS + 1) // ly)
    full = gx <= 2 * hops_x + 1 and gy <= hops_y + 1
    return Geometry(lx, ly, lz, gx, gy, gz, hops_x, hops_y, full)


def places(geo):
    result, tile, at = [], 0, 0
    for reach in REACHES:
        for _ in range(geo.lx):
            if at + 2 * reach > geo.lz:
                tile, at = tile + 1, 0
            result.append((tile, at + reach))
            at += 2 * reach
    return result, tile + 1


def left_lanes(geo):
    spots, tiles = places(geo)
    mask = np.zeros((tiles, 1, geo.lz), np.bool_)
    for index, (tile, centre) in enumerate(spots):
        mask[tile, 0, centre - REACHES[index // geo.lx] : centre] = True
    return mask


def iota(shape, dim):
    return lax.broadcasted_iota(jnp.int32, shape, dim)


def pack_kernel(geo, new, old, energy_max, region, dirichlet, main, slab):
    spots, tiles = places(geo)
    lane = iota((geo.ly, geo.lz), 1)
    edges = [jnp.zeros((geo.ly, geo.lz), jnp.float32)] * tiles
    for i in range(geo.lx):
        share = (1 - dirichlet[i]).astype(jnp.float32)
        values = [new[a, i] * share for a in range(3)]
        values += [energy_max[i], region[i].astype(jnp.float32)]
        values += [old[a, i] * share for a in range(3)]
        for f, value in enumerate(values):
            main[f * geo.lx + i] = value
            tile, centre = spots[f * geo.lx + i]
            inside = (lane >= centre - REACHES[f]) & (lane < centre + REACHES[f])
            edges[tile] = jnp.where(inside, pltpu.roll(value, centre, 1), edges[tile])
    for tile in range(tiles):
        slab[tile] = edges[tile]


def lookup(table, label):
    value = jnp.full(label.shape, table[table.shape[0] - 1], jnp.float32)
    for index in range(table.shape[0] - 1):
        value = jnp.where(label == index, table[index], value)
    return value


def deviator(grad):
    trace_third = (grad[0][0] + grad[1][1] + grad[2][2]) / 3.0
    return [
        grad[0][0] - trace_third,
        grad[1][1] - trace_third,
        grad[2][2] - trace_third,
        0.5 * (grad[1][2] + grad[2][1]),
        0.5 * (grad[0][2] + grad[2][0]),
        0.5 * (grad[1][0] + grad[0][1]),
    ]


def contract(dev):
    return (
        dev[0] * dev[0]
        + dev[1] * dev[1]
        + dev[2] * dev[2]
        + 2.0 * (dev[3] * dev[3] + dev[4] * dev[4] + dev[5] * dev[5])
    )


def soften(energy, energy_next, scale, ratio):
    return 1.0 - lax.erf((energy_next - energy) / scale) / ratio


def basis_kernel(geo, shear, ratio, scale, blocks, basis, dev_own, grams, held, field, dev_all):
    lx, ly, lz = geo.lx, geo.ly, geo.lz
    planes, rows, lanes = geo.bx * lx, geo.by * ly, 2 * lz
    spots, _ = places(geo)
    row, lane = iota((rows, lanes), 0), iota((rows, lanes), 1)
    index_y, index_z = lax.axis_index("gy"), lax.axis_index("gz")
    if geo.full:
        grid_row = row
        own_x, own_y = lax.axis_index("gx") * lx, pl.multiple_of(index_y * ly, ly)
    else:
        grid_row = index_y * ly + jnp.where(row < (1 + geo.hops_y) * ly, row, row - rows)
        own_x, own_y = 0, 0
    end_y, start_y = grid_row == geo.gy * ly - 1, grid_row == 0
    end_z = (lane == lz - 1) & (index_z == geo.gz - 1)
    start_z = (lane == 0) & (index_z == 0)

    def whole_plane(f, p):
        tile, centre = spots[f * lx + p % lx]
        parts = []
        for b in range(geo.by):
            at = (p // lx) * geo.by + b
            edge = pltpu.roll(blocks[at, FIELDS * lx + tile], lz - centre, 1)
            parts.append(jnp.concatenate([blocks[at, f * lx + p % lx], edge], axis=1))
        return jnp.concatenate(parts, axis=0)

    def beside(value):
        next_y = jnp.where(end_y, 0.0, pltpu.roll(value, rows - 1, 0))
        prev_y = jnp.where(start_y, 0.0, pltpu.roll(value, 1, 0))
        next_z = jnp.where(end_z, 0.0, pltpu.roll(value, lanes - 1, 1))
        prev_z = jnp.where(start_z, 0.0, pltpu.roll(value, 1, 1))
        return next_y, prev_y, next_z, prev_z

    for p in range(planes):
        for a in range(3):
            held[a, p] = whole_plane(a, p)
    for p in range(planes):
        grad = []
        for a in range(3):
            next_y, prev_y, next_z, prev_z = beside(held[a, p])
            next_x, prev_x = held[a, (p + 1) % planes], held[a, (p - 1) % planes]
            grad.append([0.5 * (next_x - prev_x), 0.5 * (next_y - prev_y), 0.5 * (next_z - prev_z)])
        dev = deviator(grad)
        for k in range(6):
            dev_all[k, p] = dev[k][:, :lz]
        label = whole_plane(4, p)
        energy = lookup(shear, label) * contract(dev)
        energy_next = jnp.maximum(whole_plane(3, p), energy)
        softening = soften(energy, energy_next, lookup(scale, label), lookup(ratio, label))
        field[0, p] = softening * energy
    for j, shift in enumerate(SHIFTS):
        for p in range(planes):
            value = field[j, p]
            next_y, prev_y, next_z, prev_z = beside(value)
            next_x, prev_x = field[j, (p + 1) % planes], field[j, (p - 1) % planes]
            image = (value - next_x) + (value - prev_x)
            image += (value - next_y) + (value - prev_y)
            image += (value - next_z) + (value - prev_z)
            field[j + 1, p] = image - shift * value if shift else image

    grams[...] = jnp.zeros(grams.shape, jnp.float32)
    sums = [jnp.zeros((ly, lz), jnp.float32)] * len(PAIRS)
    for p in range(planes if geo.full else lx):
        for b in range(geo.by if geo.full else 1):
            own = [field[j, p, b * ly : (b + 1) * ly, :lz] for j in range(ITERS + 1)]
            sums = [total + own[i] * own[j] for total, (i, j) in zip(sums, PAIRS)]
    for k, total in enumerate(sums):
        grams[k : k + 1, :] = jnp.sum(total, axis=0, keepdims=True)
    for i in range(lx):
        for j in range(ITERS + 1):
            basis[j, i] = field[j, own_x + i, pl.ds(own_y, ly), :lz]
        for k in range(6):
            dev_own[k, i] = dev_all[k, own_x + i, pl.ds(own_y, ly), :]


def visco_kernel(
    geo, moduli, times, shear, ratio, scale, blocks, dev_own, visco, energy_max, region, stress, visco_next, energy_next
):
    lx, ly, lz = geo.lx, geo.ly, geo.lz
    spots, _ = places(geo)
    row, lane = iota((ly, lz), 0), iota((ly, lz), 1)
    index_y = lax.axis_index("gy")
    own_x, own_y = (lax.axis_index("gx"), index_y) if geo.full else (0, 0)

    def block(step_x, step_y):
        return lax.rem(own_x + step_x + geo.bx, geo.bx) * geo.by + lax.rem(own_y + step_y + geo.by, geo.by)

    here, right, left, above, below = block(0, 0), block(1, 0), block(-1, 0), block(0, 1), block(0, -1)
    regions, terms = moduli.shape
    for i in range(lx):
        grad = []
        for a in range(3):
            at = (WIDE + a) * lx + i
            value = blocks[here, at]
            next_x = blocks[here, at + 1] if i + 1 < lx else blocks[right, at + 1 - lx]
            prev_x = blocks[here, at - 1] if i else blocks[left, at + lx - 1]
            first = jnp.where(index_y == geo.gy - 1, 0.0, blocks[above, at])
            last = jnp.where(index_y == 0, 0.0, blocks[below, at])
            next_y = pltpu.roll(jnp.where(row == 0, first, value), ly - 1, 0)
            prev_y = pltpu.roll(jnp.where(row == ly - 1, last, value), 1, 0)
            tile, centre = spots[at]
            edge = blocks[here, FIELDS * lx + tile]
            next_z = jnp.where(lane == lz - 1, pltpu.roll(edge, lz - 1 - centre, 1), pltpu.roll(value, lz - 1, 1))
            prev_z = jnp.where(lane == 0, pltpu.roll(edge, lz + 1 - centre, 1), pltpu.roll(value, 1, 1))
            grad.append([0.5 * (next_x - prev_x), 0.5 * (next_y - prev_y), 0.5 * (next_z - prev_z)])
        dev_old = deviator(grad)
        dev_new = [dev_own[k, i] for k in range(6)]
        label = region[i]
        masks = [label == index for index in range(regions - 1)]

        def choose(entries):
            value = jnp.full(label.shape, entries[-1], jnp.float32)
            for mask, entry in zip(masks, entries):
                value = jnp.where(mask, entry, value)
            return value

        shear_cells = choose([shear[r] for r in range(regions)])
        energy = shear_cells * contract(dev_new)
        energy_after = jnp.maximum(energy_max[i], energy)
        energy_next[i] = energy_after
        softening = soften(
            energy,
            energy_after,
            choose([scale[r] for r in range(regions)]),
            choose([ratio[r] for r in range(regions)]),
        )
        jump = [2.0 * shear_cells * (dev_new[k] - dev_old[k]) for k in range(6)]
        totals, long_term = [0.0] * 6, 1.0
        for term in range(terms):
            modulus = choose([moduli[r, term] for r in range(regions)])
            time = choose([times[r, term] for r in range(regions)])
            decay = jnp.exp(-1.0 / time)
            weight = modulus * (1.0 - decay) * time
            long_term = long_term - modulus
            for k in range(6):
                value = decay * visco[term, k, i] + weight * jump[k]
                visco_next[term, k, i] = value
                totals[k] = totals[k] + value
        for k in range(6):
            stress[k, i] = softening * (long_term * 2.0 * shear_cells * dev_new[k] + totals[k])


def solve_kernel(geo, grams, basis, damage, residual):
    total = grams[0]
    for n in range(1, grams.shape[0]):
        total = total + grams[n]
    column = jnp.sum(total, axis=1, keepdims=True)
    gram = {}
    for k, (i, j) in enumerate(PAIRS):
        gram[i, j] = gram[j, i] = column[k : k + 1]

    def image_of(p):
        out = [(1.0 + LENGTH_SQUARED * SHIFTS[j]) * p[j] for j in range(len(p))]
        out.append(LENGTH_SQUARED * p[-1])
        for j in range(1, len(p)):
            out[j] = out[j] + LENGTH_SQUARED * p[j - 1]
        return out

    def product(u, v):
        value = None
        for i in range(len(u)):
            inner = None
            for j in range(len(v)):
                inner = gram[i, j] * v[j] if inner is None else inner + gram[i, j] * v[j]
            value = u[i] * inner if value is None else value + u[i] * inner
        return value

    one = jnp.ones((1, 1), jnp.float32)
    field, rest, direction = [], [one], [one]
    norm_now = gram[0, 0]
    for iteration in range(ITERS):
        image = image_of(direction)
        alpha = norm_now / product(image, direction)
        field = [x + alpha * d for x, d in zip(field, direction)] + [alpha * direction[-1]]
        rest = [r - alpha * w for r, w in zip(rest, image)] + [-alpha * image[-1]]
        if iteration + 1 < ITERS:
            norm_next = product(rest, rest)
            beta = norm_next / norm_now
            direction = [r + beta * d for r, d in zip(rest, direction)] + [rest[-1]]
            norm_now = norm_next
    for i in range(geo.lx):
        vectors = [basis[j, i] for j in range(ITERS + 1)]
        damage[i] = functools.reduce(jnp.add, [c * t for c, t in zip(field, vectors)])
        residual[i] = functools.reduce(jnp.add, [c * t for c, t in zip(rest, vectors)])


def shaped(*shape):
    return jax.ShapeDtypeStruct(shape, jnp.float32)


def call(kernel, outs, tables, arrays, scratch=(), flops=0, vmem=32 * MB):
    smem, vmem_spec = pl.BlockSpec(memory_space=pltpu.SMEM), pl.BlockSpec(memory_space=pltpu.VMEM)
    moved = 4 * sum(int(np.prod(a.shape)) for a in list(arrays) + list(outs))
    return pl.pallas_call(
        kernel,
        out_shape=outs,
        in_specs=[smem] * len(tables) + [vmem_spec] * len(arrays),
        out_specs=[vmem_spec] * len(outs),
        scratch_shapes=list(scratch),
        compiler_params=pltpu.CompilerParams(vmem_limit_bytes=vmem),
        cost_estimate=pl.CostEstimate(flops=flops, bytes_accessed=moved, transcendentals=0),
    )(*tables, *arrays)


def ring(shard, axis, hops):
    count = lax.axis_size(axis)
    steps = list(range(hops + 1)) + list(range(-hops, 0))
    moved = [lax.ppermute(shard, axis, [((i + step) % count, i) for i in range(count)]) if step else shard for step in steps]
    return jnp.stack(moved)


def on_device(
    displacement,
    displacement_old,
    visco_state,
    energy_max,
    region,
    dirichlet,
    prony_moduli,
    prony_times,
    shear_modulus,
    mullins_ratio,
    mullins_scale,
):
    geo = geometry(energy_max.shape)
    lx, ly, lz = energy_max.shape
    _, tiles = places(geo)
    main, slab = call(
        functools.partial(pack_kernel, geo),
        [shaped(FIELDS * lx, ly, lz), shaped(tiles, ly, lz)],
        [],
        [displacement, displacement_old, energy_max, region, dirichlet],
    )
    up = [(i, i + 1) for i in range(geo.gz - 1)]
    down = [(j, i) for i, j in up]
    from_left, from_right = lax.ppermute(slab, "gz", up), lax.ppermute(slab, "gz", down)
    edges = jnp.where(left_lanes(geo), from_left, from_right)
    payload = jnp.concatenate([main, edges], axis=0)
    if geo.full:
        blocks = lax.all_gather(payload, ("gx", "gy"))
    else:
        blocks = ring(ring(payload, "gy", geo.hops_y), "gx", geo.hops_x)
        blocks = blocks.reshape((geo.bx * geo.by,) + payload.shape)
    planes, rows = geo.bx * lx, geo.by * ly
    basis, dev_own, grams = call(
        functools.partial(basis_kernel, geo),
        [shaped(ITERS + 1, lx, ly, lz), shaped(6, lx, ly, lz), shaped(-(-len(PAIRS) // 8) * 8, lz)],
        [shear_modulus, mullins_ratio, mullins_scale],
        [blocks],
        [
            pltpu.VMEM((3, planes, rows, 2 * lz), jnp.float32),
            pltpu.VMEM((ITERS + 1, planes, rows, 2 * lz), jnp.float32),
            pltpu.VMEM((6, planes, rows, lz), jnp.float32),
        ],
        flops=planes * rows * lz * 500,
    )
    if geo.full:
        sums = lax.all_gather(grams, "gz")
    else:
        sums = lax.psum(grams, ("gx", "gy", "gz"))[None]
    stress, visco_next, energy_next = call(
        functools.partial(visco_kernel, geo),
        [shaped(6, lx, ly, lz), shaped(*visco_state.shape), shaped(lx, ly, lz)],
        [prony_moduli, prony_times, shear_modulus, mullins_ratio, mullins_scale],
        [blocks, dev_own, visco_state, energy_max, region],
        flops=lx * ly * lz * 500,
    )
    damage_field, residual = call(
        functools.partial(solve_kernel, geo),
        [shaped(lx, ly, lz), shaped(lx, ly, lz)],
        [],
        [sums, basis],
    )
    return (stress, visco_next, energy_next, damage_field, residual)


def solution(mesh):
    in_specs = (
        P(None, "gx", "gy", "gz"),
        P(None, "gx", "gy", "gz"),
        P(None, None, "gx", "gy", "gz"),
        P("gx", "gy", "gz"),
        P("gx", "gy", "gz"),
        P("gx", "gy", "gz"),
        P(),
        P(),
        P(),
        P(),
        P(),
    )
    out_specs = (
        P(None, "gx", "gy", "gz"),
        P(None, None, "gx", "gy", "gz"),
        P("gx", "gy", "gz"),
        P("gx", "gy", "gz"),
        P("gx", "gy", "gz"),
    )
    return jax.shard_map(
        on_device, mesh=mesh, in_specs=in_specs, out_specs=out_specs, check_vma=False
    )
```

```python
import functools
import typing

import jax
import jax.numpy as jnp
import numpy as np
from jax import lax
from jax.experimental import pallas as pl
from jax.experimental.pallas import tpu as pltpu
from jax.sharding import PartitionSpec as P

ITERS = 4
LENGTH_SQUARED = 4.0

SHIFTS = (0.0, 6.0, 1.5, 9.0)
PAIRS = [(i, j) for i in range(ITERS + 1) for j in range(i, ITERS + 1) if i < ITERS]

WIDE, NARROW = 5, 3
REACHES = (ITERS + 1,) * WIDE + (1,) * NARROW
FIELDS = WIDE + NARROW
MB = 1 << 20


class Geometry(typing.NamedTuple):
    lx: int
    ly: int
    lz: int
    gx: int
    gy: int
    gz: int
    hops_x: int
    hops_y: int
    full: bool

    @property
    def bx(self):
        return self.gx if self.full else 2 * self.hops_x + 1

    @property
    def by(self):
        return self.gy if self.full else 2 * self.hops_y + 1


def geometry(block):
    lx, ly, lz = block
    gx, gy, gz = (lax.axis_size(name) for name in ("gx", "gy", "gz"))
    hops_x, hops_y = -(-(ITERS + 1) // lx), -(-(ITERS + 1) // ly)
    full = gx <= 2 * hops_x + 1 and gy <= hops_y + 1
    return Geometry(lx, ly, lz, gx, gy, gz, hops_x, hops_y, full)


def places(geo):
    result, tile, at = [], 0, 0
    for reach in REACHES:
        for _ in range(geo.lx):
            if at + 2 * reach > geo.lz:
                tile, at = tile + 1, 0
            result.append((tile, at + reach))
            at += 2 * reach
    return result, tile + 1


def left_lanes(geo):
    spots, tiles = places(geo)
    mask = np.zeros((tiles, 1, geo.lz), np.bool_)
    for index, (tile, centre) in enumerate(spots):
        mask[tile, 0, centre - REACHES[index // geo.lx] : centre] = True
    return mask


def iota(shape, dim):
    return lax.broadcasted_iota(jnp.int32, shape, dim)


def pack_kernel(
    geo,
    new_hbm,
    old_hbm,
    energy_hbm,
    region_hbm,
    dirichlet_hbm,
    moduli_hbm,
    times_hbm,
    shear_hbm,
    ratio_hbm,
    scale_hbm,
    main,
    slab,
    tables,
    new,
    old,
    energy_max,
    region,
    dirichlet,
    moduli,
    times,
    shear,
    ratio,
    scale,
    arrived,
):
    sources = (new_hbm, old_hbm, energy_hbm, region_hbm, dirichlet_hbm)
    sources += (moduli_hbm, times_hbm, shear_hbm, ratio_hbm, scale_hbm)
    targets = (new, old, energy_max, region, dirichlet, moduli, times, shear, ratio, scale)
    copies = [pltpu.make_async_copy(a, b, arrived.at[n]) for n, (a, b) in enumerate(zip(sources, targets))]
    for copy in copies:
        copy.start()
    for copy in copies:
        copy.wait()
    spots, tiles = places(geo)
    lane = iota((geo.ly, geo.lz), 1)
    edges = [jnp.zeros((geo.ly, geo.lz), jnp.float32)] * tiles
    for i in range(geo.lx):
        share = (1 - dirichlet[i]).astype(jnp.float32)
        values = [new[a, i] * share for a in range(3)]
        values += [energy_max[i], region[i].astype(jnp.float32)]
        values += [old[a, i] * share for a in range(3)]
        for f, value in enumerate(values):
            main[f * geo.lx + i] = value
            tile, centre = spots[f * geo.lx + i]
            inside = (lane >= centre - REACHES[f]) & (lane < centre + REACHES[f])
            edges[tile] = jnp.where(inside, pltpu.roll(value, centre, 1), edges[tile])
    for tile in range(tiles):
        slab[tile] = edges[tile]
    regions, terms = moduli.shape
    for r in range(regions):
        entries = [shear[r], ratio[r], scale[r]]
        entries += [moduli[r, k] for k in range(terms)] + [times[r, k] for k in range(terms)]
        for k, entry in enumerate(entries):
            tables[k, r : r + 1, :] = jnp.full((1, geo.lz), entry, jnp.float32)


SHEAR, RATIO, SCALE, MODULI = range(4)


def lookup(tables, entry, masks):
    value = tables[entry, len(masks) : len(masks) + 1, :]
    for r, mask in enumerate(masks):
        value = jnp.where(mask, tables[entry, r : r + 1, :], value)
    return value


def deviator(grad):
    trace_third = (grad[0][0] + grad[1][1] + grad[2][2]) / 3.0
    return [
        grad[0][0] - trace_third,
        grad[1][1] - trace_third,
        grad[2][2] - trace_third,
        0.5 * (grad[1][2] + grad[2][1]),
        0.5 * (grad[0][2] + grad[2][0]),
        0.5 * (grad[1][0] + grad[0][1]),
    ]


def contract(dev):
    return (
        dev[0] * dev[0]
        + dev[1] * dev[1]
        + dev[2] * dev[2]
        + 2.0 * (dev[3] * dev[3] + dev[4] * dev[4] + dev[5] * dev[5])
    )


def soften(energy, energy_next, scale, ratio):
    return 1.0 - lax.erf((energy_next - energy) / scale) / ratio


def basis_kernel(geo, tables, blocks, basis, dev_own, grams, held, field, dev_all):
    lx, ly, lz = geo.lx, geo.ly, geo.lz
    planes, rows, lanes = geo.bx * lx, geo.by * ly, 2 * lz
    regions = tables.shape[1]
    spots, _ = places(geo)
    row, lane = iota((rows, lanes), 0), iota((rows, lanes), 1)
    index_y, index_z = lax.axis_index("gy"), lax.axis_index("gz")
    if geo.full:
        grid_row = row
        own_x, own_y = lax.axis_index("gx") * lx, pl.multiple_of(index_y * ly, ly)
    else:
        grid_row = index_y * ly + jnp.where(row < (1 + geo.hops_y) * ly, row, row - rows)
        own_x, own_y = 0, 0
    end_y, start_y = grid_row == geo.gy * ly - 1, grid_row == 0
    end_z = (lane == lz - 1) & (index_z == geo.gz - 1)
    start_z = (lane == 0) & (index_z == 0)

    def whole_plane(f, p):
        tile, centre = spots[f * lx + p % lx]
        parts = []
        for b in range(geo.by):
            at = (p // lx) * geo.by + b
            edge = pltpu.roll(blocks[at, FIELDS * lx + tile], lz - centre, 1)
            parts.append(jnp.concatenate([blocks[at, f * lx + p % lx], edge], axis=1))
        return jnp.concatenate(parts, axis=0)

    def beside(value):
        next_y = jnp.where(end_y, 0.0, pltpu.roll(value, rows - 1, 0))
        prev_y = jnp.where(start_y, 0.0, pltpu.roll(value, 1, 0))
        next_z = jnp.where(end_z, 0.0, pltpu.roll(value, lanes - 1, 1))
        prev_z = jnp.where(start_z, 0.0, pltpu.roll(value, 1, 1))
        return next_y, prev_y, next_z, prev_z

    for p in range(planes):
        for a in range(3):
            held[a, p] = whole_plane(a, p)
    for p in range(planes):
        grad = []
        for a in range(3):
            next_y, prev_y, next_z, prev_z = beside(held[a, p])
            next_x, prev_x = held[a, (p + 1) % planes], held[a, (p - 1) % planes]
            grad.append([0.5 * (next_x - prev_x), 0.5 * (next_y - prev_y), 0.5 * (next_z - prev_z)])
        dev = deviator(grad)
        for k in range(6):
            dev_all[k, p] = dev[k][:, :lz]
        label = whole_plane(4, p)
        halves = []
        for half in (slice(0, lz), slice(lz, lanes)):
            masks = [label[:, half] == r for r in range(regions - 1)]
            halves.append([lookup(tables, entry, masks) for entry in (SHEAR, SCALE, RATIO)])
        shear_cells, scale_cells, ratio_cells = [jnp.concatenate(pair, axis=1) for pair in zip(*halves)]
        energy = shear_cells * contract(dev)
        energy_next = jnp.maximum(whole_plane(3, p), energy)
        softening = soften(energy, energy_next, scale_cells, ratio_cells)
        field[0, p] = softening * energy
    for j, shift in enumerate(SHIFTS):
        for p in range(planes):
            value = field[j, p]
            next_y, prev_y, next_z, prev_z = beside(value)
            next_x, prev_x = field[j, (p + 1) % planes], field[j, (p - 1) % planes]
            image = (value - next_x) + (value - prev_x)
            image += (value - next_y) + (value - prev_y)
            image += (value - next_z) + (value - prev_z)
            field[j + 1, p] = image - shift * value if shift else image

    grams[...] = jnp.zeros(grams.shape, jnp.float32)
    sums = [jnp.zeros((ly, lz), jnp.float32)] * len(PAIRS)
    for p in range(planes if geo.full else lx):
        for b in range(geo.by if geo.full else 1):
            own = [field[j, p, b * ly : (b + 1) * ly, :lz] for j in range(ITERS + 1)]
            sums = [total + own[i] * own[j] for total, (i, j) in zip(sums, PAIRS)]
    for k, total in enumerate(sums):
        grams[k : k + 1, :] = jnp.sum(total, axis=0, keepdims=True)
    for i in range(lx):
        for j in range(ITERS + 1):
            basis[j, i] = field[j, own_x + i, pl.ds(own_y, ly), :lz]
        for k in range(6):
            dev_own[k, i] = dev_all[k, own_x + i, pl.ds(own_y, ly), :]


def visco_kernel(
    geo, tables, blocks, dev_own, visco, stress, visco_next, energy_next
):
    lx, ly, lz = geo.lx, geo.ly, geo.lz
    spots, _ = places(geo)
    row, lane = iota((ly, lz), 0), iota((ly, lz), 1)
    index_y = lax.axis_index("gy")
    own_x, own_y = (lax.axis_index("gx"), index_y) if geo.full else (0, 0)

    def block(step_x, step_y):
        return lax.rem(own_x + step_x + geo.bx, geo.bx) * geo.by + lax.rem(own_y + step_y + geo.by, geo.by)

    here, right, left, above, below = block(0, 0), block(1, 0), block(-1, 0), block(0, 1), block(0, -1)
    regions, terms = tables.shape[1], visco.shape[0]
    for i in range(lx):
        grad = []
        for a in range(3):
            at = (WIDE + a) * lx + i
            value = blocks[here, at]
            next_x = blocks[here, at + 1] if i + 1 < lx else blocks[right, at + 1 - lx]
            prev_x = blocks[here, at - 1] if i else blocks[left, at + lx - 1]
            first = jnp.where(index_y == geo.gy - 1, 0.0, blocks[above, at])
            last = jnp.where(index_y == 0, 0.0, blocks[below, at])
            next_y = pltpu.roll(jnp.where(row == 0, first, value), ly - 1, 0)
            prev_y = pltpu.roll(jnp.where(row == ly - 1, last, value), 1, 0)
            tile, centre = spots[at]
            edge = blocks[here, FIELDS * lx + tile]
            next_z = jnp.where(lane == lz - 1, pltpu.roll(edge, lz - 1 - centre, 1), pltpu.roll(value, lz - 1, 1))
            prev_z = jnp.where(lane == 0, pltpu.roll(edge, lz + 1 - centre, 1), pltpu.roll(value, 1, 1))
            grad.append([0.5 * (next_x - prev_x), 0.5 * (next_y - prev_y), 0.5 * (next_z - prev_z)])
        dev_old = deviator(grad)
        dev_new = [dev_own[k, i] for k in range(6)]
        label = blocks[here, 4 * lx + i]
        masks = [label == r for r in range(regions - 1)]
        shear_cells, ratio_cells, scale_cells = [lookup(tables, entry, masks) for entry in (SHEAR, RATIO, SCALE)]
        energy = shear_cells * contract(dev_new)
        energy_after = jnp.maximum(blocks[here, 3 * lx + i], energy)
        energy_next[i] = energy_after
        softening = soften(energy, energy_after, scale_cells, ratio_cells)
        jump = [2.0 * shear_cells * (dev_new[k] - dev_old[k]) for k in range(6)]
        totals, long_term = [0.0] * 6, 1.0
        for term in range(terms):
            modulus = lookup(tables, MODULI + term, masks)
            time = lookup(tables, MODULI + terms + term, masks)
            decay = jnp.exp(-1.0 / time)
            weight = modulus * (1.0 - decay) * time
            long_term = long_term - modulus
            for k in range(6):
                value = decay * visco[term, k, i] + weight * jump[k]
                visco_next[term, k, i] = value
                totals[k] = totals[k] + value
        for k in range(6):
            stress[k, i] = softening * (long_term * 2.0 * shear_cells * dev_new[k] + totals[k])


def solve_kernel(geo, grams, basis, damage, residual):
    total = grams[0]
    for n in range(1, grams.shape[0]):
        total = total + grams[n]
    column = jnp.sum(total, axis=1, keepdims=True)
    gram = {}
    for k, (i, j) in enumerate(PAIRS):
        gram[i, j] = gram[j, i] = column[k : k + 1]

    def image_of(p):
        out = [(1.0 + LENGTH_SQUARED * SHIFTS[j]) * p[j] for j in range(len(p))]
        out.append(LENGTH_SQUARED * p[-1])
        for j in range(1, len(p)):
            out[j] = out[j] + LENGTH_SQUARED * p[j - 1]
        return out

    def product(u, v):
        value = None
        for i in range(len(u)):
            inner = None
            for j in range(len(v)):
                inner = gram[i, j] * v[j] if inner is None else inner + gram[i, j] * v[j]
            value = u[i] * inner if value is None else value + u[i] * inner
        return value

    one = jnp.ones((1, 1), jnp.float32)
    field, rest, direction = [], [one], [one]
    norm_now = gram[0, 0]
    for iteration in range(ITERS):
        image = image_of(direction)
        alpha = norm_now / product(image, direction)
        field = [x + alpha * d for x, d in zip(field, direction)] + [alpha * direction[-1]]
        rest = [r - alpha * w for r, w in zip(rest, image)] + [-alpha * image[-1]]
        if iteration + 1 < ITERS:
            norm_next = product(rest, rest)
            beta = norm_next / norm_now
            direction = [r + beta * d for r, d in zip(rest, direction)] + [rest[-1]]
            norm_now = norm_next
    for i in range(geo.lx):
        vectors = [basis[j, i] for j in range(ITERS + 1)]
        damage[i] = functools.reduce(jnp.add, [c * t for c, t in zip(field, vectors)])
        residual[i] = functools.reduce(jnp.add, [c * t for c, t in zip(rest, vectors)])


def shaped(*shape):
    return jax.ShapeDtypeStruct(shape, jnp.float32)


def call(kernel, outs, arrays, scratch=(), flops=0, space=pltpu.VMEM, vmem=32 * MB):
    moved = 4 * sum(int(np.prod(a.shape)) for a in list(arrays) + list(outs))
    return pl.pallas_call(
        kernel,
        out_shape=outs,
        in_specs=[pl.BlockSpec(memory_space=space)] * len(arrays),
        out_specs=[pl.BlockSpec(memory_space=pltpu.VMEM)] * len(outs),
        scratch_shapes=list(scratch),
        compiler_params=pltpu.CompilerParams(vmem_limit_bytes=vmem),
        cost_estimate=pl.CostEstimate(flops=flops, bytes_accessed=moved, transcendentals=0),
    )(*arrays)


def ring(shard, axis, hops):
    count = lax.axis_size(axis)
    steps = list(range(hops + 1)) + list(range(-hops, 0))
    moved = [lax.ppermute(shard, axis, [((i + step) % count, i) for i in range(count)]) if step else shard for step in steps]
    return jnp.stack(moved)


def summed(terms, axis):
    count = lax.axis_size(axis)
    if count & (count - 1):
        return lax.psum(terms, axis)[None]
    step, parts = 1, [terms]
    while step < count:
        total = functools.reduce(jnp.add, parts)
        parts = [total, lax.ppermute(total, axis, [(i, i ^ step) for i in range(count)])]
        step *= 2
    return jnp.stack(parts)


def on_device(
    displacement,
    displacement_old,
    visco_state,
    energy_max,
    region,
    dirichlet,
    prony_moduli,
    prony_times,
    shear_modulus,
    mullins_ratio,
    mullins_scale,
):
    geo = geometry(energy_max.shape)
    lx, ly, lz = energy_max.shape
    _, tiles = places(geo)
    regions, terms = prony_moduli.shape
    arguments = [displacement, displacement_old, energy_max, region, dirichlet]
    parameters = [prony_moduli, prony_times, shear_modulus, mullins_ratio, mullins_scale]
    main, slab, tables = call(
        functools.partial(pack_kernel, geo),
        [shaped(FIELDS * lx, ly, lz), shaped(tiles, ly, lz), shaped(MODULI + 2 * terms, regions, lz)],
        arguments + parameters,
        [pltpu.VMEM(a.shape, a.dtype) for a in arguments]
        + [pltpu.SMEM(a.shape, a.dtype) for a in parameters]
        + [pltpu.SemaphoreType.DMA((len(arguments) + len(parameters),))],
        space=pl.ANY,
        vmem=56 * MB,
    )
    up = [(i, i + 1) for i in range(geo.gz - 1)]
    down = [(j, i) for i, j in up]
    from_left, from_right = lax.ppermute(slab, "gz", up), lax.ppermute(slab, "gz", down)
    edges = jnp.where(left_lanes(geo), from_left, from_right)
    payload = jnp.concatenate([main, edges], axis=0)
    if geo.full:
        copies = jnp.broadcast_to(payload[None], (geo.gx * geo.gy,) + payload.shape)
        blocks = lax.all_to_all(copies, ("gx", "gy"), 0, 0)
    else:
        blocks = ring(ring(payload, "gy", geo.hops_y), "gx", geo.hops_x)
        blocks = blocks.reshape((geo.bx * geo.by,) + payload.shape)
    planes, rows = geo.bx * lx, geo.by * ly
    basis, dev_own, grams = call(
        functools.partial(basis_kernel, geo),
        [shaped(ITERS + 1, lx, ly, lz), shaped(6, lx, ly, lz), shaped(-(-len(PAIRS) // 8) * 8, lz)],
        [tables, blocks],
        [
            pltpu.VMEM((3, planes, rows, 2 * lz), jnp.float32),
            pltpu.VMEM((ITERS + 1, planes, rows, 2 * lz), jnp.float32),
            pltpu.VMEM((6, planes, rows, lz), jnp.float32),
        ],
        flops=planes * rows * lz * 500,
    )
    if geo.full:
        sums = summed(grams, "gz")
    else:
        sums = lax.psum(grams, ("gx", "gy", "gz"))[None]
    stress, visco_next, energy_next = call(
        functools.partial(visco_kernel, geo),
        [shaped(6, lx, ly, lz), shaped(*visco_state.shape), shaped(lx, ly, lz)],
        [tables, blocks, dev_own, visco_state],
        flops=lx * ly * lz * 500,
    )
    damage_field, residual = call(
        functools.partial(solve_kernel, geo),
        [shaped(lx, ly, lz), shaped(lx, ly, lz)],
        [sums, basis],
    )
    return (stress, visco_next, energy_next, damage_field, residual)


def solution(mesh):
    in_specs = (
        P(None, "gx", "gy", "gz"),
        P(None, "gx", "gy", "gz"),
        P(None, None, "gx", "gy", "gz"),
        P("gx", "gy", "gz"),
        P("gx", "gy", "gz"),
        P("gx", "gy", "gz"),
        P(),
        P(),
        P(),
        P(),
        P(),
    )
    out_specs = (
        P(None, "gx", "gy", "gz"),
        P(None, None, "gx", "gy", "gz"),
        P("gx", "gy", "gz"),
        P("gx", "gy", "gz"),
        P("gx", "gy", "gz"),
    )
    return jax.shard_map(
        on_device, mesh=mesh, in_specs=in_specs, out_specs=out_specs, check_vma=False
    )
```

```python
import functools
import typing

import jax
import jax.numpy as jnp
import numpy as np
from jax import lax
from jax.experimental import pallas as pl
from jax.experimental.pallas import tpu as pltpu
from jax.sharding import PartitionSpec as P

ITERS = 4
LENGTH_SQUARED = 4.0

SHIFTS = (0.0, 6.0, 1.5, 9.0)
PAIRS = [(i, j) for i in range(ITERS + 1) for j in range(i, ITERS + 1) if i < ITERS]

WIDE, NARROW = 5, 3
REACHES = (ITERS + 1,) * WIDE + (1,) * NARROW
FIELDS = WIDE + NARROW
MB = 1 << 20


class Geometry(typing.NamedTuple):
    lx: int
    ly: int
    lz: int
    gx: int
    gy: int
    gz: int
    hops_x: int
    hops_y: int
    full: bool

    @property
    def bx(self):
        return self.gx if self.full else 2 * self.hops_x + 1

    @property
    def by(self):
        return self.gy if self.full else 2 * self.hops_y + 1

    def beside(self, code, step, index_x):
        if not self.full:
            return (code + step) % self.bx
        return (((index_x ^ code) + step) & (self.gx - 1)) ^ index_x


def geometry(block):
    lx, ly, lz = block
    gx, gy, gz = (lax.axis_size(name) for name in ("gx", "gy", "gz"))
    hops_x, hops_y = -(-(ITERS + 1) // lx), -(-(ITERS + 1) // ly)
    full = gx <= 2 * hops_x + 1 and not gx & (gx - 1) and gy <= 2
    return Geometry(lx, ly, lz, gx, gy, gz, hops_x, hops_y, full)


def places(geo):
    result, tile, at = [], 0, 0
    for reach in REACHES:
        for _ in range(geo.lx):
            if at + 2 * reach > geo.lz:
                tile, at = tile + 1, 0
            result.append((tile, at + reach))
            at += 2 * reach
    return result, tile + 1


def left_lanes(geo):
    spots, tiles = places(geo)
    mask = np.zeros((tiles, 1, geo.lz), np.bool_)
    for index, (tile, centre) in enumerate(spots):
        mask[tile, 0, centre - REACHES[index // geo.lx] : centre] = True
    return mask


def iota(shape, dim):
    return lax.broadcasted_iota(jnp.int32, shape, dim)


def pack_kernel(
    geo,
    new_hbm,
    old_hbm,
    energy_hbm,
    region_hbm,
    dirichlet_hbm,
    moduli_hbm,
    times_hbm,
    shear_hbm,
    ratio_hbm,
    scale_hbm,
    main,
    slab,
    tables,
    new,
    old,
    energy_max,
    region,
    dirichlet,
    moduli,
    times,
    shear,
    ratio,
    scale,
    arrived,
):
    sources = (new_hbm, old_hbm, energy_hbm, region_hbm, dirichlet_hbm)
    sources += (moduli_hbm, times_hbm, shear_hbm, ratio_hbm, scale_hbm)
    targets = (new, old, energy_max, region, dirichlet, moduli, times, shear, ratio, scale)
    copies = [pltpu.make_async_copy(a, b, arrived.at[n]) for n, (a, b) in enumerate(zip(sources, targets))]
    for copy in copies:
        copy.start()
    for copy in copies:
        copy.wait()
    spots, tiles = places(geo)
    lane = iota((geo.ly, geo.lz), 1)
    edges = [jnp.zeros((geo.ly, geo.lz), jnp.float32)] * tiles
    for i in range(geo.lx):
        share = (1 - dirichlet[i]).astype(jnp.float32)
        values = [new[a, i] * share for a in range(3)]
        values += [energy_max[i], region[i].astype(jnp.float32)]
        values += [old[a, i] * share for a in range(3)]
        for f, value in enumerate(values):
            main[f * geo.lx + i] = value
            tile, centre = spots[f * geo.lx + i]
            inside = (lane >= centre - REACHES[f]) & (lane < centre + REACHES[f])
            edges[tile] = jnp.where(inside, pltpu.roll(value, centre, 1), edges[tile])
    for tile in range(tiles):
        slab[tile] = edges[tile]
    regions, terms = moduli.shape
    for r in range(regions):
        entries = [shear[r], ratio[r], scale[r]]
        entries += [moduli[r, k] for k in range(terms)] + [times[r, k] for k in range(terms)]
        for k, entry in enumerate(entries):
            tables[k, r : r + 1, :] = jnp.full((1, geo.lz), entry, jnp.float32)


SHEAR, RATIO, SCALE, MODULI = range(4)


def lookup(tables, entry, masks):
    value = tables[entry, len(masks) : len(masks) + 1, :]
    for r, mask in enumerate(masks):
        value = jnp.where(mask, tables[entry, r : r + 1, :], value)
    return value


def deviator(grad):
    trace_third = (grad[0][0] + grad[1][1] + grad[2][2]) / 3.0
    return [
        grad[0][0] - trace_third,
        grad[1][1] - trace_third,
        grad[2][2] - trace_third,
        0.5 * (grad[1][2] + grad[2][1]),
        0.5 * (grad[0][2] + grad[2][0]),
        0.5 * (grad[1][0] + grad[0][1]),
    ]


def contract(dev):
    return (
        dev[0] * dev[0]
        + dev[1] * dev[1]
        + dev[2] * dev[2]
        + 2.0 * (dev[3] * dev[3] + dev[4] * dev[4] + dev[5] * dev[5])
    )


def soften(energy, energy_next, scale, ratio):
    return 1.0 - lax.erf((energy_next - energy) / scale) / ratio


def basis_kernel(geo, where, *refs):
    tables, blocks = refs[0], refs[1:-5]
    basis, dev_own, grams, held, field = refs[-5:]
    lx, ly, lz = geo.lx, geo.ly, geo.lz
    planes, rows, lanes = geo.bx * lx, geo.by * ly, 2 * lz
    regions = tables.shape[1]
    spots, _ = places(geo)
    row, lane = iota((rows, lanes), 0), iota((rows, lanes), 1)
    index_x, index_y, index_z = (lax.axis_index(name) for name in ("gx", "gy", "gz"))
    if geo.full:
        grid_row = jnp.where(row < ly, row + index_y * ly, row - index_y * ly)
    else:
        grid_row = index_y * ly + jnp.where(row < (1 + geo.hops_y) * ly, row, row - rows)
    end_y, start_y = grid_row == geo.gy * ly - 1, grid_row == 0
    end_z = (lane == lz - 1) & (index_z == geo.gz - 1)
    start_z = (lane == 0) & (index_z == 0)

    def next_plane(p):
        return p + 1 if p % lx + 1 < lx else geo.beside(p // lx, 1, index_x) * lx

    def prev_plane(p):
        return p - 1 if p % lx else geo.beside(p // lx, -1, index_x) * lx + lx - 1

    def whole_plane(f, p):
        tile, centre = spots[f * lx + p % lx]
        parts = []
        for b in range(geo.by):
            array, at = where[p // lx, b]
            edge = pltpu.roll(blocks[array][at, FIELDS * lx + tile], lz - centre, 1)
            parts.append(jnp.concatenate([blocks[array][at, f * lx + p % lx], edge], axis=1))
        return jnp.concatenate(parts, axis=0)

    def beside(value):
        next_y = jnp.where(end_y, 0.0, pltpu.roll(value, rows - 1, 0))
        prev_y = jnp.where(start_y, 0.0, pltpu.roll(value, 1, 0))
        next_z = jnp.where(end_z, 0.0, pltpu.roll(value, lanes - 1, 1))
        prev_z = jnp.where(start_z, 0.0, pltpu.roll(value, 1, 1))
        return next_y, prev_y, next_z, prev_z

    for p in range(planes):
        for a in range(3):
            held[a, p] = whole_plane(a, p)
    for p in range(planes):
        grad = []
        for a in range(3):
            next_y, prev_y, next_z, prev_z = beside(held[a, p])
            next_x, prev_x = held[a, next_plane(p)], held[a, prev_plane(p)]
            grad.append([0.5 * (next_x - prev_x), 0.5 * (next_y - prev_y), 0.5 * (next_z - prev_z)])
        dev = deviator(grad)
        if p < lx:
            for k in range(6):
                dev_own[k, p] = dev[k][:ly, :lz]
        label = whole_plane(4, p)
        halves = []
        for half in (slice(0, lz), slice(lz, lanes)):
            masks = [label[:, half] == r for r in range(regions - 1)]
            halves.append([lookup(tables, entry, masks) for entry in (SHEAR, SCALE, RATIO)])
        shear_cells, scale_cells, ratio_cells = [jnp.concatenate(pair, axis=1) for pair in zip(*halves)]
        energy = shear_cells * contract(dev)
        energy_next = jnp.maximum(whole_plane(3, p), energy)
        softening = soften(energy, energy_next, scale_cells, ratio_cells)
        field[0, p] = softening * energy
    for j, shift in enumerate(SHIFTS):
        for p in range(planes):
            value = field[j, p]
            next_y, prev_y, next_z, prev_z = beside(value)
            next_x, prev_x = field[j, next_plane(p)], field[j, prev_plane(p)]
            image = (value - next_x) + (value - prev_x)
            image += (value - next_y) + (value - prev_y)
            image += (value - next_z) + (value - prev_z)
            field[j + 1, p] = image - shift * value if shift else image

    grams[...] = jnp.zeros(grams.shape, jnp.float32)
    sums = [jnp.zeros((ly, lz), jnp.float32)] * len(PAIRS)
    for p in range(planes if geo.full else lx):
        for b in range(geo.by if geo.full else 1):
            own = [field[j, p, b * ly : (b + 1) * ly, :lz] for j in range(ITERS + 1)]
            sums = [total + own[i] * own[j] for total, (i, j) in zip(sums, PAIRS)]
    for k, total in enumerate(sums):
        grams[k : k + 1, :] = jnp.sum(total, axis=0, keepdims=True)
    for i in range(lx):
        for j in range(ITERS + 1):
            basis[j, i] = field[j, i, :ly, :lz]


def visco_kernel(geo, where, *refs):
    tables, dev_own, visco, blocks = refs[0], refs[1], refs[2], refs[3:-3]
    stress, visco_next, energy_next = refs[-3:]
    lx, ly, lz = geo.lx, geo.ly, geo.lz
    spots, _ = places(geo)
    row, lane = iota((ly, lz), 0), iota((ly, lz), 1)
    index_x, index_y = lax.axis_index("gx"), lax.axis_index("gy")
    regions, terms = tables.shape[1], visco.shape[0]

    def own(at, code_y=0):
        array, place = where[0, code_y % geo.by]
        return blocks[array][place, at]

    def along_x(step, at):
        target = geo.beside(0, step, index_x)
        if not geo.full:
            array, place = where[target, 0]
            return blocks[array][place, at]
        value = None
        for code in {geo.beside(0, step, index) for index in range(geo.gx)}:
            array, place = where[code, 0]
            found = blocks[array][place, at]
            value = found if value is None else jnp.where(target == code, found, value)
        return value

    for i in range(lx):
        grad = []
        for a in range(3):
            at = (WIDE + a) * lx + i
            value = own(at)
            next_x = own(at + 1) if i + 1 < lx else along_x(1, at + 1 - lx)
            prev_x = own(at - 1) if i else along_x(-1, at + lx - 1)
            first = jnp.where(index_y == geo.gy - 1, 0.0, own(at, 1))
            last = jnp.where(index_y == 0, 0.0, own(at, -1))
            next_y = pltpu.roll(jnp.where(row == 0, first, value), ly - 1, 0)
            prev_y = pltpu.roll(jnp.where(row == ly - 1, last, value), 1, 0)
            tile, centre = spots[at]
            edge = own(FIELDS * lx + tile)
            next_z = jnp.where(lane == lz - 1, pltpu.roll(edge, lz - 1 - centre, 1), pltpu.roll(value, lz - 1, 1))
            prev_z = jnp.where(lane == 0, pltpu.roll(edge, lz + 1 - centre, 1), pltpu.roll(value, 1, 1))
            grad.append([0.5 * (next_x - prev_x), 0.5 * (next_y - prev_y), 0.5 * (next_z - prev_z)])
        dev_old = deviator(grad)
        dev_new = [dev_own[k, i] for k in range(6)]
        label = own(4 * lx + i)
        masks = [label == r for r in range(regions - 1)]
        shear_cells, ratio_cells, scale_cells = [lookup(tables, entry, masks) for entry in (SHEAR, RATIO, SCALE)]
        energy = shear_cells * contract(dev_new)
        energy_after = jnp.maximum(own(3 * lx + i), energy)
        energy_next[i] = energy_after
        softening = soften(energy, energy_after, scale_cells, ratio_cells)
        jump = [2.0 * shear_cells * (dev_new[k] - dev_old[k]) for k in range(6)]
        totals, long_term = [0.0] * 6, 1.0
        for term in range(terms):
            modulus = lookup(tables, MODULI + term, masks)
            time = lookup(tables, MODULI + terms + term, masks)
            decay = jnp.exp(-1.0 / time)
            weight = modulus * (1.0 - decay) * time
            long_term = long_term - modulus
            for k in range(6):
                value = decay * visco[term, k, i] + weight * jump[k]
                visco_next[term, k, i] = value
                totals[k] = totals[k] + value
        for k in range(6):
            stress[k, i] = softening * (long_term * 2.0 * shear_cells * dev_new[k] + totals[k])


def solve_kernel(geo, basis, *refs):
    grams, damage, residual = refs[:-2], refs[-2], refs[-1]
    total = functools.reduce(jnp.add, [part[...] for part in grams])
    column = jnp.sum(total, axis=1, keepdims=True)
    gram = {}
    for k, (i, j) in enumerate(PAIRS):
        gram[i, j] = gram[j, i] = column[k : k + 1]

    def image_of(p):
        out = [(1.0 + LENGTH_SQUARED * SHIFTS[j]) * p[j] for j in range(len(p))]
        out.append(LENGTH_SQUARED * p[-1])
        for j in range(1, len(p)):
            out[j] = out[j] + LENGTH_SQUARED * p[j - 1]
        return out

    def product(u, v):
        value = None
        for i in range(len(u)):
            inner = None
            for j in range(len(v)):
                inner = gram[i, j] * v[j] if inner is None else inner + gram[i, j] * v[j]
            value = u[i] * inner if value is None else value + u[i] * inner
        return value

    one = jnp.ones((1, 1), jnp.float32)
    field, rest, direction = [], [one], [one]
    norm_now = gram[0, 0]
    for iteration in range(ITERS):
        image = image_of(direction)
        alpha = norm_now / product(image, direction)
        field = [x + alpha * d for x, d in zip(field, direction)] + [alpha * direction[-1]]
        rest = [r - alpha * w for r, w in zip(rest, image)] + [-alpha * image[-1]]
        if iteration + 1 < ITERS:
            norm_next = product(rest, rest)
            beta = norm_next / norm_now
            direction = [r + beta * d for r, d in zip(rest, direction)] + [rest[-1]]
            norm_now = norm_next
    for i in range(geo.lx):
        vectors = [basis[j, i] for j in range(ITERS + 1)]
        damage[i] = functools.reduce(jnp.add, [c * t for c, t in zip(field, vectors)])
        residual[i] = functools.reduce(jnp.add, [c * t for c, t in zip(rest, vectors)])


def shaped(*shape):
    return jax.ShapeDtypeStruct(shape, jnp.float32)


def call(kernel, outs, arrays, scratch=(), flops=0, space=pltpu.VMEM, vmem=32 * MB):
    moved = 4 * sum(int(np.prod(a.shape)) for a in list(arrays) + list(outs))
    return pl.pallas_call(
        kernel,
        out_shape=outs,
        in_specs=[pl.BlockSpec(memory_space=space)] * len(arrays),
        out_specs=[pl.BlockSpec(memory_space=pltpu.VMEM)] * len(outs),
        scratch_shapes=list(scratch),
        compiler_params=pltpu.CompilerParams(vmem_limit_bytes=vmem),
        cost_estimate=pl.CostEstimate(flops=flops, bytes_accessed=moved, transcendentals=0),
    )(*arrays)


def moved(shard, axis, target):
    return lax.ppermute(shard, axis, [(i, target(i)) for i in range(lax.axis_size(axis))])


def ring(shard, axis, hops):
    count = lax.axis_size(axis)
    steps = list(range(hops + 1)) + list(range(-hops, 0))
    return jnp.stack([moved(shard, axis, lambda i: (i - step) % count) if step else shard for step in steps])


def gathered(payload, geo):
    if not geo.full:
        blocks = ring(ring(payload, "gy", geo.hops_y), "gx", geo.hops_x)
        where = {(x, y): (0, x * geo.by + y) for x in range(geo.bx) for y in range(geo.by)}
        return [blocks.reshape((geo.bx * geo.by,) + payload.shape)], where
    steps = [("gy", 0, 1)] * (geo.gy - 1)
    steps += [("gx", 1 << bit, 0) for bit in reversed(range(geo.gx.bit_length() - 1))]
    arrays, codes = [payload[None]], [[(0, 0)]]
    for axis, step_x, step_y in steps:
        if len(arrays) == 2:
            arrays, codes = [jnp.concatenate(arrays, axis=0)], [codes[0] + codes[1]]
        arrays.append(moved(arrays[0], axis, lambda i: i ^ (step_x + step_y)))
        codes.append([(x ^ step_x, y ^ step_y) for x, y in codes[0]])
    where = {code: (n, place) for n, held in enumerate(codes) for place, code in enumerate(held)}
    return arrays, where


def summed(terms, axis):
    count = lax.axis_size(axis)
    if count > 4:
        return [lax.psum(terms, axis)]
    return [terms] + [moved(terms, axis, lambda i: (i + step) % count) for step in range(1, count)]


def on_device(
    displacement,
    displacement_old,
    visco_state,
    energy_max,
    region,
    dirichlet,
    prony_moduli,
    prony_times,
    shear_modulus,
    mullins_ratio,
    mullins_scale,
):
    geo = geometry(energy_max.shape)
    lx, ly, lz = energy_max.shape
    _, tiles = places(geo)
    regions, terms = prony_moduli.shape
    arguments = [displacement, displacement_old, energy_max, region, dirichlet]
    parameters = [prony_moduli, prony_times, shear_modulus, mullins_ratio, mullins_scale]
    main, slab, tables = call(
        functools.partial(pack_kernel, geo),
        [shaped(FIELDS * lx, ly, lz), shaped(tiles, ly, lz), shaped(MODULI + 2 * terms, regions, lz)],
        arguments + parameters,
        [pltpu.VMEM(a.shape, a.dtype) for a in arguments]
        + [pltpu.SMEM(a.shape, a.dtype) for a in parameters]
        + [pltpu.SemaphoreType.DMA((len(arguments) + len(parameters),))],
        space=pltpu.HBM,
    )
    up = [(i, i + 1) for i in range(geo.gz - 1)]
    down = [(j, i) for i, j in up]
    from_left, from_right = lax.ppermute(slab, "gz", up), lax.ppermute(slab, "gz", down)
    edges = jnp.where(left_lanes(geo), from_left, from_right)
    payload = jnp.concatenate([main, edges], axis=0)
    blocks, where = gathered(payload, geo)
    planes, rows = geo.bx * lx, geo.by * ly
    basis, dev_own, grams = call(
        functools.partial(basis_kernel, geo, where),
        [shaped(ITERS + 1, lx, ly, lz), shaped(6, lx, ly, lz), shaped(-(-len(PAIRS) // 8) * 8, lz)],
        [tables, *blocks],
        [
            pltpu.VMEM((3, planes, rows, 2 * lz), jnp.float32),
            pltpu.VMEM((ITERS + 1, planes, rows, 2 * lz), jnp.float32),
        ],
        flops=planes * rows * lz * 500,
    )
    if geo.full:
        sums = summed(grams, "gz")
    else:
        sums = [lax.psum(grams, ("gx", "gy", "gz"))]
    stress, visco_next, energy_next = call(
        functools.partial(visco_kernel, geo, where),
        [shaped(6, lx, ly, lz), shaped(*visco_state.shape), shaped(lx, ly, lz)],
        [tables, dev_own, visco_state, *blocks],
        flops=lx * ly * lz * 500,
    )
    damage_field, residual = call(
        functools.partial(solve_kernel, geo),
        [shaped(lx, ly, lz), shaped(lx, ly, lz)],
        [basis, *sums],
    )
    return (stress, visco_next, energy_next, damage_field, residual)


def solution(mesh):
    in_specs = (
        P(None, "gx", "gy", "gz"),
        P(None, "gx", "gy", "gz"),
        P(None, None, "gx", "gy", "gz"),
        P("gx", "gy", "gz"),
        P("gx", "gy", "gz"),
        P("gx", "gy", "gz"),
        P(),
        P(),
        P(),
        P(),
        P(),
    )
    out_specs = (
        P(None, "gx", "gy", "gz"),
        P(None, None, "gx", "gy", "gz"),
        P("gx", "gy", "gz"),
        P("gx", "gy", "gz"),
        P("gx", "gy", "gz"),
    )
    return jax.shard_map(
        on_device, mesh=mesh, in_specs=in_specs, out_specs=out_specs, check_vma=False
    )
```

```python
import functools
import typing

import jax
import jax.numpy as jnp
import numpy as np
from jax import lax
from jax.experimental import pallas as pl
from jax.experimental.pallas import tpu as pltpu
from jax.sharding import PartitionSpec as P

ITERS = 4
LENGTH_SQUARED = 4.0

SHIFTS = (0.0, 6.0, 1.5, 9.0)
PAIRS = [(i, j) for i in range(ITERS + 1) for j in range(i, ITERS + 1) if i < ITERS]

WIDE, NARROW = 5, 3
REACHES = (ITERS + 1,) * WIDE + (1,) * NARROW
FIELDS = WIDE + NARROW
MB = 1 << 20


class Geometry(typing.NamedTuple):
    lx: int
    ly: int
    lz: int
    gx: int
    gy: int
    gz: int
    hops_x: int
    hops_y: int
    full: bool

    @property
    def bx(self):
        return self.gx if self.full else 2 * self.hops_x + 1

    @property
    def by(self):
        return self.gy if self.full else 2 * self.hops_y + 1

    def beside(self, code, step, index_x):
        if not self.full:
            return (code + step) % self.bx
        return (((index_x ^ code) + step) & (self.gx - 1)) ^ index_x


def geometry(block):
    lx, ly, lz = block
    gx, gy, gz = (lax.axis_size(name) for name in ("gx", "gy", "gz"))
    hops_x, hops_y = -(-(ITERS + 1) // lx), -(-(ITERS + 1) // ly)
    full = gx <= 2 * hops_x + 1 and not gx & (gx - 1) and gy <= 2
    return Geometry(lx, ly, lz, gx, gy, gz, hops_x, hops_y, full)


def places(geo):
    result, tile, at = [], 0, 0
    for reach in REACHES:
        for _ in range(geo.lx):
            if at + 2 * reach > geo.lz:
                tile, at = tile + 1, 0
            result.append((tile, at + reach))
            at += 2 * reach
    return result, tile + 1


def iota(shape, dim):
    return lax.broadcasted_iota(jnp.int32, shape, dim)


def pack_kernel(
    geo,
    new_hbm,
    old_hbm,
    energy_hbm,
    region_hbm,
    dirichlet_hbm,
    moduli_hbm,
    times_hbm,
    shear_hbm,
    ratio_hbm,
    scale_hbm,
    payload,
    tables,
    new,
    old,
    energy_max,
    region,
    dirichlet,
    moduli,
    times,
    shear,
    ratio,
    scale,
    arrived,
):
    sources = (new_hbm, old_hbm, energy_hbm, region_hbm, dirichlet_hbm)
    sources += (moduli_hbm, times_hbm, shear_hbm, ratio_hbm, scale_hbm)
    targets = (new, old, energy_max, region, dirichlet, moduli, times, shear, ratio, scale)
    copies = [pltpu.make_async_copy(a, b, arrived.at[n]) for n, (a, b) in enumerate(zip(sources, targets))]
    for copy in copies:
        copy.start()
    for copy in copies:
        copy.wait()
    spots, tiles = places(geo)
    lane = iota((geo.ly, geo.lz), 1)
    edges = [jnp.zeros((geo.ly, geo.lz), jnp.float32)] * tiles
    for i in range(geo.lx):
        share = (1 - dirichlet[i]).astype(jnp.float32)
        values = [new[a, i] * share for a in range(3)]
        values += [energy_max[i], region[i].astype(jnp.float32)]
        values += [old[a, i] * share for a in range(3)]
        for f, value in enumerate(values):
            payload[f * geo.lx + i] = value
            tile, centre = spots[f * geo.lx + i]
            inside = (lane >= centre - REACHES[f]) & (lane < centre + REACHES[f])
            edges[tile] = jnp.where(inside, pltpu.roll(value, centre, 1), edges[tile])
    for tile in range(tiles):
        payload[FIELDS * geo.lx + tile] = edges[tile]
    regions, terms = moduli.shape
    for r in range(regions):
        entries = [shear[r], ratio[r], scale[r]]
        entries += [moduli[r, k] for k in range(terms)] + [times[r, k] for k in range(terms)]
        for k, entry in enumerate(entries):
            tables[k, r : r + 1, :] = jnp.full((1, geo.lz), entry, jnp.float32)


SHEAR, RATIO, SCALE, MODULI = range(4)


def lookup(tables, entry, masks):
    value = tables[entry, len(masks) : len(masks) + 1, :]
    for r, mask in enumerate(masks):
        value = jnp.where(mask, tables[entry, r : r + 1, :], value)
    return value


def deviator(grad):
    trace_third = (grad[0][0] + grad[1][1] + grad[2][2]) / 3.0
    return [
        grad[0][0] - trace_third,
        grad[1][1] - trace_third,
        grad[2][2] - trace_third,
        0.5 * (grad[1][2] + grad[2][1]),
        0.5 * (grad[0][2] + grad[2][0]),
        0.5 * (grad[1][0] + grad[0][1]),
    ]


def contract(dev):
    return (
        dev[0] * dev[0]
        + dev[1] * dev[1]
        + dev[2] * dev[2]
        + 2.0 * (dev[3] * dev[3] + dev[4] * dev[4] + dev[5] * dev[5])
    )


def soften(energy, energy_next, scale, ratio):
    return 1.0 - lax.erf((energy_next - energy) / scale) / ratio


def basis_kernel(geo, where, *refs):
    tables, blocks, halos = refs[0], refs[1:-5:2], refs[2:-5:2]
    basis, dev_own, grams, held, field = refs[-5:]
    lx, ly, lz = geo.lx, geo.ly, geo.lz
    planes, rows, lanes = geo.bx * lx, geo.by * ly, 2 * lz
    regions = tables.shape[1]
    spots, _ = places(geo)
    row, lane = iota((rows, lanes), 0), iota((rows, lanes), 1)
    index_x, index_y, index_z = (lax.axis_index(name) for name in ("gx", "gy", "gz"))
    if geo.full:
        grid_row = jnp.where(row < ly, row + index_y * ly, row - index_y * ly)
    else:
        grid_row = index_y * ly + jnp.where(row < (1 + geo.hops_y) * ly, row, row - rows)
    end_y, start_y = grid_row == geo.gy * ly - 1, grid_row == 0
    end_z = (lane == lz - 1) & (index_z == geo.gz - 1)
    start_z = (lane == 0) & (index_z == 0)

    def next_plane(p):
        return p + 1 if p % lx + 1 < lx else geo.beside(p // lx, 1, index_x) * lx

    def prev_plane(p):
        return p - 1 if p % lx else geo.beside(p // lx, -1, index_x) * lx + lx - 1

    def whole_plane(f, p):
        tile, centre = spots[f * lx + p % lx]
        parts = []
        for b in range(geo.by):
            array, at = where[p // lx, b]
            left, right = halos[array][0, at, tile], halos[array][1, at, tile]
            edge = pltpu.roll(jnp.where(lane[:ly, :lz] < centre, left, right), lz - centre, 1)
            parts.append(jnp.concatenate([blocks[array][at, f * lx + p % lx], edge], axis=1))
        return jnp.concatenate(parts, axis=0)

    def beside(value):
        next_y = jnp.where(end_y, 0.0, pltpu.roll(value, rows - 1, 0))
        prev_y = jnp.where(start_y, 0.0, pltpu.roll(value, 1, 0))
        next_z = jnp.where(end_z, 0.0, pltpu.roll(value, lanes - 1, 1))
        prev_z = jnp.where(start_z, 0.0, pltpu.roll(value, 1, 1))
        return next_y, prev_y, next_z, prev_z

    for p in range(planes):
        for a in range(3):
            held[a, p] = whole_plane(a, p)
    for p in range(planes):
        grad = []
        for a in range(3):
            next_y, prev_y, next_z, prev_z = beside(held[a, p])
            next_x, prev_x = held[a, next_plane(p)], held[a, prev_plane(p)]
            grad.append([0.5 * (next_x - prev_x), 0.5 * (next_y - prev_y), 0.5 * (next_z - prev_z)])
        dev = deviator(grad)
        if p < lx:
            for k in range(6):
                dev_own[k, p] = dev[k][:ly, :lz]
        label = whole_plane(4, p)
        halves = []
        for half in (slice(0, lz), slice(lz, lanes)):
            masks = [label[:, half] == r for r in range(regions - 1)]
            halves.append([lookup(tables, entry, masks) for entry in (SHEAR, SCALE, RATIO)])
        shear_cells, scale_cells, ratio_cells = [jnp.concatenate(pair, axis=1) for pair in zip(*halves)]
        energy = shear_cells * contract(dev)
        energy_next = jnp.maximum(whole_plane(3, p), energy)
        softening = soften(energy, energy_next, scale_cells, ratio_cells)
        field[0, p] = softening * energy
    for j, shift in enumerate(SHIFTS):
        for p in range(planes):
            value = field[j, p]
            next_y, prev_y, next_z, prev_z = beside(value)
            next_x, prev_x = field[j, next_plane(p)], field[j, prev_plane(p)]
            image = (value - next_x) + (value - prev_x)
            image += (value - next_y) + (value - prev_y)
            image += (value - next_z) + (value - prev_z)
            field[j + 1, p] = image - shift * value if shift else image

    grams[...] = jnp.zeros(grams.shape, jnp.float32)
    sums = [jnp.zeros((ly, lz), jnp.float32)] * len(PAIRS)
    for p in range(planes if geo.full else lx):
        for b in range(geo.by if geo.full else 1):
            own = [field[j, p, b * ly : (b + 1) * ly, :lz] for j in range(ITERS + 1)]
            sums = [total + own[i] * own[j] for total, (i, j) in zip(sums, PAIRS)]
    for k, total in enumerate(sums):
        grams[k : k + 1, :] = jnp.sum(total, axis=0, keepdims=True)
    for i in range(lx):
        for j in range(ITERS + 1):
            basis[j, i] = field[j, i, :ly, :lz]


def visco_kernel(geo, where, *refs):
    tables, dev_own, visco, blocks, halos = refs[0], refs[1], refs[2], refs[3:-3:2], refs[4:-3:2]
    stress, visco_next, energy_next = refs[-3:]
    lx, ly, lz = geo.lx, geo.ly, geo.lz
    spots, _ = places(geo)
    row, lane = iota((ly, lz), 0), iota((ly, lz), 1)
    index_x, index_y = lax.axis_index("gx"), lax.axis_index("gy")
    regions, terms = tables.shape[1], visco.shape[0]

    def own(at, code_y=0):
        array, place = where[0, code_y % geo.by]
        return blocks[array][place, at]

    def along_x(step, at):
        target = geo.beside(0, step, index_x)
        if not geo.full:
            array, place = where[target, 0]
            return blocks[array][place, at]
        value = None
        for code in {geo.beside(0, step, index) for index in range(geo.gx)}:
            array, place = where[code, 0]
            found = blocks[array][place, at]
            value = found if value is None else jnp.where(target == code, found, value)
        return value

    for i in range(lx):
        grad = []
        for a in range(3):
            at = (WIDE + a) * lx + i
            value = own(at)
            next_x = own(at + 1) if i + 1 < lx else along_x(1, at + 1 - lx)
            prev_x = own(at - 1) if i else along_x(-1, at + lx - 1)
            first = jnp.where(index_y == geo.gy - 1, 0.0, own(at, 1))
            last = jnp.where(index_y == 0, 0.0, own(at, -1))
            next_y = pltpu.roll(jnp.where(row == 0, first, value), ly - 1, 0)
            prev_y = pltpu.roll(jnp.where(row == ly - 1, last, value), 1, 0)
            tile, centre = spots[at]
            left, right = halos[0][0, 0, tile], halos[0][1, 0, tile]
            next_z = jnp.where(lane == lz - 1, pltpu.roll(right, lz - 1 - centre, 1), pltpu.roll(value, lz - 1, 1))
            prev_z = jnp.where(lane == 0, pltpu.roll(left, lz + 1 - centre, 1), pltpu.roll(value, 1, 1))
            grad.append([0.5 * (next_x - prev_x), 0.5 * (next_y - prev_y), 0.5 * (next_z - prev_z)])
        dev_old = deviator(grad)
        dev_new = [dev_own[k, i] for k in range(6)]
        label = own(4 * lx + i)
        masks = [label == r for r in range(regions - 1)]
        shear_cells, ratio_cells, scale_cells = [lookup(tables, entry, masks) for entry in (SHEAR, RATIO, SCALE)]
        energy = shear_cells * contract(dev_new)
        energy_after = jnp.maximum(own(3 * lx + i), energy)
        energy_next[i] = energy_after
        softening = soften(energy, energy_after, scale_cells, ratio_cells)
        jump = [2.0 * shear_cells * (dev_new[k] - dev_old[k]) for k in range(6)]
        totals, long_term = [0.0] * 6, 1.0
        for term in range(terms):
            modulus = lookup(tables, MODULI + term, masks)
            time = lookup(tables, MODULI + terms + term, masks)
            decay = jnp.exp(-1.0 / time)
            weight = modulus * (1.0 - decay) * time
            long_term = long_term - modulus
            for k in range(6):
                value = decay * visco[term, k, i] + weight * jump[k]
                visco_next[term, k, i] = value
                totals[k] = totals[k] + value
        for k in range(6):
            stress[k, i] = softening * (long_term * 2.0 * shear_cells * dev_new[k] + totals[k])


def solve_kernel(geo, basis, *refs):
    grams, damage, residual = refs[:-2], refs[-2], refs[-1]
    total = functools.reduce(jnp.add, [part[...] for part in grams])
    column = jnp.sum(total, axis=1, keepdims=True)
    gram = {}
    for k, (i, j) in enumerate(PAIRS):
        gram[i, j] = gram[j, i] = column[k : k + 1]

    def image_of(p):
        out = [(1.0 + LENGTH_SQUARED * SHIFTS[j]) * p[j] for j in range(len(p))]
        out.append(LENGTH_SQUARED * p[-1])
        for j in range(1, len(p)):
            out[j] = out[j] + LENGTH_SQUARED * p[j - 1]
        return out

    def product(u, v):
        value = None
        for i in range(len(u)):
            inner = None
            for j in range(len(v)):
                inner = gram[i, j] * v[j] if inner is None else inner + gram[i, j] * v[j]
            value = u[i] * inner if value is None else value + u[i] * inner
        return value

    one = jnp.ones((1, 1), jnp.float32)
    field, rest, direction = [], [one], [one]
    norm_now = gram[0, 0]
    for iteration in range(ITERS):
        image = image_of(direction)
        alpha = norm_now / product(image, direction)
        field = [x + alpha * d for x, d in zip(field, direction)] + [alpha * direction[-1]]
        rest = [r - alpha * w for r, w in zip(rest, image)] + [-alpha * image[-1]]
        if iteration + 1 < ITERS:
            norm_next = product(rest, rest)
            beta = norm_next / norm_now
            direction = [r + beta * d for r, d in zip(rest, direction)] + [rest[-1]]
            norm_now = norm_next
    for i in range(geo.lx):
        vectors = [basis[j, i] for j in range(ITERS + 1)]
        damage[i] = functools.reduce(jnp.add, [c * t for c, t in zip(field, vectors)])
        residual[i] = functools.reduce(jnp.add, [c * t for c, t in zip(rest, vectors)])


def shaped(*shape):
    return jax.ShapeDtypeStruct(shape, jnp.float32)


def call(kernel, outs, arrays, scratch=(), flops=0, space=pltpu.VMEM, vmem=32 * MB):
    moved = 4 * sum(int(np.prod(a.shape)) for a in list(arrays) + list(outs))
    return pl.pallas_call(
        kernel,
        out_shape=outs,
        in_specs=[pl.BlockSpec(memory_space=space)] * len(arrays),
        out_specs=[pl.BlockSpec(memory_space=pltpu.VMEM)] * len(outs),
        scratch_shapes=list(scratch),
        compiler_params=pltpu.CompilerParams(vmem_limit_bytes=vmem),
        cost_estimate=pl.CostEstimate(flops=flops, bytes_accessed=moved, transcendentals=0),
    )(*arrays)


def moved(shard, axis, target):
    return lax.ppermute(shard, axis, [(i, target(i)) for i in range(lax.axis_size(axis))])


def ring(shard, axis, hops):
    count = lax.axis_size(axis)
    steps = list(range(hops + 1)) + list(range(-hops, 0))
    return jnp.stack([moved(shard, axis, lambda i: (i - step) % count) if step else shard for step in steps])


def edges_along_z(parts, geo):
    slabs = jnp.concatenate([part[FIELDS * geo.lx :] for part in parts])
    up = [(i, i + 1) for i in range(geo.gz - 1)]
    down = [(j, i) for i, j in up]
    pair = jnp.concatenate([lax.ppermute(slabs, "gz", up), lax.ppermute(slabs, "gz", down)])
    return pair.reshape((2, len(parts), -1) + pair.shape[1:])


def gathered(payload, geo):
    if not geo.full:
        blocks = ring(ring(payload, "gy", geo.hops_y), "gx", geo.hops_x)
        blocks = blocks.reshape((geo.bx * geo.by,) + payload.shape)
        where = {(x, y): (0, x * geo.by + y) for x in range(geo.bx) for y in range(geo.by)}
        return [blocks, edges_along_z(list(blocks), geo)], where
    codes = [(x, y) for x in range(0, geo.gx, 2) for y in range(geo.gy)]
    parts = [payload]
    for x, y in codes[1:]:
        parts.append(moved(payload, ("gx", "gy"), lambda i: (i // geo.gy ^ x) * geo.gy + (i % geo.gy ^ y)))
    blocks = jnp.concatenate(parts)
    halos = edges_along_z(parts, geo)
    where = {code: (0, place) for place, code in enumerate(codes)}
    shape = (len(parts),) + payload.shape
    if geo.gx == 1:
        return [blocks.reshape(shape), halos], where
    where.update({(x + 1, y): (1, place) for place, (x, y) in enumerate(codes)})
    other, other_halos = moved(blocks, "gx", lambda i: i ^ 1), moved(halos, "gx", lambda i: i ^ 1)
    return [blocks.reshape(shape), halos, other.reshape(shape), other_halos], where


def summed(terms, axis):
    count = lax.axis_size(axis)
    if count > 4:
        return [lax.psum(terms, axis)]
    return [terms] + [moved(terms, axis, lambda i: (i + step) % count) for step in range(1, count)]


def on_device(
    displacement,
    displacement_old,
    visco_state,
    energy_max,
    region,
    dirichlet,
    prony_moduli,
    prony_times,
    shear_modulus,
    mullins_ratio,
    mullins_scale,
):
    geo = geometry(energy_max.shape)
    lx, ly, lz = energy_max.shape
    _, tiles = places(geo)
    regions, terms = prony_moduli.shape
    arguments = [displacement, displacement_old, energy_max, region, dirichlet]
    parameters = [prony_moduli, prony_times, shear_modulus, mullins_ratio, mullins_scale]
    payload, tables = call(
        functools.partial(pack_kernel, geo),
        [shaped(FIELDS * lx + tiles, ly, lz), shaped(MODULI + 2 * terms, regions, lz)],
        arguments + parameters,
        [pltpu.VMEM(a.shape, a.dtype) for a in arguments]
        + [pltpu.SMEM(a.shape, a.dtype) for a in parameters]
        + [pltpu.SemaphoreType.DMA((len(arguments) + len(parameters),))],
        space=pl.ANY,
        vmem=56 * MB,
    )
    blocks, where = gathered(payload, geo)
    planes, rows = geo.bx * lx, geo.by * ly
    basis, dev_own, grams = call(
        functools.partial(basis_kernel, geo, where),
        [shaped(ITERS + 1, lx, ly, lz), shaped(6, lx, ly, lz), shaped(-(-len(PAIRS) // 8) * 8, lz)],
        [tables, *blocks],
        [
            pltpu.VMEM((3, planes, rows, 2 * lz), jnp.float32),
            pltpu.VMEM((ITERS + 1, planes, rows, 2 * lz), jnp.float32),
        ],
        flops=planes * rows * lz * 500,
    )
    if geo.full:
        sums = summed(grams, "gz")
    else:
        sums = [lax.psum(grams, ("gx", "gy", "gz"))]
    stress, visco_next, energy_next = call(
        functools.partial(visco_kernel, geo, where),
        [shaped(6, lx, ly, lz), shaped(*visco_state.shape), shaped(lx, ly, lz)],
        [tables, dev_own, visco_state, *blocks],
        flops=lx * ly * lz * 500,
    )
    damage_field, residual = call(
        functools.partial(solve_kernel, geo),
        [shaped(lx, ly, lz), shaped(lx, ly, lz)],
        [basis, *sums],
    )
    return (stress, visco_next, energy_next, damage_field, residual)


def solution(mesh):
    in_specs = (
        P(None, "gx", "gy", "gz"),
        P(None, "gx", "gy", "gz"),
        P(None, None, "gx", "gy", "gz"),
        P("gx", "gy", "gz"),
        P("gx", "gy", "gz"),
        P("gx", "gy", "gz"),
        P(),
        P(),
        P(),
        P(),
        P(),
    )
    out_specs = (
        P(None, "gx", "gy", "gz"),
        P(None, None, "gx", "gy", "gz"),
        P("gx", "gy", "gz"),
        P("gx", "gy", "gz"),
        P("gx", "gy", "gz"),
    )
    return jax.shard_map(
        on_device, mesh=mesh, in_specs=in_specs, out_specs=out_specs, check_vma=False
    )
```

```python
import functools
import typing

import jax
import jax.numpy as jnp
import numpy as np
from jax import lax
from jax.experimental import pallas as pl
from jax.experimental.pallas import tpu as pltpu
from jax.sharding import PartitionSpec as P

ITERS = 4
LENGTH_SQUARED = 4.0

SHIFTS = (0.0, 6.0, 1.5, 9.0)
PAIRS = [(i, j) for i in range(ITERS + 1) for j in range(i, ITERS + 1) if i < ITERS]

WIDE, NARROW = 5, 3
REACHES = (ITERS + 1,) * WIDE + (1,) * NARROW
FIELDS = WIDE + NARROW
MB = 1 << 20


class Geometry(typing.NamedTuple):
    lx: int
    ly: int
    lz: int
    gx: int
    gy: int
    gz: int
    hops_x: int
    hops_y: int
    full: bool

    @property
    def bx(self):
        return self.gx if self.full else 2 * self.hops_x + 1

    @property
    def by(self):
        return self.gy if self.full else 2 * self.hops_y + 1

    def beside(self, code, step, index_x):
        if not self.full:
            return (code + step) % self.bx
        return (((index_x ^ code) + step) & (self.gx - 1)) ^ index_x


def geometry(block):
    lx, ly, lz = block
    gx, gy, gz = (lax.axis_size(name) for name in ("gx", "gy", "gz"))
    hops_x, hops_y = -(-(ITERS + 1) // lx), -(-(ITERS + 1) // ly)
    full = gx <= 2 * hops_x + 1 and not gx & (gx - 1) and gy <= 2
    return Geometry(lx, ly, lz, gx, gy, gz, hops_x, hops_y, full)


def places(geo):
    result, tile, at = [], 0, 0
    for reach in REACHES:
        for _ in range(geo.lx):
            if at + 2 * reach > geo.lz:
                tile, at = tile + 1, 0
            result.append((tile, at + reach))
            at += 2 * reach
    return result, tile + 1


def iota(shape, dim):
    return lax.broadcasted_iota(jnp.int32, shape, dim)


def first_kernel(zeros):
    zeros[...] = jnp.zeros(zeros.shape, jnp.float32)


def pack_kernel(
    geo, moduli, times, shear, ratio, scale, zeros, new, old, energy_max, region, dirichlet, payload, tables
):
    spots, tiles = places(geo)
    lane = iota((geo.ly, geo.lz), 1)
    edges = [zeros[...]] * tiles
    for i in range(geo.lx):
        share = (1 - dirichlet[i]).astype(jnp.float32)
        values = [new[a, i] * share for a in range(3)]
        values += [energy_max[i], region[i].astype(jnp.float32)]
        values += [old[a, i] * share for a in range(3)]
        for f, value in enumerate(values):
            payload[f * geo.lx + i] = value
            tile, centre = spots[f * geo.lx + i]
            inside = (lane >= centre - REACHES[f]) & (lane < centre + REACHES[f])
            edges[tile] = jnp.where(inside, pltpu.roll(value, centre, 1), edges[tile])
    for tile in range(tiles):
        payload[FIELDS * geo.lx + tile] = edges[tile]
    regions, terms = moduli.shape
    for r in range(regions):
        entries = [shear[r], ratio[r], scale[r]]
        entries += [moduli[r, k] for k in range(terms)] + [times[r, k] for k in range(terms)]
        for k, entry in enumerate(entries):
            tables[k, r : r + 1, :] = jnp.full((1, geo.lz), entry, jnp.float32)


SHEAR, RATIO, SCALE, MODULI = range(4)


def lookup(tables, entry, masks):
    value = tables[entry, len(masks) : len(masks) + 1, :]
    for r, mask in enumerate(masks):
        value = jnp.where(mask, tables[entry, r : r + 1, :], value)
    return value


def deviator(grad):
    trace_third = (grad[0][0] + grad[1][1] + grad[2][2]) / 3.0
    return [
        grad[0][0] - trace_third,
        grad[1][1] - trace_third,
        grad[2][2] - trace_third,
        0.5 * (grad[1][2] + grad[2][1]),
        0.5 * (grad[0][2] + grad[2][0]),
        0.5 * (grad[1][0] + grad[0][1]),
    ]


def contract(dev):
    return (
        dev[0] * dev[0]
        + dev[1] * dev[1]
        + dev[2] * dev[2]
        + 2.0 * (dev[3] * dev[3] + dev[4] * dev[4] + dev[5] * dev[5])
    )


def soften(energy, energy_next, scale, ratio):
    return 1.0 - lax.erf((energy_next - energy) / scale) / ratio


def basis_kernel(geo, where, *refs):
    tables, blocks, halos = refs[0], refs[1:-5:2], refs[2:-5:2]
    basis, dev_own, grams, held, field = refs[-5:]
    lx, ly, lz = geo.lx, geo.ly, geo.lz
    planes, rows, lanes = geo.bx * lx, geo.by * ly, 2 * lz
    regions = tables.shape[1]
    spots, _ = places(geo)
    row, lane = iota((rows, lanes), 0), iota((rows, lanes), 1)
    index_x, index_y, index_z = (lax.axis_index(name) for name in ("gx", "gy", "gz"))
    if geo.full:
        grid_row = jnp.where(row < ly, row + index_y * ly, row - index_y * ly)
    else:
        grid_row = index_y * ly + jnp.where(row < (1 + geo.hops_y) * ly, row, row - rows)
    end_y, start_y = grid_row == geo.gy * ly - 1, grid_row == 0
    end_z = (lane == lz - 1) & (index_z == geo.gz - 1)
    start_z = (lane == 0) & (index_z == 0)

    def next_plane(p):
        return p + 1 if p % lx + 1 < lx else geo.beside(p // lx, 1, index_x) * lx

    def prev_plane(p):
        return p - 1 if p % lx else geo.beside(p // lx, -1, index_x) * lx + lx - 1

    def whole_plane(f, p):
        tile, centre = spots[f * lx + p % lx]
        parts = []
        for b in range(geo.by):
            array, at = where[p // lx, b]
            left, right = halos[array][0, at, tile], halos[array][1, at, tile]
            edge = pltpu.roll(jnp.where(lane[:ly, :lz] < centre, left, right), lz - centre, 1)
            parts.append(jnp.concatenate([blocks[array][at, f * lx + p % lx], edge], axis=1))
        return jnp.concatenate(parts, axis=0)

    def beside(value):
        next_y = jnp.where(end_y, 0.0, pltpu.roll(value, rows - 1, 0))
        prev_y = jnp.where(start_y, 0.0, pltpu.roll(value, 1, 0))
        next_z = jnp.where(end_z, 0.0, pltpu.roll(value, lanes - 1, 1))
        prev_z = jnp.where(start_z, 0.0, pltpu.roll(value, 1, 1))
        return next_y, prev_y, next_z, prev_z

    for p in range(planes):
        for a in range(3):
            held[a, p] = whole_plane(a, p)
    for p in range(planes):
        grad = []
        for a in range(3):
            next_y, prev_y, next_z, prev_z = beside(held[a, p])
            next_x, prev_x = held[a, next_plane(p)], held[a, prev_plane(p)]
            grad.append([0.5 * (next_x - prev_x), 0.5 * (next_y - prev_y), 0.5 * (next_z - prev_z)])
        dev = deviator(grad)
        if p < lx:
            for k in range(6):
                dev_own[k, p] = dev[k][:ly, :lz]
        label = whole_plane(4, p)
        halves = []
        for half in (slice(0, lz), slice(lz, lanes)):
            masks = [label[:, half] == r for r in range(regions - 1)]
            halves.append([lookup(tables, entry, masks) for entry in (SHEAR, SCALE, RATIO)])
        shear_cells, scale_cells, ratio_cells = [jnp.concatenate(pair, axis=1) for pair in zip(*halves)]
        energy = shear_cells * contract(dev)
        energy_next = jnp.maximum(whole_plane(3, p), energy)
        softening = soften(energy, energy_next, scale_cells, ratio_cells)
        field[0, p] = softening * energy
    for j, shift in enumerate(SHIFTS):
        for p in range(planes):
            value = field[j, p]
            next_y, prev_y, next_z, prev_z = beside(value)
            next_x, prev_x = field[j, next_plane(p)], field[j, prev_plane(p)]
            image = (value - next_x) + (value - prev_x)
            image += (value - next_y) + (value - prev_y)
            image += (value - next_z) + (value - prev_z)
            field[j + 1, p] = image - shift * value if shift else image

    grams[...] = jnp.zeros(grams.shape, jnp.float32)
    sums = [jnp.zeros((ly, lz), jnp.float32)] * len(PAIRS)
    for p in range(planes if geo.full else lx):
        for b in range(geo.by if geo.full else 1):
            own = [field[j, p, b * ly : (b + 1) * ly, :lz] for j in range(ITERS + 1)]
            sums = [total + own[i] * own[j] for total, (i, j) in zip(sums, PAIRS)]
    for k, total in enumerate(sums):
        grams[k : k + 1, :] = jnp.sum(total, axis=0, keepdims=True)
    for i in range(lx):
        for j in range(ITERS + 1):
            basis[j, i] = field[j, i, :ly, :lz]


def visco_kernel(geo, where, *refs):
    tables, dev_own, visco, blocks, halos = refs[0], refs[1], refs[2], refs[3:-3:2], refs[4:-3:2]
    stress, visco_next, energy_next = refs[-3:]
    lx, ly, lz = geo.lx, geo.ly, geo.lz
    spots, _ = places(geo)
    row, lane = iota((ly, lz), 0), iota((ly, lz), 1)
    index_x, index_y, index_z = (lax.axis_index(name) for name in ("gx", "gy", "gz"))
    regions, terms = tables.shape[1], visco.shape[0]

    def own(at, code_y=0):
        array, place = where[0, code_y % geo.by]
        return blocks[array][place, at]

    def along_x(step, at):
        target = geo.beside(0, step, index_x)
        if not geo.full:
            array, place = where[target, 0]
            return blocks[array][place, at]
        value = None
        for code in {geo.beside(0, step, index) for index in range(geo.gx)}:
            array, place = where[code, 0]
            found = blocks[array][place, at]
            value = found if value is None else jnp.where(target == code, found, value)
        return value

    for i in range(lx):
        grad = []
        for a in range(3):
            at = (WIDE + a) * lx + i
            value = own(at)
            next_x = own(at + 1) if i + 1 < lx else along_x(1, at + 1 - lx)
            prev_x = own(at - 1) if i else along_x(-1, at + lx - 1)
            first = jnp.where(index_y == geo.gy - 1, 0.0, own(at, 1))
            last = jnp.where(index_y == 0, 0.0, own(at, -1))
            next_y = pltpu.roll(jnp.where(row == 0, first, value), ly - 1, 0)
            prev_y = pltpu.roll(jnp.where(row == ly - 1, last, value), 1, 0)
            tile, centre = spots[at]
            left, right = halos[0][0, 0, tile], halos[0][1, 0, tile]
            right = jnp.where(index_z == geo.gz - 1, 0.0, pltpu.roll(right, lz - 1 - centre, 1))
            left = jnp.where(index_z == 0, 0.0, pltpu.roll(left, lz + 1 - centre, 1))
            next_z = jnp.where(lane == lz - 1, right, pltpu.roll(value, lz - 1, 1))
            prev_z = jnp.where(lane == 0, left, pltpu.roll(value, 1, 1))
            grad.append([0.5 * (next_x - prev_x), 0.5 * (next_y - prev_y), 0.5 * (next_z - prev_z)])
        dev_old = deviator(grad)
        dev_new = [dev_own[k, i] for k in range(6)]
        label = own(4 * lx + i)
        masks = [label == r for r in range(regions - 1)]
        shear_cells, ratio_cells, scale_cells = [lookup(tables, entry, masks) for entry in (SHEAR, RATIO, SCALE)]
        energy = shear_cells * contract(dev_new)
        energy_after = jnp.maximum(own(3 * lx + i), energy)
        energy_next[i] = energy_after
        softening = soften(energy, energy_after, scale_cells, ratio_cells)
        jump = [2.0 * shear_cells * (dev_new[k] - dev_old[k]) for k in range(6)]
        totals, long_term = [0.0] * 6, 1.0
        for term in range(terms):
            modulus = lookup(tables, MODULI + term, masks)
            time = lookup(tables, MODULI + terms + term, masks)
            decay = jnp.exp(-1.0 / time)
            weight = modulus * (1.0 - decay) * time
            long_term = long_term - modulus
            for k in range(6):
                value = decay * visco[term, k, i] + weight * jump[k]
                visco_next[term, k, i] = value
                totals[k] = totals[k] + value
        for k in range(6):
            stress[k, i] = softening * (long_term * 2.0 * shear_cells * dev_new[k] + totals[k])


def solve_kernel(geo, basis, *refs):
    grams, damage, residual = refs[:-2], refs[-2], refs[-1]
    total = functools.reduce(jnp.add, [part[...] for part in grams])
    column = jnp.sum(total, axis=1, keepdims=True)
    gram = {}
    for k, (i, j) in enumerate(PAIRS):
        gram[i, j] = gram[j, i] = column[k : k + 1]

    def image_of(p):
        out = [(1.0 + LENGTH_SQUARED * SHIFTS[j]) * p[j] for j in range(len(p))]
        out.append(LENGTH_SQUARED * p[-1])
        for j in range(1, len(p)):
            out[j] = out[j] + LENGTH_SQUARED * p[j - 1]
        return out

    def product(u, v):
        value = None
        for i in range(len(u)):
            inner = None
            for j in range(len(v)):
                inner = gram[i, j] * v[j] if inner is None else inner + gram[i, j] * v[j]
            value = u[i] * inner if value is None else value + u[i] * inner
        return value

    one = jnp.ones((1, 1), jnp.float32)
    field, rest, direction = [], [one], [one]
    norm_now = gram[0, 0]
    for iteration in range(ITERS):
        image = image_of(direction)
        alpha = norm_now / product(image, direction)
        field = [x + alpha * d for x, d in zip(field, direction)] + [alpha * direction[-1]]
        rest = [r - alpha * w for r, w in zip(rest, image)] + [-alpha * image[-1]]
        if iteration + 1 < ITERS:
            norm_next = product(rest, rest)
            beta = norm_next / norm_now
            direction = [r + beta * d for r, d in zip(rest, direction)] + [rest[-1]]
            norm_now = norm_next
    for i in range(geo.lx):
        vectors = [basis[j, i] for j in range(ITERS + 1)]
        damage[i] = functools.reduce(jnp.add, [c * t for c, t in zip(field, vectors)])
        residual[i] = functools.reduce(jnp.add, [c * t for c, t in zip(rest, vectors)])


def shaped(*shape):
    return jax.ShapeDtypeStruct(shape, jnp.float32)


def call(kernel, outs, arrays, scratch=(), flops=0, parameters=(), moved=None):
    if moved is None:
        moved = 4 * sum(int(np.prod(a.shape)) for a in list(arrays) + list(outs))
    smem, vmem = pl.BlockSpec(memory_space=pltpu.SMEM), pl.BlockSpec(memory_space=pltpu.VMEM)
    return pl.pallas_call(
        kernel,
        out_shape=outs,
        in_specs=[smem] * len(parameters) + [vmem] * len(arrays),
        out_specs=[vmem] * len(outs),
        scratch_shapes=list(scratch),
        compiler_params=pltpu.CompilerParams(vmem_limit_bytes=32 * MB),
        cost_estimate=pl.CostEstimate(flops=flops, bytes_accessed=moved, transcendentals=0),
    )(*parameters, *arrays)


def moved(shard, axis, target):
    return lax.ppermute(shard, axis, [(i, target(i)) for i in range(lax.axis_size(axis))])


def ring(shard, axis, hops):
    count = lax.axis_size(axis)
    steps = list(range(hops + 1)) + list(range(-hops, 0))
    return jnp.stack([moved(shard, axis, lambda i: (i - step) % count) if step else shard for step in steps])


def edges_along_z(slabs, blocks, geo):
    pair = jnp.concatenate([moved(slabs, "gz", lambda i: (i + step) % geo.gz) for step in (1, -1)])
    return pair.reshape((2, blocks, -1) + pair.shape[1:])


def assemble_kernel(geo, *refs):
    parts, blocks, slabs = refs[:-2], refs[-2], refs[-1]
    size, tiles = parts[0].shape[0], parts[0].shape[0] - FIELDS * geo.lx
    for n, part in enumerate(parts):
        blocks[n * size : (n + 1) * size] = part[...]
        slabs[n * tiles : (n + 1) * tiles] = part[FIELDS * geo.lx :]


def gathered(payload, geo):
    if not geo.full:
        blocks = ring(ring(payload, "gy", geo.hops_y), "gx", geo.hops_x)
        blocks = blocks.reshape((geo.bx * geo.by,) + payload.shape)
        where = {(x, y): (0, x * geo.by + y) for x in range(geo.bx) for y in range(geo.by)}
        slabs = blocks[:, FIELDS * geo.lx :].reshape((-1,) + payload.shape[1:])
        return [blocks, edges_along_z(slabs, blocks.shape[0], geo)], where
    codes = [(x, y) for x in range(0, geo.gx, 2) for y in range(geo.gy)]
    parts = [payload]
    for x, y in codes[1:]:
        parts.append(moved(payload, ("gx", "gy"), lambda i: (i // geo.gy ^ x) * geo.gy + (i % geo.gy ^ y)))
    size, plane = payload.shape[0], payload.shape[1:]
    tiles = size - FIELDS * geo.lx
    blocks, slabs = call(
        functools.partial(assemble_kernel, geo),
        [shaped(len(parts) * size, *plane), shaped(len(parts) * tiles, *plane)],
        parts,
    )
    halos = edges_along_z(slabs, len(parts), geo)
    where = {code: (0, place) for place, code in enumerate(codes)}
    shape = (len(parts),) + payload.shape
    if geo.gx == 1:
        return [blocks.reshape(shape), halos], where
    where.update({(x + 1, y): (1, place) for place, (x, y) in enumerate(codes)})
    other, other_halos = moved(blocks, "gx", lambda i: i ^ 1), moved(halos, "gx", lambda i: i ^ 1)
    return [blocks.reshape(shape), halos, other.reshape(shape), other_halos], where


def summed(terms, axis):
    count = lax.axis_size(axis)
    if count > 4:
        return [lax.psum(terms, axis)]
    return [terms] + [moved(terms, axis, lambda i: (i + step) % count) for step in range(1, count)]


def on_device(
    displacement,
    displacement_old,
    visco_state,
    energy_max,
    region,
    dirichlet,
    prony_moduli,
    prony_times,
    shear_modulus,
    mullins_ratio,
    mullins_scale,
):
    geo = geometry(energy_max.shape)
    lx, ly, lz = energy_max.shape
    _, tiles = places(geo)
    regions, terms = prony_moduli.shape
    (zeros,) = call(first_kernel, [shaped(ly, lz)], [], flops=1 << 34, moved=0)
    payload, tables = call(
        functools.partial(pack_kernel, geo),
        [shaped(FIELDS * lx + tiles, ly, lz), shaped(MODULI + 2 * terms, regions, lz)],
        [zeros, displacement, displacement_old, energy_max, region, dirichlet],
        parameters=[prony_moduli, prony_times, shear_modulus, mullins_ratio, mullins_scale],
    )
    blocks, where = gathered(payload, geo)
    planes, rows = geo.bx * lx, geo.by * ly
    basis, dev_own, grams = call(
        functools.partial(basis_kernel, geo, where),
        [shaped(ITERS + 1, lx, ly, lz), shaped(6, lx, ly, lz), shaped(-(-len(PAIRS) // 8) * 8, lz)],
        [tables, *blocks],
        [
            pltpu.VMEM((3, planes, rows, 2 * lz), jnp.float32),
            pltpu.VMEM((ITERS + 1, planes, rows, 2 * lz), jnp.float32),
        ],
        flops=planes * rows * lz * 500,
    )
    if geo.full:
        sums = summed(grams, "gz")
    else:
        sums = [lax.psum(grams, ("gx", "gy", "gz"))]
    stress, visco_next, energy_next = call(
        functools.partial(visco_kernel, geo, where),
        [shaped(6, lx, ly, lz), shaped(*visco_state.shape), shaped(lx, ly, lz)],
        [tables, dev_own, visco_state, *blocks],
        flops=lx * ly * lz * 500,
    )
    damage_field, residual = call(
        functools.partial(solve_kernel, geo),
        [shaped(lx, ly, lz), shaped(lx, ly, lz)],
        [basis, *sums],
    )
    return (stress, visco_next, energy_next, damage_field, residual)


def solution(mesh):
    in_specs = (
        P(None, "gx", "gy", "gz"),
        P(None, "gx", "gy", "gz"),
        P(None, None, "gx", "gy", "gz"),
        P("gx", "gy", "gz"),
        P("gx", "gy", "gz"),
        P("gx", "gy", "gz"),
        P(),
        P(),
        P(),
        P(),
        P(),
    )
    out_specs = (
        P(None, "gx", "gy", "gz"),
        P(None, None, "gx", "gy", "gz"),
        P("gx", "gy", "gz"),
        P("gx", "gy", "gz"),
        P("gx", "gy", "gz"),
    )
    return jax.shard_map(
        on_device, mesh=mesh, in_specs=in_specs, out_specs=out_specs, check_vma=False
    )
```

```python
import functools
import typing

import jax
import jax.numpy as jnp
import numpy as np
from jax import lax
from jax.experimental import pallas as pl
from jax.experimental.pallas import tpu as pltpu
from jax.sharding import PartitionSpec as P

ITERS = 4
LENGTH_SQUARED = 4.0

SHIFTS = (0.0, 6.0, 1.5, 9.0)
PAIRS = [(i, j) for i in range(ITERS + 1) for j in range(i, ITERS + 1) if i < ITERS]

WIDE, NARROW = 5, 3
REACHES = (ITERS + 1,) * WIDE + (1,) * NARROW
FIELDS = WIDE + NARROW
MB = 1 << 20


class Geometry(typing.NamedTuple):
    lx: int
    ly: int
    lz: int
    gx: int
    gy: int
    gz: int
    hops_x: int
    hops_y: int
    full: bool

    @property
    def bx(self):
        return self.gx if self.full else 2 * self.hops_x + 1

    @property
    def by(self):
        return self.gy if self.full else 2 * self.hops_y + 1

    @property
    def split(self):
        return self.full and self.gx > 1

    def beside(self, code, step, index_x):
        if not self.full:
            return (code + step) % self.bx
        return (((index_x ^ code) + step) & (self.gx - 1)) ^ index_x


def geometry(block):
    lx, ly, lz = block
    gx, gy, gz = (lax.axis_size(name) for name in ("gx", "gy", "gz"))
    hops_x, hops_y = -(-(ITERS + 1) // lx), -(-(ITERS + 1) // ly)
    full = gx <= 2 * hops_x + 1 and not gx & (gx - 1) and gy <= 2
    return Geometry(lx, ly, lz, gx, gy, gz, hops_x, hops_y, full)


def places(geo):
    result, tile, at = [], 0, 0
    for reach in REACHES:
        for _ in range(geo.lx):
            if at + 2 * reach > geo.lz:
                tile, at = tile + 1, 0
            result.append((tile, at + reach))
            at += 2 * reach
    return result, tile + 1


def iota(shape, dim):
    return lax.broadcasted_iota(jnp.int32, shape, dim)


def first_kernel(zeros):
    zeros[...] = jnp.zeros(zeros.shape, jnp.float32)


def pack_kernel(geo, zeros, new, old, energy_max, region, dirichlet, payload):
    spots, tiles = places(geo)
    lane = iota((geo.ly, geo.lz), 1)
    edges = [zeros[...]] * tiles
    for i in range(geo.lx):
        share = (1 - dirichlet[i]).astype(jnp.float32)
        values = [new[a, i] * share for a in range(3)]
        values += [energy_max[i], region[i].astype(jnp.float32)]
        values += [old[a, i] * share for a in range(3)]
        for f, value in enumerate(values):
            payload[f * geo.lx + i] = value
            tile, centre = spots[f * geo.lx + i]
            inside = (lane >= centre - REACHES[f]) & (lane < centre + REACHES[f])
            edges[tile] = jnp.where(inside, pltpu.roll(value, centre, 1), edges[tile])
    for tile in range(tiles):
        payload[FIELDS * geo.lx + tile] = edges[tile]


def tables_kernel(moduli, times, shear, ratio, scale, tables):
    regions, terms = moduli.shape
    for r in range(regions):
        entries = [shear[r], ratio[r], scale[r]]
        entries += [moduli[r, k] for k in range(terms)] + [times[r, k] for k in range(terms)]
        for k, entry in enumerate(entries):
            tables[k, r : r + 1, :] = jnp.full((1, tables.shape[2]), entry, jnp.float32)


SHEAR, RATIO, SCALE, MODULI = range(4)


def lookup(tables, entry, masks):
    value = tables[entry, len(masks) : len(masks) + 1, :]
    for r, mask in enumerate(masks):
        value = jnp.where(mask, tables[entry, r : r + 1, :], value)
    return value


def deviator(grad):
    trace_third = (grad[0][0] + grad[1][1] + grad[2][2]) / 3.0
    return [
        grad[0][0] - trace_third,
        grad[1][1] - trace_third,
        grad[2][2] - trace_third,
        0.5 * (grad[1][2] + grad[2][1]),
        0.5 * (grad[0][2] + grad[2][0]),
        0.5 * (grad[1][0] + grad[0][1]),
    ]


def contract(dev):
    return (
        dev[0] * dev[0]
        + dev[1] * dev[1]
        + dev[2] * dev[2]
        + 2.0 * (dev[3] * dev[3] + dev[4] * dev[4] + dev[5] * dev[5])
    )


def soften(energy, energy_next, scale, ratio):
    return 1.0 - lax.erf((energy_next - energy) / scale) / ratio


def z_edges(geo, halos, array, at, tile):
    count = halos[0].shape[0] // (2 if geo.split else 1)
    theirs = 1 - array if geo.split else array
    return halos[0][array * count + at, tile], halos[1][theirs * count + at, tile]


def basis_kernel(geo, where, *refs):
    tables, halos, blocks = refs[0], refs[1:3], refs[3:-5]
    basis, dev_own, grams, held, field = refs[-5:]
    lx, ly, lz = geo.lx, geo.ly, geo.lz
    planes, rows, lanes = geo.bx * lx, geo.by * ly, 2 * lz
    regions = tables.shape[1]
    spots, _ = places(geo)
    row, lane = iota((rows, lanes), 0), iota((rows, lanes), 1)
    index_x, index_y, index_z = (lax.axis_index(name) for name in ("gx", "gy", "gz"))
    if geo.full:
        grid_row = jnp.where(row < ly, row + index_y * ly, row - index_y * ly)
    else:
        grid_row = index_y * ly + jnp.where(row < (1 + geo.hops_y) * ly, row, row - rows)
    end_y, start_y = grid_row == geo.gy * ly - 1, grid_row == 0
    end_z = (lane == lz - 1) & (index_z == geo.gz - 1)
    start_z = (lane == 0) & (index_z == 0)

    upward = (index_x & 1) == 0 if geo.split else True

    def next_plane(p):
        return p + 1 if p % lx + 1 < lx else geo.beside(p // lx, 1, index_x) * lx

    def prev_plane(p):
        return p - 1 if p % lx else geo.beside(p // lx, -1, index_x) * lx + lx - 1

    def whole_plane(f, p):
        tile, centre = spots[f * lx + p % lx]
        parts = []
        for b in range(geo.by):
            array, at = where[p // lx, b]
            mine, theirs = z_edges(geo, halos, array, at, tile)
            edge = pltpu.roll(jnp.where((lane[:ly, :lz] < centre) ^ upward, theirs, mine), lz - centre, 1)
            parts.append(jnp.concatenate([blocks[array][at, f * lx + p % lx], edge], axis=1))
        return jnp.concatenate(parts, axis=0)

    def beside(value):
        next_y = jnp.where(end_y, 0.0, pltpu.roll(value, rows - 1, 0))
        prev_y = jnp.where(start_y, 0.0, pltpu.roll(value, 1, 0))
        next_z = jnp.where(end_z, 0.0, pltpu.roll(value, lanes - 1, 1))
        prev_z = jnp.where(start_z, 0.0, pltpu.roll(value, 1, 1))
        return next_y, prev_y, next_z, prev_z

    for p in range(planes):
        for a in range(3):
            held[a, p] = whole_plane(a, p)
    for p in range(planes):
        grad = []
        for a in range(3):
            next_y, prev_y, next_z, prev_z = beside(held[a, p])
            next_x, prev_x = held[a, next_plane(p)], held[a, prev_plane(p)]
            grad.append([0.5 * (next_x - prev_x), 0.5 * (next_y - prev_y), 0.5 * (next_z - prev_z)])
        dev = deviator(grad)
        if p < lx:
            for k in range(6):
                dev_own[k, p] = dev[k][:ly, :lz]
        label = whole_plane(4, p)
        halves = []
        for half in (slice(0, lz), slice(lz, lanes)):
            masks = [label[:, half] == r for r in range(regions - 1)]
            halves.append([lookup(tables, entry, masks) for entry in (SHEAR, SCALE, RATIO)])
        shear_cells, scale_cells, ratio_cells = [jnp.concatenate(pair, axis=1) for pair in zip(*halves)]
        energy = shear_cells * contract(dev)
        energy_next = jnp.maximum(whole_plane(3, p), energy)
        softening = soften(energy, energy_next, scale_cells, ratio_cells)
        field[0, p] = softening * energy
    for j, shift in enumerate(SHIFTS):
        for p in range(planes):
            value = field[j, p]
            next_y, prev_y, next_z, prev_z = beside(value)
            next_x, prev_x = field[j, next_plane(p)], field[j, prev_plane(p)]
            image = (value - next_x) + (value - prev_x)
            image += (value - next_y) + (value - prev_y)
            image += (value - next_z) + (value - prev_z)
            field[j + 1, p] = image - shift * value if shift else image

    grams[...] = jnp.zeros(grams.shape, jnp.float32)
    sums = [jnp.zeros((ly, lz), jnp.float32)] * len(PAIRS)
    for p in range(planes if geo.full else lx):
        for b in range(geo.by if geo.full else 1):
            own = [field[j, p, b * ly : (b + 1) * ly, :lz] for j in range(ITERS + 1)]
            sums = [total + own[i] * own[j] for total, (i, j) in zip(sums, PAIRS)]
    for k, total in enumerate(sums):
        grams[k : k + 1, :] = jnp.sum(total, axis=0, keepdims=True)
    for i in range(lx):
        for j in range(ITERS + 1):
            basis[j, i] = field[j, i, :ly, :lz]


def visco_kernel(geo, where, *refs):
    tables, dev_own, visco, halos, blocks = refs[0], refs[1], refs[2], refs[3:5], refs[5:-3]
    stress, visco_next, energy_next = refs[-3:]
    lx, ly, lz = geo.lx, geo.ly, geo.lz
    spots, _ = places(geo)
    row, lane = iota((ly, lz), 0), iota((ly, lz), 1)
    index_x, index_y, index_z = (lax.axis_index(name) for name in ("gx", "gy", "gz"))
    regions, terms = tables.shape[1], visco.shape[0]
    odd = (index_x & 1) == 1

    def own(at, code_y=0):
        array, place = where[0, code_y % geo.by]
        return blocks[array][place, at]

    def along_x(step, at):
        target = geo.beside(0, step, index_x)
        if not geo.full:
            array, place = where[target, 0]
            return blocks[array][place, at]
        value = None
        for code in {geo.beside(0, step, index) for index in range(geo.gx)}:
            array, place = where[code, 0]
            found = blocks[array][place, at]
            value = found if value is None else jnp.where(target == code, found, value)
        return value

    for i in range(lx):
        grad = []
        for a in range(3):
            at = (WIDE + a) * lx + i
            value = own(at)
            next_x = own(at + 1) if i + 1 < lx else along_x(1, at + 1 - lx)
            prev_x = own(at - 1) if i else along_x(-1, at + lx - 1)
            first = jnp.where(index_y == geo.gy - 1, 0.0, own(at, 1))
            last = jnp.where(index_y == 0, 0.0, own(at, -1))
            next_y = pltpu.roll(jnp.where(row == 0, first, value), ly - 1, 0)
            prev_y = pltpu.roll(jnp.where(row == ly - 1, last, value), 1, 0)
            tile, centre = spots[at]
            left, right = z_edges(geo, halos, 0, 0, tile)
            if geo.split:
                left, right = jnp.where(odd, right, left), jnp.where(odd, left, right)
            right = jnp.where(index_z == geo.gz - 1, 0.0, pltpu.roll(right, lz - 1 - centre, 1))
            left = jnp.where(index_z == 0, 0.0, pltpu.roll(left, lz + 1 - centre, 1))
            next_z = jnp.where(lane == lz - 1, right, pltpu.roll(value, lz - 1, 1))
            prev_z = jnp.where(lane == 0, left, pltpu.roll(value, 1, 1))
            grad.append([0.5 * (next_x - prev_x), 0.5 * (next_y - prev_y), 0.5 * (next_z - prev_z)])
        dev_old = deviator(grad)
        dev_new = [dev_own[k, i] for k in range(6)]
        label = own(4 * lx + i)
        masks = [label == r for r in range(regions - 1)]
        shear_cells, ratio_cells, scale_cells = [lookup(tables, entry, masks) for entry in (SHEAR, RATIO, SCALE)]
        energy = shear_cells * contract(dev_new)
        energy_after = jnp.maximum(own(3 * lx + i), energy)
        energy_next[i] = energy_after
        softening = soften(energy, energy_after, scale_cells, ratio_cells)
        jump = [2.0 * shear_cells * (dev_new[k] - dev_old[k]) for k in range(6)]
        totals, long_term = [0.0] * 6, 1.0
        for term in range(terms):
            modulus = lookup(tables, MODULI + term, masks)
            time = lookup(tables, MODULI + terms + term, masks)
            decay = jnp.exp(-1.0 / time)
            weight = modulus * (1.0 - decay) * time
            long_term = long_term - modulus
            for k in range(6):
                value = decay * visco[term, k, i] + weight * jump[k]
                visco_next[term, k, i] = value
                totals[k] = totals[k] + value
        for k in range(6):
            stress[k, i] = softening * (long_term * 2.0 * shear_cells * dev_new[k] + totals[k])


def solve_kernel(geo, basis, *refs):
    grams, damage, residual = refs[:-2], refs[-2], refs[-1]
    total = functools.reduce(jnp.add, [part[...] for part in grams])
    column = jnp.sum(total, axis=1, keepdims=True)
    gram = {}
    for k, (i, j) in enumerate(PAIRS):
        gram[i, j] = gram[j, i] = column[k : k + 1]

    def image_of(p):
        out = [(1.0 + LENGTH_SQUARED * SHIFTS[j]) * p[j] for j in range(len(p))]
        out.append(LENGTH_SQUARED * p[-1])
        for j in range(1, len(p)):
            out[j] = out[j] + LENGTH_SQUARED * p[j - 1]
        return out

    def product(u, v):
        value = None
        for i in range(len(u)):
            inner = None
            for j in range(len(v)):
                inner = gram[i, j] * v[j] if inner is None else inner + gram[i, j] * v[j]
            value = u[i] * inner if value is None else value + u[i] * inner
        return value

    one = jnp.ones((1, 1), jnp.float32)
    field, rest, direction = [], [one], [one]
    norm_now = gram[0, 0]
    for iteration in range(ITERS):
        image = image_of(direction)
        alpha = norm_now / product(image, direction)
        field = [x + alpha * d for x, d in zip(field, direction)] + [alpha * direction[-1]]
        rest = [r - alpha * w for r, w in zip(rest, image)] + [-alpha * image[-1]]
        if iteration + 1 < ITERS:
            norm_next = product(rest, rest)
            beta = norm_next / norm_now
            direction = [r + beta * d for r, d in zip(rest, direction)] + [rest[-1]]
            norm_now = norm_next
    for i in range(geo.lx):
        vectors = [basis[j, i] for j in range(ITERS + 1)]
        damage[i] = functools.reduce(jnp.add, [c * t for c, t in zip(field, vectors)])
        residual[i] = functools.reduce(jnp.add, [c * t for c, t in zip(rest, vectors)])


def shaped(*shape):
    return jax.ShapeDtypeStruct(shape, jnp.float32)


def call(kernel, outs, arrays, scratch=(), flops=0, parameters=(), moved=None):
    if moved is None:
        moved = 4 * sum(int(np.prod(a.shape)) for a in list(arrays) + list(outs))
    smem, vmem = pl.BlockSpec(memory_space=pltpu.SMEM), pl.BlockSpec(memory_space=pltpu.VMEM)
    return pl.pallas_call(
        kernel,
        out_shape=outs,
        in_specs=[smem] * len(parameters) + [vmem] * len(arrays),
        out_specs=[vmem] * len(outs),
        scratch_shapes=list(scratch),
        compiler_params=pltpu.CompilerParams(vmem_limit_bytes=32 * MB),
        cost_estimate=pl.CostEstimate(flops=flops, bytes_accessed=moved, transcendentals=0),
    )(*parameters, *arrays)


def moved(shard, axis, target):
    return lax.ppermute(shard, axis, [(i, target(i)) for i in range(lax.axis_size(axis))])


def ring(shard, axis, hops):
    count = lax.axis_size(axis)
    steps = list(range(hops + 1)) + list(range(-hops, 0))
    return jnp.stack([moved(shard, axis, lambda i: (i - step) % count) if step else shard for step in steps])


def assemble_kernel(geo, *refs):
    parts, blocks, slabs = refs[:-2], refs[-2], refs[-1]
    size, tiles = parts[0].shape[0], parts[0].shape[0] - FIELDS * geo.lx
    for n, part in enumerate(parts):
        blocks[n * size : (n + 1) * size] = part[...]
        slabs[n * tiles : (n + 1) * tiles] = part[FIELDS * geo.lx :]


def gathered(payload, geo):
    if not geo.full:
        blocks = ring(ring(payload, "gy", geo.hops_y), "gx", geo.hops_x)
        blocks = blocks.reshape((geo.bx * geo.by,) + payload.shape)
        where = {(x, y): (0, x * geo.by + y) for x in range(geo.bx) for y in range(geo.by)}
        slabs = blocks[:, FIELDS * geo.lx :]
        return [moved(slabs, "gz", lambda i: (i + step) % geo.gz) for step in (1, -1)] + [blocks], where
    codes = [(x, y) for x in range(0, geo.gx, 2) for y in range(geo.gy)]
    parts = [payload]
    for x, y in codes[1:]:
        parts.append(moved(payload, ("gx", "gy"), lambda i: (i // geo.gy ^ x) * geo.gy + (i % geo.gy ^ y)))
    size, plane = payload.shape[0], payload.shape[1:]
    tiles = size - FIELDS * geo.lx
    blocks, slabs = call(
        functools.partial(assemble_kernel, geo),
        [shaped(len(parts) * size, *plane), shaped(len(parts) * tiles, *plane)],
        parts,
    )
    where = {code: (0, place) for place, code in enumerate(codes)}
    shape, edge_shape = (len(parts),) + payload.shape, (-1, tiles) + plane
    if not geo.split:
        edges = [moved(slabs, "gz", lambda i: (i + step) % geo.gz) for step in (1, -1)]
        return [edge.reshape(edge_shape) for edge in edges] + [blocks.reshape(shape)], where
    where.update({(x + 1, y): (1, place) for place, (x, y) in enumerate(codes)})
    both = jnp.concatenate([slabs, moved(slabs, "gx", lambda i: i ^ 1)])
    other = moved(blocks, "gx", lambda i: i ^ 1)
    mine = moved(both, ("gx", "gz"), lambda i: i - i % geo.gz + (i % geo.gz + 1 - 2 * (i // geo.gz % 2)) % geo.gz)
    theirs = moved(mine, "gx", lambda i: i ^ 1)
    edges = [mine.reshape(edge_shape), theirs.reshape(edge_shape)]
    return edges + [blocks.reshape(shape), other.reshape(shape)], where


def summed(terms, axis):
    count = lax.axis_size(axis)
    if count > 4:
        return [lax.psum(terms, axis)]
    return [terms] + [moved(terms, axis, lambda i: (i + step) % count) for step in range(1, count)]


def on_device(
    displacement,
    displacement_old,
    visco_state,
    energy_max,
    region,
    dirichlet,
    prony_moduli,
    prony_times,
    shear_modulus,
    mullins_ratio,
    mullins_scale,
):
    geo = geometry(energy_max.shape)
    lx, ly, lz = energy_max.shape
    _, tiles = places(geo)
    regions, terms = prony_moduli.shape
    (zeros,) = call(first_kernel, [shaped(ly, lz)], [], flops=1 << 34, moved=0)
    (payload,) = call(
        functools.partial(pack_kernel, geo),
        [shaped(FIELDS * lx + tiles, ly, lz)],
        [zeros, displacement, displacement_old, energy_max, region, dirichlet],
    )
    (tables,) = call(
        tables_kernel,
        [shaped(MODULI + 2 * terms, regions, lz)],
        [],
        parameters=[prony_moduli, prony_times, shear_modulus, mullins_ratio, mullins_scale],
        flops=1 << 24,
    )
    blocks, where = gathered(payload, geo)
    planes, rows = geo.bx * lx, geo.by * ly
    basis, dev_own, grams = call(
        functools.partial(basis_kernel, geo, where),
        [shaped(ITERS + 1, lx, ly, lz), shaped(6, lx, ly, lz), shaped(-(-len(PAIRS) // 8) * 8, lz)],
        [tables, *blocks],
        [
            pltpu.VMEM((3, planes, rows, 2 * lz), jnp.float32),
            pltpu.VMEM((ITERS + 1, planes, rows, 2 * lz), jnp.float32),
        ],
        flops=planes * rows * lz * 500,
    )
    if geo.full:
        sums = summed(grams, "gz")
    else:
        sums = [lax.psum(grams, ("gx", "gy", "gz"))]
    stress, visco_next, energy_next = call(
        functools.partial(visco_kernel, geo, where),
        [shaped(6, lx, ly, lz), shaped(*visco_state.shape), shaped(lx, ly, lz)],
        [tables, dev_own, visco_state, *blocks],
        flops=lx * ly * lz * 500,
    )
    damage_field, residual = call(
        functools.partial(solve_kernel, geo),
        [shaped(lx, ly, lz), shaped(lx, ly, lz)],
        [basis, *sums],
    )
    return (stress, visco_next, energy_next, damage_field, residual)


def solution(mesh):
    in_specs = (
        P(None, "gx", "gy", "gz"),
        P(None, "gx", "gy", "gz"),
        P(None, None, "gx", "gy", "gz"),
        P("gx", "gy", "gz"),
        P("gx", "gy", "gz"),
        P("gx", "gy", "gz"),
        P(),
        P(),
        P(),
        P(),
        P(),
    )
    out_specs = (
        P(None, "gx", "gy", "gz"),
        P(None, None, "gx", "gy", "gz"),
        P("gx", "gy", "gz"),
        P("gx", "gy", "gz"),
        P("gx", "gy", "gz"),
    )
    return jax.shard_map(
        on_device, mesh=mesh, in_specs=in_specs, out_specs=out_specs, check_vma=False
    )
```

```python
import functools
import typing

import jax
import jax.numpy as jnp
import numpy as np
from jax import lax
from jax.experimental import pallas as pl
from jax.experimental.pallas import tpu as pltpu
from jax.sharding import PartitionSpec as P

ITERS = 4
LENGTH_SQUARED = 4.0

SHIFTS = (0.0, 6.0, 1.5, 9.0)
PAIRS = [(i, j) for i in range(ITERS + 1) for j in range(i, ITERS + 1) if i < ITERS]

WIDE, NARROW = 5, 3
REACHES = (ITERS + 1,) * WIDE + (1,) * NARROW
FIELDS = WIDE + NARROW
MB = 1 << 20


class Geometry(typing.NamedTuple):
    lx: int
    ly: int
    lz: int
    gx: int
    gy: int
    gz: int
    hops_x: int
    hops_y: int
    full: bool

    @property
    def bx(self):
        return self.gx if self.full else 2 * self.hops_x + 1

    @property
    def by(self):
        return self.gy if self.full else 2 * self.hops_y + 1

    @property
    def split(self):
        return self.full and self.gx > 1

    def beside(self, code, step, index_x):
        if not self.full:
            return (code + step) % self.bx
        return (((index_x ^ code) + step) & (self.gx - 1)) ^ index_x


def geometry(block):
    lx, ly, lz = block
    gx, gy, gz = (lax.axis_size(name) for name in ("gx", "gy", "gz"))
    hops_x, hops_y = -(-(ITERS + 1) // lx), -(-(ITERS + 1) // ly)
    full = gx <= 2 * hops_x + 1 and not gx & (gx - 1) and gy <= 2
    return Geometry(lx, ly, lz, gx, gy, gz, hops_x, hops_y, full)


def places(geo):
    result, tile, at = [], 0, 0
    for reach in REACHES:
        for _ in range(geo.lx):
            if at + 2 * reach > geo.lz:
                tile, at = tile + 1, 0
            result.append((tile, at + reach))
            at += 2 * reach
    return result, tile + 1


def iota(shape, dim):
    return lax.broadcasted_iota(jnp.int32, shape, dim)


def first_kernel(zeros):
    zeros[...] = jnp.zeros(zeros.shape, jnp.float32)


def pack_kernel(geo, zeros, new, old, energy_max, region, dirichlet, payload):
    spots, tiles = places(geo)
    lane = iota((geo.ly, geo.lz), 1)
    edges = [zeros[...]] * tiles
    for i in range(geo.lx):
        share = (1 - dirichlet[i]).astype(jnp.float32)
        values = [new[a, i] * share for a in range(3)]
        values += [energy_max[i], region[i].astype(jnp.float32)]
        values += [old[a, i] * share for a in range(3)]
        for f, value in enumerate(values):
            payload[f * geo.lx + i] = value
            tile, centre = spots[f * geo.lx + i]
            inside = (lane >= centre - REACHES[f]) & (lane < centre + REACHES[f])
            edges[tile] = jnp.where(inside, pltpu.roll(value, centre, 1), edges[tile])
    for tile in range(tiles):
        payload[FIELDS * geo.lx + tile] = edges[tile]


def tables_kernel(moduli, times, shear, ratio, scale, tables):
    regions, terms = moduli.shape
    for r in range(regions):
        entries = [shear[r], ratio[r], scale[r]]
        entries += [moduli[r, k] for k in range(terms)] + [times[r, k] for k in range(terms)]
        for k, entry in enumerate(entries):
            tables[k, r : r + 1, :] = jnp.full((1, tables.shape[2]), entry, jnp.float32)


SHEAR, RATIO, SCALE, MODULI = range(4)


def lookup(tables, entry, masks):
    value = tables[entry, len(masks) : len(masks) + 1, :]
    for r, mask in enumerate(masks):
        value = jnp.where(mask, tables[entry, r : r + 1, :], value)
    return value


def deviator(grad):
    trace_third = (grad[0][0] + grad[1][1] + grad[2][2]) / 3.0
    return [
        grad[0][0] - trace_third,
        grad[1][1] - trace_third,
        grad[2][2] - trace_third,
        0.5 * (grad[1][2] + grad[2][1]),
        0.5 * (grad[0][2] + grad[2][0]),
        0.5 * (grad[1][0] + grad[0][1]),
    ]


def contract(dev):
    return (
        dev[0] * dev[0]
        + dev[1] * dev[1]
        + dev[2] * dev[2]
        + 2.0 * (dev[3] * dev[3] + dev[4] * dev[4] + dev[5] * dev[5])
    )


def soften(energy, energy_next, scale, ratio):
    return 1.0 - lax.erf((energy_next - energy) / scale) / ratio


def z_edges(geo, halos, array, at, tile):
    place = array * (halos[0].shape[0] // (2 if geo.split else 1)) + at
    return halos[0][place, tile], halos[1][place, tile]


def basis_kernel(geo, where, *refs):
    tables, halos, blocks = refs[0], refs[1:3], refs[3:-5]
    basis, dev_own, grams, held, field = refs[-5:]
    lx, ly, lz = geo.lx, geo.ly, geo.lz
    planes, rows, lanes = geo.bx * lx, geo.by * ly, 2 * lz
    regions = tables.shape[1]
    spots, _ = places(geo)
    row, lane = iota((rows, lanes), 0), iota((rows, lanes), 1)
    index_x, index_y, index_z = (lax.axis_index(name) for name in ("gx", "gy", "gz"))
    if geo.full:
        grid_row = jnp.where(row < ly, row + index_y * ly, row - index_y * ly)
    else:
        grid_row = index_y * ly + jnp.where(row < (1 + geo.hops_y) * ly, row, row - rows)
    end_y, start_y = grid_row == geo.gy * ly - 1, grid_row == 0
    end_z = (lane == lz - 1) & (index_z == geo.gz - 1)
    start_z = (lane == 0) & (index_z == 0)

    upward = (index_x & 1) == 0 if geo.split else True

    def next_plane(p):
        return p + 1 if p % lx + 1 < lx else geo.beside(p // lx, 1, index_x) * lx

    def prev_plane(p):
        return p - 1 if p % lx else geo.beside(p // lx, -1, index_x) * lx + lx - 1

    def whole_plane(f, p):
        tile, centre = spots[f * lx + p % lx]
        parts = []
        for b in range(geo.by):
            array, at = where[p // lx, b]
            first, second = z_edges(geo, halos, array, at, tile)
            edge = pltpu.roll(jnp.where((lane[:ly, :lz] < centre) ^ upward, second, first), lz - centre, 1)
            parts.append(jnp.concatenate([blocks[array][at, f * lx + p % lx], edge], axis=1))
        return jnp.concatenate(parts, axis=0)

    def beside(value):
        next_y = jnp.where(end_y, 0.0, pltpu.roll(value, rows - 1, 0))
        prev_y = jnp.where(start_y, 0.0, pltpu.roll(value, 1, 0))
        next_z = jnp.where(end_z, 0.0, pltpu.roll(value, lanes - 1, 1))
        prev_z = jnp.where(start_z, 0.0, pltpu.roll(value, 1, 1))
        return next_y, prev_y, next_z, prev_z

    for p in range(planes):
        for a in range(3):
            held[a, p] = whole_plane(a, p)
    for p in range(planes):
        grad = []
        for a in range(3):
            next_y, prev_y, next_z, prev_z = beside(held[a, p])
            next_x, prev_x = held[a, next_plane(p)], held[a, prev_plane(p)]
            grad.append([0.5 * (next_x - prev_x), 0.5 * (next_y - prev_y), 0.5 * (next_z - prev_z)])
        dev = deviator(grad)
        if p < lx:
            for k in range(6):
                dev_own[k, p] = dev[k][:ly, :lz]
        label = whole_plane(4, p)
        halves = []
        for half in (slice(0, lz), slice(lz, lanes)):
            masks = [label[:, half] == r for r in range(regions - 1)]
            halves.append([lookup(tables, entry, masks) for entry in (SHEAR, SCALE, RATIO)])
        shear_cells, scale_cells, ratio_cells = [jnp.concatenate(pair, axis=1) for pair in zip(*halves)]
        energy = shear_cells * contract(dev)
        energy_next = jnp.maximum(whole_plane(3, p), energy)
        softening = soften(energy, energy_next, scale_cells, ratio_cells)
        field[0, p] = softening * energy
    for j, shift in enumerate(SHIFTS):
        for p in range(planes):
            value = field[j, p]
            next_y, prev_y, next_z, prev_z = beside(value)
            next_x, prev_x = field[j, next_plane(p)], field[j, prev_plane(p)]
            image = (value - next_x) + (value - prev_x)
            image += (value - next_y) + (value - prev_y)
            image += (value - next_z) + (value - prev_z)
            field[j + 1, p] = image - shift * value if shift else image

    grams[...] = jnp.zeros(grams.shape, jnp.float32)
    sums = [jnp.zeros((ly, lz), jnp.float32)] * len(PAIRS)
    for p in range(planes if geo.full else lx):
        for b in range(geo.by if geo.full else 1):
            own = [field[j, p, b * ly : (b + 1) * ly, :lz] for j in range(ITERS + 1)]
            sums = [total + own[i] * own[j] for total, (i, j) in zip(sums, PAIRS)]
    for k, total in enumerate(sums):
        grams[k : k + 1, :] = jnp.sum(total, axis=0, keepdims=True)
    for i in range(lx):
        for j in range(ITERS + 1):
            basis[j, i] = field[j, i, :ly, :lz]


def visco_kernel(geo, where, *refs):
    tables, dev_own, visco, halos, blocks = refs[0], refs[1], refs[2], refs[3:5], refs[5:-3]
    stress, visco_next, energy_next = refs[-3:]
    lx, ly, lz = geo.lx, geo.ly, geo.lz
    spots, _ = places(geo)
    row, lane = iota((ly, lz), 0), iota((ly, lz), 1)
    index_x, index_y, index_z = (lax.axis_index(name) for name in ("gx", "gy", "gz"))
    regions, terms = tables.shape[1], visco.shape[0]
    odd = (index_x & 1) == 1

    def own(at, code_y=0):
        array, place = where[0, code_y % geo.by]
        return blocks[array][place, at]

    def along_x(step, at):
        target = geo.beside(0, step, index_x)
        if not geo.full:
            array, place = where[target, 0]
            return blocks[array][place, at]
        value = None
        for code in {geo.beside(0, step, index) for index in range(geo.gx)}:
            array, place = where[code, 0]
            found = blocks[array][place, at]
            value = found if value is None else jnp.where(target == code, found, value)
        return value

    for i in range(lx):
        grad = []
        for a in range(3):
            at = (WIDE + a) * lx + i
            value = own(at)
            next_x = own(at + 1) if i + 1 < lx else along_x(1, at + 1 - lx)
            prev_x = own(at - 1) if i else along_x(-1, at + lx - 1)
            first = jnp.where(index_y == geo.gy - 1, 0.0, own(at, 1))
            last = jnp.where(index_y == 0, 0.0, own(at, -1))
            next_y = pltpu.roll(jnp.where(row == 0, first, value), ly - 1, 0)
            prev_y = pltpu.roll(jnp.where(row == ly - 1, last, value), 1, 0)
            tile, centre = spots[at]
            left, right = z_edges(geo, halos, 0, 0, tile)
            if geo.split:
                left, right = jnp.where(odd, right, left), jnp.where(odd, left, right)
            right = jnp.where(index_z == geo.gz - 1, 0.0, pltpu.roll(right, lz - 1 - centre, 1))
            left = jnp.where(index_z == 0, 0.0, pltpu.roll(left, lz + 1 - centre, 1))
            next_z = jnp.where(lane == lz - 1, right, pltpu.roll(value, lz - 1, 1))
            prev_z = jnp.where(lane == 0, left, pltpu.roll(value, 1, 1))
            grad.append([0.5 * (next_x - prev_x), 0.5 * (next_y - prev_y), 0.5 * (next_z - prev_z)])
        dev_old = deviator(grad)
        dev_new = [dev_own[k, i] for k in range(6)]
        label = own(4 * lx + i)
        masks = [label == r for r in range(regions - 1)]
        shear_cells, ratio_cells, scale_cells = [lookup(tables, entry, masks) for entry in (SHEAR, RATIO, SCALE)]
        energy = shear_cells * contract(dev_new)
        energy_after = jnp.maximum(own(3 * lx + i), energy)
        energy_next[i] = energy_after
        softening = soften(energy, energy_after, scale_cells, ratio_cells)
        jump = [2.0 * shear_cells * (dev_new[k] - dev_old[k]) for k in range(6)]
        totals, long_term = [0.0] * 6, 1.0
        for term in range(terms):
            modulus = lookup(tables, MODULI + term, masks)
            time = lookup(tables, MODULI + terms + term, masks)
            decay = jnp.exp(-1.0 / time)
            weight = modulus * (1.0 - decay) * time
            long_term = long_term - modulus
            for k in range(6):
                value = decay * visco[term, k, i] + weight * jump[k]
                visco_next[term, k, i] = value
                totals[k] = totals[k] + value
        for k in range(6):
            stress[k, i] = softening * (long_term * 2.0 * shear_cells * dev_new[k] + totals[k])


def solve_kernel(geo, basis, *refs):
    grams, damage, residual = refs[:-2], refs[-2], refs[-1]
    total = functools.reduce(jnp.add, [part[...] for part in grams])
    column = jnp.sum(total, axis=1, keepdims=True)
    gram = {}
    for k, (i, j) in enumerate(PAIRS):
        gram[i, j] = gram[j, i] = column[k : k + 1]

    def image_of(p):
        out = [(1.0 + LENGTH_SQUARED * SHIFTS[j]) * p[j] for j in range(len(p))]
        out.append(LENGTH_SQUARED * p[-1])
        for j in range(1, len(p)):
            out[j] = out[j] + LENGTH_SQUARED * p[j - 1]
        return out

    def product(u, v):
        value = None
        for i in range(len(u)):
            inner = None
            for j in range(len(v)):
                inner = gram[i, j] * v[j] if inner is None else inner + gram[i, j] * v[j]
            value = u[i] * inner if value is None else value + u[i] * inner
        return value

    one = jnp.ones((1, 1), jnp.float32)
    field, rest, direction = [], [one], [one]
    norm_now = gram[0, 0]
    for iteration in range(ITERS):
        image = image_of(direction)
        alpha = norm_now / product(image, direction)
        field = [x + alpha * d for x, d in zip(field, direction)] + [alpha * direction[-1]]
        rest = [r - alpha * w for r, w in zip(rest, image)] + [-alpha * image[-1]]
        if iteration + 1 < ITERS:
            norm_next = product(rest, rest)
            beta = norm_next / norm_now
            direction = [r + beta * d for r, d in zip(rest, direction)] + [rest[-1]]
            norm_now = norm_next
    for i in range(geo.lx):
        vectors = [basis[j, i] for j in range(ITERS + 1)]
        damage[i] = functools.reduce(jnp.add, [c * t for c, t in zip(field, vectors)])
        residual[i] = functools.reduce(jnp.add, [c * t for c, t in zip(rest, vectors)])


def shaped(*shape):
    return jax.ShapeDtypeStruct(shape, jnp.float32)


def call(kernel, outs, arrays, scratch=(), flops=0, parameters=(), moved=None):
    if moved is None:
        moved = 4 * sum(int(np.prod(a.shape)) for a in list(arrays) + list(outs))
    smem, vmem = pl.BlockSpec(memory_space=pltpu.SMEM), pl.BlockSpec(memory_space=pltpu.VMEM)
    return pl.pallas_call(
        kernel,
        out_shape=outs,
        in_specs=[smem] * len(parameters) + [vmem] * len(arrays),
        out_specs=[vmem] * len(outs),
        scratch_shapes=list(scratch),
        compiler_params=pltpu.CompilerParams(vmem_limit_bytes=32 * MB),
        cost_estimate=pl.CostEstimate(flops=flops, bytes_accessed=moved, transcendentals=0),
    )(*parameters, *arrays)


def moved(shard, axis, target):
    return lax.ppermute(shard, axis, [(i, target(i)) for i in range(lax.axis_size(axis))])


def ring(shard, axis, hops):
    count = lax.axis_size(axis)
    steps = list(range(hops + 1)) + list(range(-hops, 0))
    return jnp.stack([moved(shard, axis, lambda i: (i - step) % count) if step else shard for step in steps])


def assemble_kernel(*refs):
    parts, blocks = refs[:-1], refs[-1]
    size = parts[0].shape[0]
    for n, part in enumerate(parts):
        blocks[n * size : (n + 1) * size] = part[...]


def slabs_kernel(geo, *refs):
    arrays, slabs = refs[:-1], refs[-1]
    place = 0
    for array in arrays:
        for n in range(array.shape[0]):
            slabs[place] = array[n, FIELDS * geo.lx :]
            place += 1


def gathered(payload, geo):
    if not geo.full:
        blocks = ring(ring(payload, "gy", geo.hops_y), "gx", geo.hops_x)
        blocks = blocks.reshape((geo.bx * geo.by,) + payload.shape)
        where = {(x, y): (0, x * geo.by + y) for x in range(geo.bx) for y in range(geo.by)}
        slabs = blocks[:, FIELDS * geo.lx :]
        return [moved(slabs, "gz", lambda i: (i + step) % geo.gz) for step in (1, -1)] + [blocks], where
    codes = [(0, 0)] + [(x, y) for x in range(0, geo.gx, 2) for y in range(geo.gy) if x or y][::-1]
    parts = [payload]
    for x, y in codes[1:]:
        parts.append(moved(payload, ("gx", "gy"), lambda i: (i // geo.gy ^ x) * geo.gy + (i % geo.gy ^ y)))
    size, plane = payload.shape[0], payload.shape[1:]
    (blocks,) = call(assemble_kernel, [shaped(len(parts) * size, *plane)], parts)
    where = {code: (0, place) for place, code in enumerate(codes)}
    arrays = [blocks.reshape((len(parts),) + payload.shape)]
    if geo.split:
        where.update({(x + 1, y): (1, place) for place, (x, y) in enumerate(codes)})
        arrays.append(moved(arrays[0], "gx", lambda i: i ^ 1))
    tiles = size - FIELDS * geo.lx
    (slabs,) = call(functools.partial(slabs_kernel, geo), [shaped(len(arrays) * len(parts), tiles, *plane)], arrays)
    if not geo.split:
        return [moved(slabs, "gz", lambda i: (i + step) % geo.gz) for step in (1, -1)] + arrays, where
    ring_of_gz = []
    for i in range(geo.gx * geo.gz):
        x, z = divmod(i, geo.gz)
        ahead = z + 1 - 2 * (x % 2)
        ring_of_gz.append((i, x * geo.gz + ahead if 0 <= ahead < geo.gz else (x ^ 1) * geo.gz + z))
    first = lax.ppermute(slabs, ("gx", "gz"), ring_of_gz)
    second = lax.ppermute(slabs, ("gx", "gz"), [(b, a) for a, b in ring_of_gz])
    return [first, second] + arrays, where


def summed(terms, axis):
    count = lax.axis_size(axis)
    if count not in (1, 2, 4):
        return [lax.psum(terms, axis)]
    return [terms] + [moved(terms, axis, lambda i: i ^ step) for step in reversed(range(1, count))]


def on_device(
    displacement,
    displacement_old,
    visco_state,
    energy_max,
    region,
    dirichlet,
    prony_moduli,
    prony_times,
    shear_modulus,
    mullins_ratio,
    mullins_scale,
):
    geo = geometry(energy_max.shape)
    lx, ly, lz = energy_max.shape
    _, tiles = places(geo)
    regions, terms = prony_moduli.shape
    (zeros,) = call(first_kernel, [shaped(ly, lz)], [], flops=1 << 34, moved=0)
    (payload,) = call(
        functools.partial(pack_kernel, geo),
        [shaped(FIELDS * lx + tiles, ly, lz)],
        [zeros, displacement, displacement_old, energy_max, region, dirichlet],
    )
    (tables,) = call(
        tables_kernel,
        [shaped(MODULI + 2 * terms, regions, lz)],
        [],
        parameters=[prony_moduli, prony_times, shear_modulus, mullins_ratio, mullins_scale],
        flops=1 << 24,
    )
    blocks, where = gathered(payload, geo)
    planes, rows = geo.bx * lx, geo.by * ly
    basis, dev_own, grams = call(
        functools.partial(basis_kernel, geo, where),
        [shaped(ITERS + 1, lx, ly, lz), shaped(6, lx, ly, lz), shaped(-(-len(PAIRS) // 8) * 8, lz)],
        [tables, *blocks],
        [
            pltpu.VMEM((3, planes, rows, 2 * lz), jnp.float32),
            pltpu.VMEM((ITERS + 1, planes, rows, 2 * lz), jnp.float32),
        ],
        flops=planes * rows * lz * 500,
    )
    if geo.full:
        sums = summed(grams, "gz")
    else:
        sums = [lax.psum(grams, ("gx", "gy", "gz"))]
    stress, visco_next, energy_next = call(
        functools.partial(visco_kernel, geo, where),
        [shaped(6, lx, ly, lz), shaped(*visco_state.shape), shaped(lx, ly, lz)],
        [tables, dev_own, visco_state, *blocks],
        flops=lx * ly * lz * 500,
    )
    damage_field, residual = call(
        functools.partial(solve_kernel, geo),
        [shaped(lx, ly, lz), shaped(lx, ly, lz)],
        [basis, *sums],
    )
    return (stress, visco_next, energy_next, damage_field, residual)


def solution(mesh):
    in_specs = (
        P(None, "gx", "gy", "gz"),
        P(None, "gx", "gy", "gz"),
        P(None, None, "gx", "gy", "gz"),
        P("gx", "gy", "gz"),
        P("gx", "gy", "gz"),
        P("gx", "gy", "gz"),
        P(),
        P(),
        P(),
        P(),
        P(),
    )
    out_specs = (
        P(None, "gx", "gy", "gz"),
        P(None, None, "gx", "gy", "gz"),
        P("gx", "gy", "gz"),
        P("gx", "gy", "gz"),
        P("gx", "gy", "gz"),
    )
    return jax.shard_map(
        on_device, mesh=mesh, in_specs=in_specs, out_specs=out_specs, check_vma=False
    )
```

```python
import functools
import typing

import jax
import jax.numpy as jnp
import numpy as np
from jax import lax
from jax.experimental import pallas as pl
from jax.experimental.pallas import tpu as pltpu
from jax.sharding import PartitionSpec as P

ITERS = 4
LENGTH_SQUARED = 4.0

SHIFTS = (0.0, 6.0, 1.5, 9.0)
PAIRS = [(i, j) for i in range(ITERS + 1) for j in range(i, ITERS + 1) if i < ITERS]

WIDE, NARROW = 5, 3
REACHES = (ITERS + 1,) * WIDE + (1,) * NARROW
FIELDS = WIDE + NARROW
MB = 1 << 20


class Geometry(typing.NamedTuple):
    lx: int
    ly: int
    lz: int
    gx: int
    gy: int
    gz: int
    hops_x: int
    hops_y: int
    full: bool

    @property
    def bx(self):
        return self.gx if self.full else 2 * self.hops_x + 1

    @property
    def by(self):
        return self.gy if self.full else 2 * self.hops_y + 1

    @property
    def split(self):
        return self.full and self.gx > 1

    def beside(self, code, step, index_x):
        if not self.full:
            return (code + step) % self.bx
        return (((index_x ^ code) + step) & (self.gx - 1)) ^ index_x


def geometry(block):
    lx, ly, lz = block
    gx, gy, gz = (lax.axis_size(name) for name in ("gx", "gy", "gz"))
    hops_x, hops_y = -(-(ITERS + 1) // lx), -(-(ITERS + 1) // ly)
    full = gx <= 2 * hops_x + 1 and not gx & (gx - 1) and gy <= 2
    return Geometry(lx, ly, lz, gx, gy, gz, hops_x, hops_y, full)


def places(geo):
    result, tile, at = [], 0, 0
    for reach in REACHES:
        for _ in range(geo.lx):
            if at + 2 * reach > geo.lz:
                tile, at = tile + 1, 0
            result.append((tile, at + reach))
            at += 2 * reach
    return result, tile + 1


class Layout(typing.NamedTuple):
    edges: int
    rows: int
    old: int
    size: int


def layout(geo):
    edges = WIDE * geo.lx
    rows = edges + places(geo)[1]
    old = rows - (-NARROW * geo.lx // geo.ly)
    return Layout(edges, rows, old, old + NARROW * geo.lx)


def iota(shape, dim):
    return lax.broadcasted_iota(jnp.int32, shape, dim)


def first_kernel(zeros):
    zeros[...] = jnp.zeros(zeros.shape, jnp.float32)


def pack_kernel(geo, zeros, new, old, energy_max, region, dirichlet, *payloads):
    spots, tiles = places(geo)
    lay = layout(geo)
    row, lane = iota((geo.ly, geo.lz), 0), iota((geo.ly, geo.lz), 1)
    top = lax.axis_index("gy") == 0
    edges, rows = [zeros[...]] * tiles, [zeros[...]] * (lay.old - lay.rows)

    def write(at, value):
        for payload in payloads:
            if at < payload.shape[0]:
                payload[at] = value

    for i in range(geo.lx):
        share = (1 - dirichlet[i]).astype(jnp.float32)
        values = [new[a, i] * share for a in range(3)]
        values += [energy_max[i], region[i].astype(jnp.float32)]
        values += [old[a, i] * share for a in range(3)]
        for f, value in enumerate(values):
            at = f * geo.lx + i
            tile, centre = spots[at]
            inside = (lane >= centre - REACHES[f]) & (lane < centre + REACHES[f])
            edges[tile] = jnp.where(inside, pltpu.roll(value, centre, 1), edges[tile])
            if f < WIDE:
                write(at, value)
                continue
            at -= WIDE * geo.lx
            write(lay.old + at, value)
            facing = jnp.where(top, value[geo.ly - 1 :], value[:1])
            rows[at // geo.ly] = jnp.where(row == at % geo.ly, facing, rows[at // geo.ly])
    for n, value in enumerate(edges + rows):
        write(lay.edges + n, value)


def tables_kernel(moduli, times, shear, ratio, scale, tables):
    regions, terms = moduli.shape
    for r in range(regions):
        entries = [shear[r], ratio[r], scale[r]]
        entries += [moduli[r, k] for k in range(terms)] + [times[r, k] for k in range(terms)]
        for k, entry in enumerate(entries):
            tables[k, r : r + 1, :] = jnp.full((1, tables.shape[2]), entry, jnp.float32)


SHEAR, RATIO, SCALE, MODULI = range(4)


def lookup(tables, entry, masks):
    value = tables[entry, len(masks) : len(masks) + 1, :]
    for r, mask in enumerate(masks):
        value = jnp.where(mask, tables[entry, r : r + 1, :], value)
    return value


def deviator(grad):
    trace_third = (grad[0][0] + grad[1][1] + grad[2][2]) / 3.0
    return [
        grad[0][0] - trace_third,
        grad[1][1] - trace_third,
        grad[2][2] - trace_third,
        0.5 * (grad[1][2] + grad[2][1]),
        0.5 * (grad[0][2] + grad[2][0]),
        0.5 * (grad[1][0] + grad[0][1]),
    ]


def contract(dev):
    return (
        dev[0] * dev[0]
        + dev[1] * dev[1]
        + dev[2] * dev[2]
        + 2.0 * (dev[3] * dev[3] + dev[4] * dev[4] + dev[5] * dev[5])
    )


def soften(energy, energy_next, scale, ratio):
    return 1.0 - lax.erf((energy_next - energy) / scale) / ratio


class Place(typing.NamedTuple):
    array: int
    start: int
    edge: int


def basis_kernel(geo, where, *refs):
    tables, halos, blocks = refs[0], refs[1:3], refs[3:-5]
    basis, dev_own, grams, held, field = refs[-5:]
    lx, ly, lz = geo.lx, geo.ly, geo.lz
    planes, rows, lanes = geo.bx * lx, geo.by * ly, 2 * lz
    regions = tables.shape[1]
    spots, _ = places(geo)
    row, lane = iota((rows, lanes), 0), iota((rows, lanes), 1)
    index_x, index_y, index_z = (lax.axis_index(name) for name in ("gx", "gy", "gz"))
    if geo.full:
        grid_row = jnp.where(row < ly, row + index_y * ly, row - index_y * ly)
    else:
        grid_row = index_y * ly + jnp.where(row < (1 + geo.hops_y) * ly, row, row - rows)
    end_y, start_y = grid_row == geo.gy * ly - 1, grid_row == 0
    end_z = (lane == lz - 1) & (index_z == geo.gz - 1)
    start_z = (lane == 0) & (index_z == 0)

    upward = (index_x & 1) == 0 if geo.split else True

    def next_plane(p):
        return p + 1 if p % lx + 1 < lx else geo.beside(p // lx, 1, index_x) * lx

    def prev_plane(p):
        return p - 1 if p % lx else geo.beside(p // lx, -1, index_x) * lx + lx - 1

    def whole_plane(f, p):
        tile, centre = spots[f * lx + p % lx]
        parts = []
        for b in range(geo.by):
            array, start, place = where[p // lx, b]
            first, second = halos[0][place, tile], halos[1][place, tile]
            edge = pltpu.roll(jnp.where((lane[:ly, :lz] < centre) ^ upward, second, first), lz - centre, 1)
            parts.append(jnp.concatenate([blocks[array][start + f * lx + p % lx], edge], axis=1))
        return jnp.concatenate(parts, axis=0)

    def beside(value):
        next_y = jnp.where(end_y, 0.0, pltpu.roll(value, rows - 1, 0))
        prev_y = jnp.where(start_y, 0.0, pltpu.roll(value, 1, 0))
        next_z = jnp.where(end_z, 0.0, pltpu.roll(value, lanes - 1, 1))
        prev_z = jnp.where(start_z, 0.0, pltpu.roll(value, 1, 1))
        return next_y, prev_y, next_z, prev_z

    for p in range(planes):
        for a in range(3):
            held[a, p] = whole_plane(a, p)
    for p in range(planes):
        grad = []
        for a in range(3):
            next_y, prev_y, next_z, prev_z = beside(held[a, p])
            next_x, prev_x = held[a, next_plane(p)], held[a, prev_plane(p)]
            grad.append([0.5 * (next_x - prev_x), 0.5 * (next_y - prev_y), 0.5 * (next_z - prev_z)])
        dev = deviator(grad)
        if p < lx:
            for k in range(6):
                dev_own[k, p] = dev[k][:ly, :lz]
        label = whole_plane(4, p)
        halves = []
        for half in (slice(0, lz), slice(lz, lanes)):
            masks = [label[:, half] == r for r in range(regions - 1)]
            halves.append([lookup(tables, entry, masks) for entry in (SHEAR, SCALE, RATIO)])
        shear_cells, scale_cells, ratio_cells = [jnp.concatenate(pair, axis=1) for pair in zip(*halves)]
        energy = shear_cells * contract(dev)
        energy_next = jnp.maximum(whole_plane(3, p), energy)
        softening = soften(energy, energy_next, scale_cells, ratio_cells)
        field[0, p] = softening * energy
    for j, shift in enumerate(SHIFTS):
        for p in range(planes):
            value = field[j, p]
            next_y, prev_y, next_z, prev_z = beside(value)
            next_x, prev_x = field[j, next_plane(p)], field[j, prev_plane(p)]
            image = (value - next_x) + (value - prev_x)
            image += (value - next_y) + (value - prev_y)
            image += (value - next_z) + (value - prev_z)
            field[j + 1, p] = image - shift * value if shift else image

    grams[...] = jnp.zeros(grams.shape, jnp.float32)
    sums = [jnp.zeros((ly, lz), jnp.float32)] * len(PAIRS)
    for p in range(planes if geo.full else lx):
        for b in range(geo.by if geo.full else 1):
            own = [field[j, p, b * ly : (b + 1) * ly, :lz] for j in range(ITERS + 1)]
            sums = [total + own[i] * own[j] for total, (i, j) in zip(sums, PAIRS)]
    for k, total in enumerate(sums):
        grams[k : k + 1, :] = jnp.sum(total, axis=0, keepdims=True)
    for i in range(lx):
        for j in range(ITERS + 1):
            basis[j, i] = field[j, i, :ly, :lz]


def visco_kernel(geo, where, *refs):
    tables, dev_own, visco, halos, blocks = refs[0], refs[1], refs[2], refs[3:5], refs[5:-3]
    stress, visco_next, energy_next = refs[-3:]
    lx, ly, lz = geo.lx, geo.ly, geo.lz
    spots, _ = places(geo)
    row, lane = iota((ly, lz), 0), iota((ly, lz), 1)
    index_x, index_y, index_z = (lax.axis_index(name) for name in ("gx", "gy", "gz"))
    regions, terms = tables.shape[1], visco.shape[0]
    odd = (index_x & 1) == 1

    lay = layout(geo)

    def of(code, at):
        array, start, _ = where[code]
        return blocks[array][start + at]

    def along_x(step, at):
        target = geo.beside(0, step, index_x)
        if not geo.full:
            return of((target, 0), at)
        value = None
        for code in {geo.beside(0, step, index) for index in range(geo.gx)}:
            found = of((code, 0), at)
            value = found if value is None else jnp.where(target == code, found, value)
        return value

    def rows_along_y(at):
        if not geo.full:
            return of((0, 1), lay.old + at)[:1], of((0, geo.by - 1), lay.old + at)[ly - 1 :]
        if geo.gy == 1:
            return 0.0, 0.0
        facing = of((0, 1), lay.rows + at // ly)[at % ly : at % ly + 1]
        return facing, facing

    for i in range(lx):
        grad = []
        for a in range(3):
            at = lay.old + a * lx + i
            value = of((0, 0), at)
            next_x = of((0, 0), at + 1) if i + 1 < lx else along_x(1, at + 1 - lx)
            prev_x = of((0, 0), at - 1) if i else along_x(-1, at + lx - 1)
            after, before = rows_along_y(a * lx + i)
            first = jnp.where(index_y == geo.gy - 1, 0.0, after)
            last = jnp.where(index_y == 0, 0.0, before)
            next_y = pltpu.roll(jnp.where(row == 0, first, value), ly - 1, 0)
            prev_y = pltpu.roll(jnp.where(row == ly - 1, last, value), 1, 0)
            tile, centre = spots[(WIDE + a) * lx + i]
            left, right = halos[0][0, tile], halos[1][0, tile]
            if geo.split:
                left, right = jnp.where(odd, right, left), jnp.where(odd, left, right)
            right = jnp.where(index_z == geo.gz - 1, 0.0, pltpu.roll(right, lz - 1 - centre, 1))
            left = jnp.where(index_z == 0, 0.0, pltpu.roll(left, lz + 1 - centre, 1))
            next_z = jnp.where(lane == lz - 1, right, pltpu.roll(value, lz - 1, 1))
            prev_z = jnp.where(lane == 0, left, pltpu.roll(value, 1, 1))
            grad.append([0.5 * (next_x - prev_x), 0.5 * (next_y - prev_y), 0.5 * (next_z - prev_z)])
        dev_old = deviator(grad)
        dev_new = [dev_own[k, i] for k in range(6)]
        label = of((0, 0), 4 * lx + i)
        masks = [label == r for r in range(regions - 1)]
        shear_cells, ratio_cells, scale_cells = [lookup(tables, entry, masks) for entry in (SHEAR, RATIO, SCALE)]
        energy = shear_cells * contract(dev_new)
        energy_after = jnp.maximum(of((0, 0), 3 * lx + i), energy)
        energy_next[i] = energy_after
        softening = soften(energy, energy_after, scale_cells, ratio_cells)
        jump = [2.0 * shear_cells * (dev_new[k] - dev_old[k]) for k in range(6)]
        totals, long_term = [0.0] * 6, 1.0
        for term in range(terms):
            modulus = lookup(tables, MODULI + term, masks)
            time = lookup(tables, MODULI + terms + term, masks)
            decay = jnp.exp(-1.0 / time)
            weight = modulus * (1.0 - decay) * time
            long_term = long_term - modulus
            for k in range(6):
                value = decay * visco[term, k, i] + weight * jump[k]
                visco_next[term, k, i] = value
                totals[k] = totals[k] + value
        for k in range(6):
            stress[k, i] = softening * (long_term * 2.0 * shear_cells * dev_new[k] + totals[k])


def solve_kernel(geo, basis, *refs):
    grams, damage, residual = refs[:-2], refs[-2], refs[-1]
    total = functools.reduce(jnp.add, [part[...] for part in grams])
    column = jnp.sum(total, axis=1, keepdims=True)
    gram = {}
    for k, (i, j) in enumerate(PAIRS):
        gram[i, j] = gram[j, i] = column[k : k + 1]

    def image_of(p):
        out = [(1.0 + LENGTH_SQUARED * SHIFTS[j]) * p[j] for j in range(len(p))]
        out.append(LENGTH_SQUARED * p[-1])
        for j in range(1, len(p)):
            out[j] = out[j] + LENGTH_SQUARED * p[j - 1]
        return out

    def tree(values):
        while len(values) > 1:
            paired = [a + b for a, b in zip(values[::2], values[1::2])]
            values = paired + values[2 * len(paired) :]
        return values[0]

    def product(u, v):
        return tree([u[i] * v[j] * gram[i, j] for i in range(len(u)) for j in range(len(v))])

    one = jnp.ones((1, 1), jnp.float32)
    field, rest, direction = [], [one], [one]
    norm_now = gram[0, 0]
    for iteration in range(ITERS):
        image = image_of(direction)
        alpha = norm_now / product(image, direction)
        field = [x + alpha * d for x, d in zip(field, direction)] + [alpha * direction[-1]]
        rest = [r - alpha * w for r, w in zip(rest, image)] + [-alpha * image[-1]]
        if iteration + 1 < ITERS:
            norm_next = product(rest, rest)
            beta = norm_next / norm_now
            direction = [r + beta * d for r, d in zip(rest, direction)] + [rest[-1]]
            norm_now = norm_next
    for i in range(geo.lx):
        vectors = [basis[j, i] for j in range(ITERS + 1)]
        damage[i] = functools.reduce(jnp.add, [c * t for c, t in zip(field, vectors)])
        residual[i] = functools.reduce(jnp.add, [c * t for c, t in zip(rest, vectors)])


def shaped(*shape):
    return jax.ShapeDtypeStruct(shape, jnp.float32)


def call(kernel, outs, arrays, scratch=(), flops=0, parameters=(), moved=None):
    if moved is None:
        moved = 4 * sum(int(np.prod(a.shape)) for a in list(arrays) + list(outs))
    smem, vmem = pl.BlockSpec(memory_space=pltpu.SMEM), pl.BlockSpec(memory_space=pltpu.VMEM)
    return pl.pallas_call(
        kernel,
        out_shape=outs,
        in_specs=[smem] * len(parameters) + [vmem] * len(arrays),
        out_specs=[vmem] * len(outs),
        scratch_shapes=list(scratch),
        compiler_params=pltpu.CompilerParams(vmem_limit_bytes=32 * MB),
        cost_estimate=pl.CostEstimate(flops=flops, bytes_accessed=moved, transcendentals=0),
    )(*parameters, *arrays)


def moved(shard, axis, target):
    return lax.ppermute(shard, axis, [(i, target(i)) for i in range(lax.axis_size(axis))])


def ring(shard, axis, hops):
    count = lax.axis_size(axis)
    steps = list(range(hops + 1)) + list(range(-hops, 0))
    return jnp.stack([moved(shard, axis, lambda i: (i - step) % count) if step else shard for step in steps])


def assemble_kernel(*refs):
    parts, blocks = refs[:-1], refs[-1]
    start = 0
    for part in parts:
        blocks[start : start + part.shape[0]] = part[...]
        start += part.shape[0]


def slabs_kernel(geo, places_of, *refs):
    arrays, slabs = refs[:-1], refs[-1]
    lay = layout(geo)
    for array, start, edge in places_of:
        slabs[edge] = arrays[array][start + lay.edges : start + lay.rows]


def gathered(payloads, geo):
    lay, plane = layout(geo), payloads[0].shape[1:]
    if not geo.full:
        blocks = ring(ring(payloads[0], "gy", geo.hops_y), "gx", geo.hops_x)
        blocks = blocks.reshape((geo.bx * geo.by, lay.size) + plane)
        order = [(x, y) for x in range(geo.bx) for y in range(geo.by)]
        where = {code: Place(0, n * lay.size, n) for n, code in enumerate(order)}
        slabs = blocks[:, lay.edges : lay.rows]
        edges = [moved(slabs, "gz", lambda i: (i + step) % geo.gz) for step in (1, -1)]
        return edges + [blocks.reshape((-1,) + plane)], where
    whole, with_rows, plain = payloads
    relays = {geo.beside(0, step, index) & ~1 for step in (1, -1) for index in range(geo.gx)}
    codes = [(0, 0)] + [(x, y) for x in range(0, geo.gx, 2) for y in range(geo.gy) if x or y][::-1]
    parts = [whole]
    for x, y in codes[1:]:
        payload = whole if not y and x in relays else with_rows if not x else plain
        parts.append(moved(payload, ("gx", "gy"), lambda i: (i // geo.gy ^ x) * geo.gy + (i % geo.gy ^ y)))
    starts = np.cumsum([0] + [part.shape[0] for part in parts]).tolist()
    (blocks,) = call(assemble_kernel, [shaped(starts[-1], *plane)], parts)
    where = {code: Place(0, starts[n], n) for n, code in enumerate(codes)}
    arrays = [blocks]
    if geo.split:
        where.update({(x + 1, y): Place(1, starts[n], len(codes) + n) for n, (x, y) in enumerate(codes)})
        arrays.append(moved(blocks, "gx", lambda i: i ^ 1))
    (slabs,) = call(
        functools.partial(slabs_kernel, geo, tuple(where.values())),
        [shaped(len(where), lay.rows - lay.edges, *plane)],
        arrays,
    )
    if not geo.split:
        return [moved(slabs, "gz", lambda i: (i + step) % geo.gz) for step in (1, -1)] + arrays, where
    ring_of_gz = []
    for i in range(geo.gx * geo.gz):
        x, z = divmod(i, geo.gz)
        ahead = z + 1 - 2 * (x % 2)
        ring_of_gz.append((i, x * geo.gz + ahead if 0 <= ahead < geo.gz else (x ^ 1) * geo.gz + z))
    first = lax.ppermute(slabs, ("gx", "gz"), ring_of_gz)
    second = lax.ppermute(slabs, ("gx", "gz"), [(b, a) for a, b in ring_of_gz])
    return [first, second] + arrays, where


def summed(terms, axis):
    count = lax.axis_size(axis)
    if count not in (1, 2, 4):
        return [lax.psum(terms, axis)]
    return [terms] + [moved(terms, axis, lambda i: i ^ step) for step in reversed(range(1, count))]


def on_device(
    displacement,
    displacement_old,
    visco_state,
    energy_max,
    region,
    dirichlet,
    prony_moduli,
    prony_times,
    shear_modulus,
    mullins_ratio,
    mullins_scale,
):
    geo = geometry(energy_max.shape)
    lx, ly, lz = energy_max.shape
    regions, terms = prony_moduli.shape
    (zeros,) = call(first_kernel, [shaped(ly, lz)], [], flops=1 << 34, moved=0)
    lay = layout(geo)
    payloads = call(
        functools.partial(pack_kernel, geo),
        [shaped(size, ly, lz) for size in ((lay.size, lay.old, lay.rows) if geo.full else (lay.size,))],
        [zeros, displacement, displacement_old, energy_max, region, dirichlet],
    )
    (tables,) = call(
        tables_kernel,
        [shaped(MODULI + 2 * terms, regions, lz)],
        [],
        parameters=[prony_moduli, prony_times, shear_modulus, mullins_ratio, mullins_scale],
        flops=1 << 24,
    )
    blocks, where = gathered(payloads, geo)
    planes, rows = geo.bx * lx, geo.by * ly
    basis, dev_own, grams = call(
        functools.partial(basis_kernel, geo, where),
        [shaped(ITERS + 1, lx, ly, lz), shaped(6, lx, ly, lz), shaped(-(-len(PAIRS) // 8) * 8, lz)],
        [tables, *blocks],
        [
            pltpu.VMEM((3, planes, rows, 2 * lz), jnp.float32),
            pltpu.VMEM((ITERS + 1, planes, rows, 2 * lz), jnp.float32),
        ],
        flops=planes * rows * lz * 500,
    )
    if geo.full:
        sums = summed(grams, "gz")
    else:
        sums = [lax.psum(grams, ("gx", "gy", "gz"))]
    stress, visco_next, energy_next = call(
        functools.partial(visco_kernel, geo, where),
        [shaped(6, lx, ly, lz), shaped(*visco_state.shape), shaped(lx, ly, lz)],
        [tables, dev_own, visco_state, *blocks],
        flops=lx * ly * lz * 500,
    )
    damage_field, residual = call(
        functools.partial(solve_kernel, geo),
        [shaped(lx, ly, lz), shaped(lx, ly, lz)],
        [basis, *sums],
    )
    return (stress, visco_next, energy_next, damage_field, residual)


def solution(mesh):
    in_specs = (
        P(None, "gx", "gy", "gz"),
        P(None, "gx", "gy", "gz"),
        P(None, None, "gx", "gy", "gz"),
        P("gx", "gy", "gz"),
        P("gx", "gy", "gz"),
        P("gx", "gy", "gz"),
        P(),
        P(),
        P(),
        P(),
        P(),
    )
    out_specs = (
        P(None, "gx", "gy", "gz"),
        P(None, None, "gx", "gy", "gz"),
        P("gx", "gy", "gz"),
        P("gx", "gy", "gz"),
        P("gx", "gy", "gz"),
    )
    return jax.shard_map(
        on_device, mesh=mesh, in_specs=in_specs, out_specs=out_specs, check_vma=False
    )
```

```python
import functools
import typing

import jax
import jax.numpy as jnp
import numpy as np
from jax import lax
from jax.experimental import pallas as pl
from jax.experimental.pallas import tpu as pltpu
from jax.sharding import PartitionSpec as P

ITERS = 4
LENGTH_SQUARED = 4.0

SHIFTS = (0.0, 6.0, 1.5, 9.0)
PAIRS = [(i, j) for i in range(ITERS + 1) for j in range(i, ITERS + 1) if i < ITERS]

WIDE, NARROW = 5, 3
REACHES = (ITERS + 1,) * WIDE + (1,) * NARROW
FIELDS = WIDE + NARROW
MB = 1 << 20


class Geometry(typing.NamedTuple):
    lx: int
    ly: int
    lz: int
    gx: int
    gy: int
    gz: int
    hops_x: int
    hops_y: int
    full: bool

    @property
    def bx(self):
        return self.gx if self.full else 2 * self.hops_x + 1

    @property
    def by(self):
        return self.gy if self.full else 2 * self.hops_y + 1

    @property
    def split(self):
        return self.full and self.gx > 1

    def beside(self, code, step, index_x):
        if not self.full:
            return (code + step) % self.bx
        return (((index_x ^ code) + step) & (self.gx - 1)) ^ index_x


def geometry(block):
    lx, ly, lz = block
    gx, gy, gz = (lax.axis_size(name) for name in ("gx", "gy", "gz"))
    hops_x, hops_y = -(-(ITERS + 1) // lx), -(-(ITERS + 1) // ly)
    full = gx <= 2 * hops_x + 1 and not gx & (gx - 1) and gy <= 2
    return Geometry(lx, ly, lz, gx, gy, gz, hops_x, hops_y, full)


def places(geo):
    result, tile, at = [], 0, 0
    for reach in REACHES:
        for _ in range(geo.lx):
            if at + 2 * reach > geo.lz:
                tile, at = tile + 1, 0
            result.append((tile, at + reach))
            at += 2 * reach
    return result, tile + 1


class Layout(typing.NamedTuple):
    edges: int
    rows: int
    old: int
    size: int


def layout(geo):
    edges = WIDE * geo.lx
    rows = edges + places(geo)[1]
    old = rows - (-NARROW * geo.lx // geo.ly)
    return Layout(edges, rows, old, old + NARROW * geo.lx)


def iota(shape, dim):
    return lax.broadcasted_iota(jnp.int32, shape, dim)


def first_kernel(zeros):
    zeros[...] = jnp.zeros(zeros.shape, jnp.float32)


def pack_kernel(geo, zeros, new, old, energy_max, region, dirichlet, *payloads):
    spots, tiles = places(geo)
    lay = layout(geo)
    row, lane = iota((geo.ly, geo.lz), 0), iota((geo.ly, geo.lz), 1)
    top = lax.axis_index("gy") == 0
    edges, rows = [zeros[...]] * tiles, [zeros[...]] * (lay.old - lay.rows)

    def write(at, value):
        for payload in payloads:
            if at < payload.shape[0]:
                payload[at] = value

    for i in range(geo.lx):
        share = (1 - dirichlet[i]).astype(jnp.float32)
        values = [new[a, i] * share for a in range(3)]
        values += [energy_max[i], region[i].astype(jnp.float32)]
        values += [old[a, i] * share for a in range(3)]
        for f, value in enumerate(values):
            at = f * geo.lx + i
            tile, centre = spots[at]
            inside = (lane >= centre - REACHES[f]) & (lane < centre + REACHES[f])
            edges[tile] = jnp.where(inside, pltpu.roll(value, centre, 1), edges[tile])
            if f < WIDE:
                write(at, value)
                continue
            at -= WIDE * geo.lx
            write(lay.old + at, value)
            facing = jnp.where(top, value[geo.ly - 1 :], value[:1])
            rows[at // geo.ly] = jnp.where(row == at % geo.ly, facing, rows[at // geo.ly])
    for n, value in enumerate(edges + rows):
        write(lay.edges + n, value)


def tables_kernel(moduli, times, shear, ratio, scale, tables):
    regions, terms = moduli.shape
    for r in range(regions):
        entries = [shear[r], ratio[r], scale[r]]
        entries += [moduli[r, k] for k in range(terms)] + [times[r, k] for k in range(terms)]
        for k, entry in enumerate(entries):
            tables[k, r : r + 1, :] = jnp.full((1, tables.shape[2]), entry, jnp.float32)


SHEAR, RATIO, SCALE, MODULI = range(4)


def lookup(tables, entry, masks):
    value = tables[entry, len(masks) : len(masks) + 1, :]
    for r, mask in enumerate(masks):
        value = jnp.where(mask, tables[entry, r : r + 1, :], value)
    return value


def deviator(grad):
    trace_third = (grad[0][0] + grad[1][1] + grad[2][2]) / 3.0
    return [
        grad[0][0] - trace_third,
        grad[1][1] - trace_third,
        grad[2][2] - trace_third,
        0.5 * (grad[1][2] + grad[2][1]),
        0.5 * (grad[0][2] + grad[2][0]),
        0.5 * (grad[1][0] + grad[0][1]),
    ]


def contract(dev):
    return (
        dev[0] * dev[0]
        + dev[1] * dev[1]
        + dev[2] * dev[2]
        + 2.0 * (dev[3] * dev[3] + dev[4] * dev[4] + dev[5] * dev[5])
    )


def soften(energy, energy_next, scale, ratio):
    return 1.0 - lax.erf((energy_next - energy) / scale) / ratio


class Place(typing.NamedTuple):
    array: int
    start: int
    edge: int


def basis_kernel(geo, where, *refs):
    tables, halos, blocks = refs[0], refs[1:3], refs[3:-5]
    basis, dev_own, grams, held, field = refs[-5:]
    lx, ly, lz = geo.lx, geo.ly, geo.lz
    planes, rows, lanes = geo.bx * lx, geo.by * ly, 2 * lz
    regions = tables.shape[1]
    spots, _ = places(geo)
    row, lane = iota((rows, lanes), 0), iota((rows, lanes), 1)
    index_x, index_y, index_z = (lax.axis_index(name) for name in ("gx", "gy", "gz"))
    if geo.full:
        grid_row = jnp.where(row < ly, row + index_y * ly, row - index_y * ly)
    else:
        grid_row = index_y * ly + jnp.where(row < (1 + geo.hops_y) * ly, row, row - rows)
    end_y, start_y = grid_row == geo.gy * ly - 1, grid_row == 0
    end_z = (lane == lz - 1) & (index_z == geo.gz - 1)
    start_z = (lane == 0) & (index_z == 0)

    upward = (index_x & 1) == 0 if geo.split else True

    def next_plane(p):
        return p + 1 if p % lx + 1 < lx else geo.beside(p // lx, 1, index_x) * lx

    def prev_plane(p):
        return p - 1 if p % lx else geo.beside(p // lx, -1, index_x) * lx + lx - 1

    def whole_plane(f, p):
        tile, centre = spots[f * lx + p % lx]
        parts = []
        for b in range(geo.by):
            array, start, place = where[p // lx, b]
            first, second = halos[0][place, tile], halos[1][place, tile]
            edge = pltpu.roll(jnp.where((lane[:ly, :lz] < centre) ^ upward, second, first), lz - centre, 1)
            parts.append(jnp.concatenate([blocks[array][start + f * lx + p % lx], edge], axis=1))
        return jnp.concatenate(parts, axis=0)

    def beside(value):
        next_y = jnp.where(end_y, 0.0, pltpu.roll(value, rows - 1, 0))
        prev_y = jnp.where(start_y, 0.0, pltpu.roll(value, 1, 0))
        next_z = jnp.where(end_z, 0.0, pltpu.roll(value, lanes - 1, 1))
        prev_z = jnp.where(start_z, 0.0, pltpu.roll(value, 1, 1))
        return next_y, prev_y, next_z, prev_z

    for p in range(planes):
        for a in range(3):
            held[a, p] = whole_plane(a, p)
    for p in range(planes):
        grad = []
        for a in range(3):
            next_y, prev_y, next_z, prev_z = beside(held[a, p])
            next_x, prev_x = held[a, next_plane(p)], held[a, prev_plane(p)]
            grad.append([0.5 * (next_x - prev_x), 0.5 * (next_y - prev_y), 0.5 * (next_z - prev_z)])
        dev = deviator(grad)
        if p < lx:
            for k in range(6):
                dev_own[k, p] = dev[k][:ly, :lz]
        label = whole_plane(4, p)
        halves = []
        for half in (slice(0, lz), slice(lz, lanes)):
            masks = [label[:, half] == r for r in range(regions - 1)]
            halves.append([lookup(tables, entry, masks) for entry in (SHEAR, SCALE, RATIO)])
        shear_cells, scale_cells, ratio_cells = [jnp.concatenate(pair, axis=1) for pair in zip(*halves)]
        energy = shear_cells * contract(dev)
        energy_next = jnp.maximum(whole_plane(3, p), energy)
        softening = soften(energy, energy_next, scale_cells, ratio_cells)
        field[0, p] = softening * energy
    for j, shift in enumerate(SHIFTS):
        for p in range(planes):
            value = field[j, p]
            next_y, prev_y, next_z, prev_z = beside(value)
            next_x, prev_x = field[j, next_plane(p)], field[j, prev_plane(p)]
            image = (value - next_x) + (value - prev_x)
            image += (value - next_y) + (value - prev_y)
            image += (value - next_z) + (value - prev_z)
            field[j + 1, p] = image - shift * value if shift else image

    grams[...] = jnp.zeros(grams.shape, jnp.float32)
    sums = [jnp.zeros((ly, lz), jnp.float32)] * len(PAIRS)
    for p in range(planes if geo.full else lx):
        for b in range(geo.by if geo.full else 1):
            own = [field[j, p, b * ly : (b + 1) * ly, :lz] for j in range(ITERS + 1)]
            sums = [total + own[i] * own[j] for total, (i, j) in zip(sums, PAIRS)]
    for k, total in enumerate(sums):
        grams[k : k + 1, :] = jnp.sum(total, axis=0, keepdims=True)
    for i in range(lx):
        for j in range(ITERS + 1):
            basis[j, i] = field[j, i, :ly, :lz]


def visco_kernel(geo, where, *refs):
    tables, dev_own, visco, halos, blocks = refs[0], refs[1], refs[2], refs[3:5], refs[5:-3]
    stress, visco_next, energy_next = refs[-3:]
    lx, ly, lz = geo.lx, geo.ly, geo.lz
    spots, _ = places(geo)
    row, lane = iota((ly, lz), 0), iota((ly, lz), 1)
    index_x, index_y, index_z = (lax.axis_index(name) for name in ("gx", "gy", "gz"))
    regions, terms = tables.shape[1], visco.shape[0]
    odd = (index_x & 1) == 1

    lay = layout(geo)

    def of(code, at):
        array, start, _ = where[code]
        return blocks[array][start + at]

    def along_x(step, at):
        target = geo.beside(0, step, index_x)
        if not geo.full:
            return of((target, 0), at)
        value = None
        for code in {geo.beside(0, step, index) for index in range(geo.gx)}:
            found = of((code, 0), at)
            value = found if value is None else jnp.where(target == code, found, value)
        return value

    def rows_along_y(at):
        if not geo.full:
            return of((0, 1), lay.old + at)[:1], of((0, geo.by - 1), lay.old + at)[ly - 1 :]
        if geo.gy == 1:
            return 0.0, 0.0
        facing = of((0, 1), lay.rows + at // ly)[at % ly : at % ly + 1]
        return facing, facing

    for i in range(lx):
        grad = []
        for a in range(3):
            at = lay.old + a * lx + i
            value = of((0, 0), at)
            next_x = of((0, 0), at + 1) if i + 1 < lx else along_x(1, at + 1 - lx)
            prev_x = of((0, 0), at - 1) if i else along_x(-1, at + lx - 1)
            after, before = rows_along_y(a * lx + i)
            first = jnp.where(index_y == geo.gy - 1, 0.0, after)
            last = jnp.where(index_y == 0, 0.0, before)
            next_y = pltpu.roll(jnp.where(row == 0, first, value), ly - 1, 0)
            prev_y = pltpu.roll(jnp.where(row == ly - 1, last, value), 1, 0)
            tile, centre = spots[(WIDE + a) * lx + i]
            left, right = halos[0][0, tile], halos[1][0, tile]
            if geo.split:
                left, right = jnp.where(odd, right, left), jnp.where(odd, left, right)
            right = jnp.where(index_z == geo.gz - 1, 0.0, pltpu.roll(right, lz - 1 - centre, 1))
            left = jnp.where(index_z == 0, 0.0, pltpu.roll(left, lz + 1 - centre, 1))
            next_z = jnp.where(lane == lz - 1, right, pltpu.roll(value, lz - 1, 1))
            prev_z = jnp.where(lane == 0, left, pltpu.roll(value, 1, 1))
            grad.append([0.5 * (next_x - prev_x), 0.5 * (next_y - prev_y), 0.5 * (next_z - prev_z)])
        dev_old = deviator(grad)
        dev_new = [dev_own[k, i] for k in range(6)]
        label = of((0, 0), 4 * lx + i)
        masks = [label == r for r in range(regions - 1)]
        shear_cells, ratio_cells, scale_cells = [lookup(tables, entry, masks) for entry in (SHEAR, RATIO, SCALE)]
        energy = shear_cells * contract(dev_new)
        energy_after = jnp.maximum(of((0, 0), 3 * lx + i), energy)
        energy_next[i] = energy_after
        softening = soften(energy, energy_after, scale_cells, ratio_cells)
        jump = [2.0 * shear_cells * (dev_new[k] - dev_old[k]) for k in range(6)]
        totals, long_term = [0.0] * 6, 1.0
        for term in range(terms):
            modulus = lookup(tables, MODULI + term, masks)
            time = lookup(tables, MODULI + terms + term, masks)
            decay = jnp.exp(-1.0 / time)
            weight = modulus * (1.0 - decay) * time
            long_term = long_term - modulus
            for k in range(6):
                value = decay * visco[term, k, i] + weight * jump[k]
                visco_next[term, k, i] = value
                totals[k] = totals[k] + value
        for k in range(6):
            stress[k, i] = softening * (long_term * 2.0 * shear_cells * dev_new[k] + totals[k])


def solve_kernel(geo, basis, *refs):
    grams, damage, residual = refs[:-2], refs[-2], refs[-1]
    total = functools.reduce(jnp.add, [part[...] for part in grams])
    column = jnp.sum(total, axis=1, keepdims=True)
    gram = {}
    for k, (i, j) in enumerate(PAIRS):
        gram[i, j] = gram[j, i] = column[k : k + 1]

    def image_of(p):
        out = [(1.0 + LENGTH_SQUARED * SHIFTS[j]) * p[j] for j in range(len(p))]
        out.append(LENGTH_SQUARED * p[-1])
        for j in range(1, len(p)):
            out[j] = out[j] + LENGTH_SQUARED * p[j - 1]
        return out

    def tree(values):
        while len(values) > 1:
            paired = [a + b for a, b in zip(values[::2], values[1::2])]
            values = paired + values[2 * len(paired) :]
        return values[0]

    def product(u, v):
        return tree([u[i] * v[j] * gram[i, j] for i in range(len(u)) for j in range(len(v))])

    one = jnp.ones((1, 1), jnp.float32)
    field, rest, direction = [], [one], [one]
    norm_now = gram[0, 0]
    for iteration in range(ITERS):
        image = image_of(direction)
        alpha = norm_now / product(image, direction)
        field = [x + alpha * d for x, d in zip(field, direction)] + [alpha * direction[-1]]
        rest = [r - alpha * w for r, w in zip(rest, image)] + [-alpha * image[-1]]
        if iteration + 1 < ITERS:
            norm_next = product(rest, rest)
            beta = norm_next / norm_now
            direction = [r + beta * d for r, d in zip(rest, direction)] + [rest[-1]]
            norm_now = norm_next
    for i in range(geo.lx):
        vectors = [basis[j, i] for j in range(ITERS + 1)]
        damage[i] = functools.reduce(jnp.add, [c * t for c, t in zip(field, vectors)])
        residual[i] = functools.reduce(jnp.add, [c * t for c, t in zip(rest, vectors)])


def shaped(*shape):
    return jax.ShapeDtypeStruct(shape, jnp.float32)


def call(kernel, outs, arrays, scratch=(), flops=0, parameters=(), moved=None):
    if moved is None:
        moved = 4 * sum(int(np.prod(a.shape)) for a in list(arrays) + list(outs))
    smem, vmem = pl.BlockSpec(memory_space=pltpu.SMEM), pl.BlockSpec(memory_space=pltpu.VMEM)
    return pl.pallas_call(
        kernel,
        out_shape=outs,
        in_specs=[smem] * len(parameters) + [vmem] * len(arrays),
        out_specs=[vmem] * len(outs),
        scratch_shapes=list(scratch),
        compiler_params=pltpu.CompilerParams(vmem_limit_bytes=32 * MB),
        cost_estimate=pl.CostEstimate(flops=flops, bytes_accessed=moved, transcendentals=0),
    )(*parameters, *arrays)


def moved(shard, axis, target):
    return lax.ppermute(shard, axis, [(i, target(i)) for i in range(lax.axis_size(axis))])


def ring(shard, axis, hops):
    count = lax.axis_size(axis)
    steps = list(range(hops + 1)) + list(range(-hops, 0))
    return jnp.stack([moved(shard, axis, lambda i: (i - step) % count) if step else shard for step in steps])


def assemble_kernel(*refs):
    parts, blocks = refs[:-1], refs[-1]
    start = 0
    for part in parts:
        blocks[start : start + part.shape[0]] = part[...]
        start += part.shape[0]


def slabs_kernel(geo, places_of, *refs):
    arrays, slabs = refs[:-1], refs[-1]
    lay = layout(geo)
    for array, start, edge in places_of:
        slabs[edge] = arrays[array][start + lay.edges : start + lay.rows]


def gathered(payloads, geo):
    lay, plane = layout(geo), payloads[0].shape[1:]
    if not geo.full:
        blocks = ring(ring(payloads[0], "gy", geo.hops_y), "gx", geo.hops_x)
        blocks = blocks.reshape((geo.bx * geo.by, lay.size) + plane)
        order = [(x, y) for x in range(geo.bx) for y in range(geo.by)]
        where = {code: Place(0, n * lay.size, n) for n, code in enumerate(order)}
        slabs = blocks[:, lay.edges : lay.rows]
        edges = [moved(slabs, "gz", lambda i: (i + step) % geo.gz) for step in (1, -1)]
        return edges + [blocks.reshape((-1,) + plane)], where
    whole, with_rows, plain = payloads
    relays = {geo.beside(0, step, index) & ~1 for step in (1, -1) for index in range(geo.gx)}
    codes = [(0, 0)] + [(x, y) for x in range(0, geo.gx, 2) for y in range(geo.gy) if x or y][::-1]
    parts = [whole]
    for x, y in codes[1:]:
        payload = whole if not y and x in relays else with_rows if not x else plain
        parts.append(moved(payload, ("gx", "gy"), lambda i: (i // geo.gy ^ x) * geo.gy + (i % geo.gy ^ y)))
    starts = np.cumsum([0] + [part.shape[0] for part in parts]).tolist()
    (blocks,) = call(assemble_kernel, [shaped(starts[-1], *plane)], parts)
    where = {code: Place(0, starts[n], n) for n, code in enumerate(codes)}
    arrays = [blocks]
    if geo.split:
        where.update({(x + 1, y): Place(1, starts[n], len(codes) + n) for n, (x, y) in enumerate(codes)})
        arrays.append(moved(blocks, "gx", lambda i: i ^ 1))
    (slabs,) = call(
        functools.partial(slabs_kernel, geo, tuple(where.values())),
        [shaped(len(where), lay.rows - lay.edges, *plane)],
        arrays,
    )
    if not geo.split:
        return [moved(slabs, "gz", lambda i: (i + step) % geo.gz) for step in (1, -1)] + arrays, where
    ring_of_gz = []
    for i in range(geo.gx * geo.gz):
        x, z = divmod(i, geo.gz)
        ahead = z + 1 - 2 * (x % 2)
        ring_of_gz.append((i, x * geo.gz + ahead if 0 <= ahead < geo.gz else (x ^ 1) * geo.gz + z))
    first = lax.ppermute(slabs, ("gx", "gz"), ring_of_gz)
    second = lax.ppermute(slabs, ("gx", "gz"), [(b, a) for a, b in ring_of_gz])
    return [first, second] + arrays, where


def summed(terms, geo):
    if geo.gz not in (1, 2, 4):
        return [lax.psum(terms, "gz")]
    if geo.gz < 4 or not geo.split:
        return [terms] + [moved(terms, "gz", lambda i: i ^ step) for step in range(1, geo.gz)]
    first = moved(terms, ("gx", "gz"), lambda i: i ^ (3 if i // geo.gz % 2 else 1))
    second = moved(terms, "gz", lambda i: i ^ 2)
    return [terms, first, moved(first, "gx", lambda i: i ^ 1), second]


def on_device(
    displacement,
    displacement_old,
    visco_state,
    energy_max,
    region,
    dirichlet,
    prony_moduli,
    prony_times,
    shear_modulus,
    mullins_ratio,
    mullins_scale,
):
    geo = geometry(energy_max.shape)
    lx, ly, lz = energy_max.shape
    regions, terms = prony_moduli.shape
    (zeros,) = call(first_kernel, [shaped(ly, lz)], [], flops=1 << 34, moved=0)
    lay = layout(geo)
    payloads = call(
        functools.partial(pack_kernel, geo),
        [shaped(size, ly, lz) for size in ((lay.size, lay.old, lay.rows) if geo.full else (lay.size,))],
        [zeros, displacement, displacement_old, energy_max, region, dirichlet],
    )
    (tables,) = call(
        tables_kernel,
        [shaped(MODULI + 2 * terms, regions, lz)],
        [],
        parameters=[prony_moduli, prony_times, shear_modulus, mullins_ratio, mullins_scale],
        flops=1 << 24,
    )
    blocks, where = gathered(payloads, geo)
    planes, rows = geo.bx * lx, geo.by * ly
    basis, dev_own, grams = call(
        functools.partial(basis_kernel, geo, where),
        [shaped(ITERS + 1, lx, ly, lz), shaped(6, lx, ly, lz), shaped(-(-len(PAIRS) // 8) * 8, lz)],
        [tables, *blocks],
        [
            pltpu.VMEM((3, planes, rows, 2 * lz), jnp.float32),
            pltpu.VMEM((ITERS + 1, planes, rows, 2 * lz), jnp.float32),
        ],
        flops=planes * rows * lz * 500,
    )
    if geo.full:
        sums = summed(grams, geo)
    else:
        sums = [lax.psum(grams, ("gx", "gy", "gz"))]
    stress, visco_next, energy_next = call(
        functools.partial(visco_kernel, geo, where),
        [shaped(6, lx, ly, lz), shaped(*visco_state.shape), shaped(lx, ly, lz)],
        [tables, dev_own, visco_state, *blocks],
        flops=lx * ly * lz * 500,
    )
    damage_field, residual = call(
        functools.partial(solve_kernel, geo),
        [shaped(lx, ly, lz), shaped(lx, ly, lz)],
        [basis, *sums],
    )
    return (stress, visco_next, energy_next, damage_field, residual)


def solution(mesh):
    in_specs = (
        P(None, "gx", "gy", "gz"),
        P(None, "gx", "gy", "gz"),
        P(None, None, "gx", "gy", "gz"),
        P("gx", "gy", "gz"),
        P("gx", "gy", "gz"),
        P("gx", "gy", "gz"),
        P(),
        P(),
        P(),
        P(),
        P(),
    )
    out_specs = (
        P(None, "gx", "gy", "gz"),
        P(None, None, "gx", "gy", "gz"),
        P("gx", "gy", "gz"),
        P("gx", "gy", "gz"),
        P("gx", "gy", "gz"),
    )
    return jax.shard_map(
        on_device, mesh=mesh, in_specs=in_specs, out_specs=out_specs, check_vma=False
    )
```

```python
import functools
import typing

import jax
import jax.numpy as jnp
import numpy as np
from jax import lax
from jax.experimental import pallas as pl
from jax.experimental.pallas import tpu as pltpu
from jax.sharding import PartitionSpec as P

ITERS = 4
LENGTH_SQUARED = 4.0

SHIFTS = (0.0, 6.0, 1.5, 9.0)
PAIRS = [(i, j) for i in range(ITERS + 1) for j in range(i, ITERS + 1) if i < ITERS]

WIDE, NARROW = 5, 3
REACHES = (ITERS + 1,) * WIDE + (1,) * NARROW
FIELDS = WIDE + NARROW
MB = 1 << 20


class Geometry(typing.NamedTuple):
    lx: int
    ly: int
    lz: int
    gx: int
    gy: int
    gz: int
    hops_x: int
    hops_y: int
    full: bool

    @property
    def bx(self):
        return self.gx if self.full else 2 * self.hops_x + 1

    @property
    def by(self):
        return self.gy if self.full else 2 * self.hops_y + 1

    @property
    def split(self):
        return self.full and self.gx > 1

    def beside(self, code, step, index_x):
        if not self.full:
            return (code + step) % self.bx
        return (((index_x ^ code) + step) & (self.gx - 1)) ^ index_x


def geometry(block):
    lx, ly, lz = block
    gx, gy, gz = (lax.axis_size(name) for name in ("gx", "gy", "gz"))
    hops_x, hops_y = -(-(ITERS + 1) // lx), -(-(ITERS + 1) // ly)
    full = gx <= 2 * hops_x + 1 and not gx & (gx - 1) and gy <= 2
    return Geometry(lx, ly, lz, gx, gy, gz, hops_x, hops_y, full)


def places(geo):
    result, tile, at = [], 0, 0
    for reach in REACHES:
        for _ in range(geo.lx):
            if at + 2 * reach > geo.lz:
                tile, at = tile + 1, 0
            result.append((tile, at + reach))
            at += 2 * reach
    return result, tile + 1


class Layout(typing.NamedTuple):
    edges: int
    rows: int
    old: int
    size: int


def layout(geo):
    edges = WIDE * geo.lx
    rows = edges + places(geo)[1]
    old = rows - (-NARROW * geo.lx // geo.ly)
    return Layout(edges, rows, old, old + NARROW * geo.lx)


def iota(shape, dim):
    return lax.broadcasted_iota(jnp.int32, shape, dim)


def first_kernel(zeros):
    zeros[...] = jnp.zeros(zeros.shape, jnp.float32)


def pack_kernel(geo, zeros, new, old, energy_max, region, dirichlet, *payloads):
    spots, tiles = places(geo)
    lay = layout(geo)
    row, lane = iota((geo.ly, geo.lz), 0), iota((geo.ly, geo.lz), 1)
    top = lax.axis_index("gy") == 0
    edges, rows = [zeros[...]] * tiles, [zeros[...]] * (lay.old - lay.rows)

    def write(at, value):
        for payload in payloads:
            if at < payload.shape[0]:
                payload[at] = value

    for i in range(geo.lx):
        share = (1 - dirichlet[i]).astype(jnp.float32)
        values = [new[a, i] * share for a in range(3)]
        values += [energy_max[i], region[i].astype(jnp.float32)]
        values += [old[a, i] * share for a in range(3)]
        for f, value in enumerate(values):
            at = f * geo.lx + i
            tile, centre = spots[at]
            inside = (lane >= centre - REACHES[f]) & (lane < centre + REACHES[f])
            edges[tile] = jnp.where(inside, pltpu.roll(value, centre, 1), edges[tile])
            if f < WIDE:
                write(at, value)
                continue
            at -= WIDE * geo.lx
            write(lay.old + at, value)
            facing = jnp.where(top, value[geo.ly - 1 :], value[:1])
            rows[at // geo.ly] = jnp.where(row == at % geo.ly, facing, rows[at // geo.ly])
    for n, value in enumerate(edges + rows):
        write(lay.edges + n, value)


def tables_kernel(moduli, times, shear, ratio, scale, tables):
    regions, terms = moduli.shape
    for r in range(regions):

        def spread(entry):
            return jnp.full((1, tables.shape[2]), entry, jnp.float32)

        tables[SHEAR, r : r + 1, :] = spread(shear[r])
        tables[INVERSE_RATIO, r : r + 1, :] = spread(ratio[r])
        tables[INVERSE_SCALE, r : r + 1, :] = spread(scale[r])
        total = moduli[r, 0]
        for k in range(1, terms):
            total = total + moduli[r, k]
        tables[LONG_TERM, r : r + 1, :] = spread(1.0 - total)
        for k in range(terms):
            tables[DECAYS + k, r : r + 1, :] = spread(times[r, k])
            tables[DECAYS + terms + k, r : r + 1, :] = spread(moduli[r, k])
    tables[INVERSE_RATIO] = 1.0 / tables[INVERSE_RATIO]
    tables[INVERSE_SCALE] = 1.0 / tables[INVERSE_SCALE]
    for k in range(terms):
        time = tables[DECAYS + k]
        decay = jnp.exp(-1.0 / time)
        tables[DECAYS + k] = decay
        tables[DECAYS + terms + k] = tables[DECAYS + terms + k] * (1.0 - decay) * time


SHEAR, INVERSE_RATIO, INVERSE_SCALE, LONG_TERM, DECAYS = range(5)


def lookup(tables, entry, masks):
    value = tables[entry, len(masks) : len(masks) + 1, :]
    for r, mask in enumerate(masks):
        value = jnp.where(mask, tables[entry, r : r + 1, :], value)
    return value


def deviator(grad):
    trace_third = (grad[0][0] + grad[1][1] + grad[2][2]) * (1.0 / 3.0)
    return [
        grad[0][0] - trace_third,
        grad[1][1] - trace_third,
        grad[2][2] - trace_third,
        0.5 * (grad[1][2] + grad[2][1]),
        0.5 * (grad[0][2] + grad[2][0]),
        0.5 * (grad[1][0] + grad[0][1]),
    ]


def contract(dev):
    return (
        dev[0] * dev[0]
        + dev[1] * dev[1]
        + dev[2] * dev[2]
        + 2.0 * (dev[3] * dev[3] + dev[4] * dev[4] + dev[5] * dev[5])
    )


def soften(energy, energy_next, inverse_scale, inverse_ratio):
    return 1.0 - lax.erf((energy_next - energy) * inverse_scale) * inverse_ratio


class Place(typing.NamedTuple):
    array: int
    start: int
    edge: int


def basis_kernel(geo, where, *refs):
    tables, halos, blocks = refs[0], refs[1:3], refs[3:-5]
    basis, dev_own, grams, held, field = refs[-5:]
    lx, ly, lz = geo.lx, geo.ly, geo.lz
    planes, rows, lanes = geo.bx * lx, geo.by * ly, 2 * lz
    regions = tables.shape[1]
    spots, _ = places(geo)
    row, lane = iota((rows, lanes), 0), iota((rows, lanes), 1)
    index_x, index_y, index_z = (lax.axis_index(name) for name in ("gx", "gy", "gz"))
    if geo.full:
        grid_row = jnp.where(row < ly, row + index_y * ly, row - index_y * ly)
    else:
        grid_row = index_y * ly + jnp.where(row < (1 + geo.hops_y) * ly, row, row - rows)
    end_y, start_y = grid_row == geo.gy * ly - 1, grid_row == 0
    end_z = (lane == lz - 1) & (index_z == geo.gz - 1)
    start_z = (lane == 0) & (index_z == 0)

    upward = (index_x & 1) == 0 if geo.split else True

    def next_plane(p):
        return p + 1 if p % lx + 1 < lx else geo.beside(p // lx, 1, index_x) * lx

    def prev_plane(p):
        return p - 1 if p % lx else geo.beside(p // lx, -1, index_x) * lx + lx - 1

    def whole_plane(f, p):
        tile, centre = spots[f * lx + p % lx]
        parts = []
        for b in range(geo.by):
            array, start, place = where[p // lx, b]
            first, second = halos[0][place, tile], halos[1][place, tile]
            edge = pltpu.roll(jnp.where((lane[:ly, :lz] < centre) ^ upward, second, first), lz - centre, 1)
            parts.append(jnp.concatenate([blocks[array][start + f * lx + p % lx], edge], axis=1))
        return jnp.concatenate(parts, axis=0)

    def beside(value):
        next_y = jnp.where(end_y, 0.0, pltpu.roll(value, rows - 1, 0))
        prev_y = jnp.where(start_y, 0.0, pltpu.roll(value, 1, 0))
        next_z = jnp.where(end_z, 0.0, pltpu.roll(value, lanes - 1, 1))
        prev_z = jnp.where(start_z, 0.0, pltpu.roll(value, 1, 1))
        return next_y, prev_y, next_z, prev_z

    for p in range(planes):
        for a in range(3):
            held[a, p] = whole_plane(a, p)
    for p in range(planes):
        grad = []
        for a in range(3):
            next_y, prev_y, next_z, prev_z = beside(held[a, p])
            next_x, prev_x = held[a, next_plane(p)], held[a, prev_plane(p)]
            grad.append([next_x - prev_x, next_y - prev_y, next_z - prev_z])
        dev = deviator(grad)
        if p < lx:
            for k in range(6):
                dev_own[k, p] = 0.5 * dev[k][:ly, :lz]
        label = whole_plane(4, p)
        halves = []
        for half in (slice(0, lz), slice(lz, lanes)):
            masks = [label[:, half] == r for r in range(regions - 1)]
            halves.append([lookup(tables, entry, masks) for entry in (SHEAR, INVERSE_SCALE, INVERSE_RATIO)])
        shear_cells, scale_cells, ratio_cells = [jnp.concatenate(pair, axis=1) for pair in zip(*halves)]
        energy = 0.25 * shear_cells * contract(dev)
        energy_next = jnp.maximum(whole_plane(3, p), energy)
        softening = soften(energy, energy_next, scale_cells, ratio_cells)
        field[0, p] = softening * energy
    for j, shift in enumerate(SHIFTS):
        for p in range(planes):
            value = field[j, p]
            next_y, prev_y, next_z, prev_z = beside(value)
            next_x, prev_x = field[j, next_plane(p)], field[j, prev_plane(p)]
            image = (value - next_x) + (value - prev_x)
            image += (value - next_y) + (value - prev_y)
            image += (value - next_z) + (value - prev_z)
            field[j + 1, p] = image - shift * value if shift else image

    grams[...] = jnp.zeros(grams.shape, jnp.float32)
    sums = [jnp.zeros((ly, lz), jnp.float32)] * len(PAIRS)
    for p in range(planes if geo.full else lx):
        for b in range(geo.by if geo.full else 1):
            own = [field[j, p, b * ly : (b + 1) * ly, :lz] for j in range(ITERS + 1)]
            sums = [total + own[i] * own[j] for total, (i, j) in zip(sums, PAIRS)]
    for k, total in enumerate(sums):
        grams[k : k + 1, :] = jnp.sum(total, axis=0, keepdims=True)
    for i in range(lx):
        for j in range(ITERS + 1):
            basis[j, i] = field[j, i, :ly, :lz]


def visco_kernel(geo, where, *refs):
    tables, dev_own, visco, halos, blocks = refs[0], refs[1], refs[2], refs[3:5], refs[5:-3]
    stress, visco_next, energy_next = refs[-3:]
    lx, ly, lz = geo.lx, geo.ly, geo.lz
    spots, _ = places(geo)
    row, lane = iota((ly, lz), 0), iota((ly, lz), 1)
    index_x, index_y, index_z = (lax.axis_index(name) for name in ("gx", "gy", "gz"))
    regions, terms = tables.shape[1], visco.shape[0]
    odd = (index_x & 1) == 1

    lay = layout(geo)

    def of(code, at):
        array, start, _ = where[code]
        return blocks[array][start + at]

    def along_x(step, at):
        target = geo.beside(0, step, index_x)
        if not geo.full:
            return of((target, 0), at)
        value = None
        for code in {geo.beside(0, step, index) for index in range(geo.gx)}:
            found = of((code, 0), at)
            value = found if value is None else jnp.where(target == code, found, value)
        return value

    def rows_along_y(at):
        if not geo.full:
            return of((0, 1), lay.old + at)[:1], of((0, geo.by - 1), lay.old + at)[ly - 1 :]
        if geo.gy == 1:
            return 0.0, 0.0
        facing = of((0, 1), lay.rows + at // ly)[at % ly : at % ly + 1]
        return facing, facing

    for i in range(lx):
        grad = []
        for a in range(3):
            at = lay.old + a * lx + i
            value = of((0, 0), at)
            next_x = of((0, 0), at + 1) if i + 1 < lx else along_x(1, at + 1 - lx)
            prev_x = of((0, 0), at - 1) if i else along_x(-1, at + lx - 1)
            after, before = rows_along_y(a * lx + i)
            first = jnp.where(index_y == geo.gy - 1, 0.0, after)
            last = jnp.where(index_y == 0, 0.0, before)
            next_y = pltpu.roll(jnp.where(row == 0, first, value), ly - 1, 0)
            prev_y = pltpu.roll(jnp.where(row == ly - 1, last, value), 1, 0)
            tile, centre = spots[(WIDE + a) * lx + i]
            left, right = halos[0][0, tile], halos[1][0, tile]
            if geo.split:
                left, right = jnp.where(odd, right, left), jnp.where(odd, left, right)
            right = jnp.where(index_z == geo.gz - 1, 0.0, pltpu.roll(right, lz - 1 - centre, 1))
            left = jnp.where(index_z == 0, 0.0, pltpu.roll(left, lz + 1 - centre, 1))
            next_z = jnp.where(lane == lz - 1, right, pltpu.roll(value, lz - 1, 1))
            prev_z = jnp.where(lane == 0, left, pltpu.roll(value, 1, 1))
            grad.append([0.5 * (next_x - prev_x), 0.5 * (next_y - prev_y), 0.5 * (next_z - prev_z)])
        dev_old = deviator(grad)
        dev_new = [dev_own[k, i] for k in range(6)]
        label = of((0, 0), 4 * lx + i)
        masks = [label == r for r in range(regions - 1)]
        shear_cells, ratio_cells, scale_cells, long_term = [
            lookup(tables, entry, masks) for entry in (SHEAR, INVERSE_RATIO, INVERSE_SCALE, LONG_TERM)
        ]
        energy = shear_cells * contract(dev_new)
        energy_after = jnp.maximum(of((0, 0), 3 * lx + i), energy)
        energy_next[i] = energy_after
        softening = soften(energy, energy_after, scale_cells, ratio_cells)
        jump = [2.0 * shear_cells * (dev_new[k] - dev_old[k]) for k in range(6)]
        totals = [0.0] * 6
        for term in range(terms):
            decay = lookup(tables, DECAYS + term, masks)
            weight = lookup(tables, DECAYS + terms + term, masks)
            for k in range(6):
                value = decay * visco[term, k, i] + weight * jump[k]
                visco_next[term, k, i] = value
                totals[k] = totals[k] + value
        for k in range(6):
            stress[k, i] = softening * (long_term * 2.0 * shear_cells * dev_new[k] + totals[k])


def solve_kernel(geo, basis, *refs):
    grams, damage, residual = refs[:-2], refs[-2], refs[-1]
    total = functools.reduce(jnp.add, [part[...] for part in grams])
    column = jnp.sum(total, axis=1, keepdims=True)
    gram = {}
    for k, (i, j) in enumerate(PAIRS):
        gram[i, j] = gram[j, i] = column[k : k + 1]

    def image_of(p):
        out = [(1.0 + LENGTH_SQUARED * SHIFTS[j]) * p[j] for j in range(len(p))]
        out.append(LENGTH_SQUARED * p[-1])
        for j in range(1, len(p)):
            out[j] = out[j] + LENGTH_SQUARED * p[j - 1]
        return out

    def tree(values):
        while len(values) > 1:
            paired = [a + b for a, b in zip(values[::2], values[1::2])]
            values = paired + values[2 * len(paired) :]
        return values[0]

    def product(u, v):
        return tree([u[i] * v[j] * gram[i, j] for i in range(len(u)) for j in range(len(v))])

    one = jnp.ones((1, 1), jnp.float32)
    field, rest, direction = [], [one], [one]
    norm_now = gram[0, 0]
    for iteration in range(ITERS):
        image = image_of(direction)
        alpha = norm_now / product(image, direction)
        field = [x + alpha * d for x, d in zip(field, direction)] + [alpha * direction[-1]]
        rest = [r - alpha * w for r, w in zip(rest, image)] + [-alpha * image[-1]]
        if iteration + 1 < ITERS:
            norm_next = product(rest, rest)
            beta = norm_next / norm_now
            direction = [r + beta * d for r, d in zip(rest, direction)] + [rest[-1]]
            norm_now = norm_next
    for i in range(geo.lx):
        vectors = [basis[j, i] for j in range(ITERS + 1)]
        damage[i] = functools.reduce(jnp.add, [c * t for c, t in zip(field, vectors)])
        residual[i] = functools.reduce(jnp.add, [c * t for c, t in zip(rest, vectors)])


def shaped(*shape):
    return jax.ShapeDtypeStruct(shape, jnp.float32)


def call(kernel, outs, arrays, scratch=(), flops=0, parameters=(), moved=None):
    if moved is None:
        moved = 4 * sum(int(np.prod(a.shape)) for a in list(arrays) + list(outs))
    smem, vmem = pl.BlockSpec(memory_space=pltpu.SMEM), pl.BlockSpec(memory_space=pltpu.VMEM)
    return pl.pallas_call(
        kernel,
        out_shape=outs,
        in_specs=[smem] * len(parameters) + [vmem] * len(arrays),
        out_specs=[vmem] * len(outs),
        scratch_shapes=list(scratch),
        compiler_params=pltpu.CompilerParams(vmem_limit_bytes=32 * MB),
        cost_estimate=pl.CostEstimate(flops=flops, bytes_accessed=moved, transcendentals=0),
    )(*parameters, *arrays)


def moved(shard, axis, target):
    return lax.ppermute(shard, axis, [(i, target(i)) for i in range(lax.axis_size(axis))])


def ring(shard, axis, hops):
    count = lax.axis_size(axis)
    steps = list(range(hops + 1)) + list(range(-hops, 0))
    return jnp.stack([moved(shard, axis, lambda i: (i - step) % count) if step else shard for step in steps])


def assemble_kernel(*refs):
    parts, blocks = refs[:-1], refs[-1]
    start = 0
    for part in parts:
        blocks[start : start + part.shape[0]] = part[...]
        start += part.shape[0]


def slabs_kernel(geo, places_of, *refs):
    arrays, slabs = refs[:-1], refs[-1]
    lay = layout(geo)
    for array, start, edge in places_of:
        slabs[edge] = arrays[array][start + lay.edges : start + lay.rows]


def gathered(payloads, geo):
    lay, plane = layout(geo), payloads[0].shape[1:]
    if not geo.full:
        blocks = ring(ring(payloads[0], "gy", geo.hops_y), "gx", geo.hops_x)
        blocks = blocks.reshape((geo.bx * geo.by, lay.size) + plane)
        order = [(x, y) for x in range(geo.bx) for y in range(geo.by)]
        where = {code: Place(0, n * lay.size, n) for n, code in enumerate(order)}
        slabs = blocks[:, lay.edges : lay.rows]
        edges = [moved(slabs, "gz", lambda i: (i + step) % geo.gz) for step in (1, -1)]
        return edges + [blocks.reshape((-1,) + plane)], where
    whole, with_rows, plain = payloads
    relays = {geo.beside(0, step, index) & ~1 for step in (1, -1) for index in range(geo.gx)}
    codes = [(0, 0)] + [(x, y) for x in range(0, geo.gx, 2) for y in range(geo.gy) if x or y][::-1]
    parts = [whole]
    for x, y in codes[1:]:
        payload = whole if not y and x in relays else with_rows if not x else plain
        parts.append(moved(payload, ("gx", "gy"), lambda i: (i // geo.gy ^ x) * geo.gy + (i % geo.gy ^ y)))
    starts = np.cumsum([0] + [part.shape[0] for part in parts]).tolist()
    (blocks,) = call(assemble_kernel, [shaped(starts[-1], *plane)], parts)
    where = {code: Place(0, starts[n], n) for n, code in enumerate(codes)}
    arrays = [blocks]
    if geo.split:
        where.update({(x + 1, y): Place(1, starts[n], len(codes) + n) for n, (x, y) in enumerate(codes)})
        arrays.append(moved(blocks, "gx", lambda i: i ^ 1))
    (slabs,) = call(
        functools.partial(slabs_kernel, geo, tuple(where.values())),
        [shaped(len(where), lay.rows - lay.edges, *plane)],
        arrays,
    )
    if not geo.split:
        return [moved(slabs, "gz", lambda i: (i + step) % geo.gz) for step in (1, -1)] + arrays, where
    ring_of_gz = []
    for i in range(geo.gx * geo.gz):
        x, z = divmod(i, geo.gz)
        ahead = z + 1 - 2 * (x % 2)
        ring_of_gz.append((i, x * geo.gz + ahead if 0 <= ahead < geo.gz else (x ^ 1) * geo.gz + z))
    first = lax.ppermute(slabs, ("gx", "gz"), ring_of_gz)
    second = lax.ppermute(slabs, ("gx", "gz"), [(b, a) for a, b in ring_of_gz])
    return [first, second] + arrays, where


def summed(terms, geo):
    if geo.gz not in (1, 2, 4):
        return [lax.psum(terms, "gz")]
    if geo.gz < 4 or not geo.split:
        return [terms] + [moved(terms, "gz", lambda i: i ^ step) for step in range(1, geo.gz)]
    first = moved(terms, ("gx", "gz"), lambda i: i ^ (2 if i // geo.gz % 2 else 1))
    second = moved(terms, "gz", lambda i: i ^ 3)
    return [terms, first, moved(first, "gx", lambda i: i ^ 1), second]


def on_device(
    displacement,
    displacement_old,
    visco_state,
    energy_max,
    region,
    dirichlet,
    prony_moduli,
    prony_times,
    shear_modulus,
    mullins_ratio,
    mullins_scale,
):
    geo = geometry(energy_max.shape)
    lx, ly, lz = energy_max.shape
    regions, terms = prony_moduli.shape
    (zeros,) = call(first_kernel, [shaped(ly, lz)], [], flops=1 << 34, moved=0)
    lay = layout(geo)
    payloads = call(
        functools.partial(pack_kernel, geo),
        [shaped(size, ly, lz) for size in ((lay.size, lay.old, lay.rows) if geo.full else (lay.size,))],
        [zeros, displacement, displacement_old, energy_max, region, dirichlet],
    )
    (tables,) = call(
        tables_kernel,
        [shaped(DECAYS + 2 * terms, regions, lz)],
        [],
        parameters=[prony_moduli, prony_times, shear_modulus, mullins_ratio, mullins_scale],
        flops=1 << 24,
    )
    blocks, where = gathered(payloads, geo)
    planes, rows = geo.bx * lx, geo.by * ly
    basis, dev_own, grams = call(
        functools.partial(basis_kernel, geo, where),
        [shaped(ITERS + 1, lx, ly, lz), shaped(6, lx, ly, lz), shaped(-(-len(PAIRS) // 8) * 8, lz)],
        [tables, *blocks],
        [
            pltpu.VMEM((3, planes, rows, 2 * lz), jnp.float32),
            pltpu.VMEM((ITERS + 1, planes, rows, 2 * lz), jnp.float32),
        ],
        flops=planes * rows * lz * 500,
    )
    if geo.full:
        sums = summed(grams, geo)
    else:
        sums = [lax.psum(grams, ("gx", "gy", "gz"))]
    stress, visco_next, energy_next = call(
        functools.partial(visco_kernel, geo, where),
        [shaped(6, lx, ly, lz), shaped(*visco_state.shape), shaped(lx, ly, lz)],
        [tables, dev_own, visco_state, *blocks],
        flops=lx * ly * lz * 500,
    )
    damage_field, residual = call(
        functools.partial(solve_kernel, geo),
        [shaped(lx, ly, lz), shaped(lx, ly, lz)],
        [basis, *sums],
    )
    return (stress, visco_next, energy_next, damage_field, residual)


def solution(mesh):
    in_specs = (
        P(None, "gx", "gy", "gz"),
        P(None, "gx", "gy", "gz"),
        P(None, None, "gx", "gy", "gz"),
        P("gx", "gy", "gz"),
        P("gx", "gy", "gz"),
        P("gx", "gy", "gz"),
        P(),
        P(),
        P(),
        P(),
        P(),
    )
    out_specs = (
        P(None, "gx", "gy", "gz"),
        P(None, None, "gx", "gy", "gz"),
        P("gx", "gy", "gz"),
        P("gx", "gy", "gz"),
        P("gx", "gy", "gz"),
    )
    return jax.shard_map(
        on_device, mesh=mesh, in_specs=in_specs, out_specs=out_specs, check_vma=False
    )
```

```python
import functools
import typing

import jax
import jax.numpy as jnp
import numpy as np
from jax import lax
from jax.experimental import pallas as pl
from jax.experimental.pallas import tpu as pltpu
from jax.sharding import PartitionSpec as P

ITERS = 4
LENGTH_SQUARED = 4.0

SHIFTS = (0.0, 6.0, 1.5, 9.0)
PAIRS = [(i, j) for i in range(ITERS + 1) for j in range(i, ITERS + 1) if i < ITERS]

WIDE, NARROW = 5, 3
REACHES = (ITERS + 1,) * WIDE + (1,) * NARROW
FIELDS = WIDE + NARROW
MB = 1 << 20


class Geometry(typing.NamedTuple):
    lx: int
    ly: int
    lz: int
    gx: int
    gy: int
    gz: int
    hops_x: int
    hops_y: int
    full: bool

    @property
    def bx(self):
        return self.gx if self.full else 2 * self.hops_x + 1

    @property
    def by(self):
        return self.gy if self.full else 2 * self.hops_y + 1

    @property
    def split(self):
        return self.full and self.gx > 1

    def beside(self, code, step, index_x):
        if not self.full:
            return (code + step) % self.bx
        return (((index_x ^ code) + step) & (self.gx - 1)) ^ index_x


def geometry(block):
    lx, ly, lz = block
    gx, gy, gz = (lax.axis_size(name) for name in ("gx", "gy", "gz"))
    hops_x, hops_y = -(-(ITERS + 1) // lx), -(-(ITERS + 1) // ly)
    full = gx <= 2 * hops_x + 1 and not gx & (gx - 1) and gy <= 2
    return Geometry(lx, ly, lz, gx, gy, gz, hops_x, hops_y, full)


def places(geo):
    result, tile, at = [], 0, 0
    for reach in REACHES:
        for _ in range(geo.lx):
            if at + 2 * reach > geo.lz:
                tile, at = tile + 1, 0
            result.append((tile, at + reach))
            at += 2 * reach
    return result, tile + 1


def iota(shape, dim):
    return lax.broadcasted_iota(jnp.int32, shape, dim)


def first_kernel(zeros):
    zeros[...] = jnp.zeros(zeros.shape, jnp.float32)


def pack_kernel(geo, zeros, new, old, energy_max, region, dirichlet, payload):
    spots, tiles = places(geo)
    lane = iota((geo.ly, geo.lz), 1)
    edges = [zeros[...]] * tiles
    for i in range(geo.lx):
        share = (1 - dirichlet[i]).astype(jnp.float32)
        values = [new[a, i] * share for a in range(3)]
        values += [energy_max[i], region[i].astype(jnp.float32)]
        values += [old[a, i] * share for a in range(3)]
        for f, value in enumerate(values):
            payload[f * geo.lx + i] = value
            tile, centre = spots[f * geo.lx + i]
            inside = (lane >= centre - REACHES[f]) & (lane < centre + REACHES[f])
            edges[tile] = jnp.where(inside, pltpu.roll(value, centre, 1), edges[tile])
    for tile in range(tiles):
        payload[FIELDS * geo.lx + tile] = edges[tile]


def tables_kernel(moduli, times, shear, ratio, scale, tables):
    regions, terms = moduli.shape
    for r in range(regions):
        entries = [shear[r], ratio[r], scale[r]]
        entries += [moduli[r, k] for k in range(terms)] + [times[r, k] for k in range(terms)]
        for k, entry in enumerate(entries):
            tables[k, r : r + 1, :] = jnp.full((1, tables.shape[2]), entry, jnp.float32)


SHEAR, RATIO, SCALE, MODULI = range(4)


def lookup(tables, entry, masks):
    value = tables[entry, len(masks) : len(masks) + 1, :]
    for r, mask in enumerate(masks):
        value = jnp.where(mask, tables[entry, r : r + 1, :], value)
    return value


def deviator(grad):
    trace_third = (grad[0][0] + grad[1][1] + grad[2][2]) / 3.0
    return [
        grad[0][0] - trace_third,
        grad[1][1] - trace_third,
        grad[2][2] - trace_third,
        0.5 * (grad[1][2] + grad[2][1]),
        0.5 * (grad[0][2] + grad[2][0]),
        0.5 * (grad[1][0] + grad[0][1]),
    ]


def contract(dev):
    return (
        dev[0] * dev[0]
        + dev[1] * dev[1]
        + dev[2] * dev[2]
        + 2.0 * (dev[3] * dev[3] + dev[4] * dev[4] + dev[5] * dev[5])
    )


def soften(energy, energy_next, scale, ratio):
    return 1.0 - lax.erf((energy_next - energy) / scale) / ratio


def z_edges(geo, halos, array, at, tile):
    place = array * (halos[0].shape[0] // (2 if geo.split else 1)) + at
    return halos[0][place, tile], halos[1][place, tile]


def basis_kernel(geo, where, *refs):
    tables, halos, blocks = refs[0], refs[1:3], refs[3:-5]
    basis, dev_own, grams, held, field = refs[-5:]
    lx, ly, lz = geo.lx, geo.ly, geo.lz
    planes, rows, lanes = geo.bx * lx, geo.by * ly, 2 * lz
    regions = tables.shape[1]
    spots, _ = places(geo)
    row, lane = iota((rows, lanes), 0), iota((rows, lanes), 1)
    index_x, index_y, index_z = (lax.axis_index(name) for name in ("gx", "gy", "gz"))
    if geo.full:
        grid_row = jnp.where(row < ly, row + index_y * ly, row - index_y * ly)
    else:
        grid_row = index_y * ly + jnp.where(row < (1 + geo.hops_y) * ly, row, row - rows)
    end_y, start_y = grid_row == geo.gy * ly - 1, grid_row == 0
    end_z = (lane == lz - 1) & (index_z == geo.gz - 1)
    start_z = (lane == 0) & (index_z == 0)

    upward = (index_x & 1) == 0 if geo.split else True

    def next_plane(p):
        return p + 1 if p % lx + 1 < lx else geo.beside(p // lx, 1, index_x) * lx

    def prev_plane(p):
        return p - 1 if p % lx else geo.beside(p // lx, -1, index_x) * lx + lx - 1

    def whole_plane(f, p):
        tile, centre = spots[f * lx + p % lx]
        parts = []
        for b in range(geo.by):
            array, at = where[p // lx, b]
            first, second = z_edges(geo, halos, array, at, tile)
            edge = pltpu.roll(jnp.where((lane[:ly, :lz] < centre) ^ upward, second, first), lz - centre, 1)
            parts.append(jnp.concatenate([blocks[array][at, f * lx + p % lx], edge], axis=1))
        return jnp.concatenate(parts, axis=0)

    def beside(value):
        next_y = jnp.where(end_y, 0.0, pltpu.roll(value, rows - 1, 0))
        prev_y = jnp.where(start_y, 0.0, pltpu.roll(value, 1, 0))
        next_z = jnp.where(end_z, 0.0, pltpu.roll(value, lanes - 1, 1))
        prev_z = jnp.where(start_z, 0.0, pltpu.roll(value, 1, 1))
        return next_y, prev_y, next_z, prev_z

    for p in range(planes):
        for a in range(3):
            held[a, p] = whole_plane(a, p)
    for p in range(planes):
        grad = []
        for a in range(3):
            next_y, prev_y, next_z, prev_z = beside(held[a, p])
            next_x, prev_x = held[a, next_plane(p)], held[a, prev_plane(p)]
            grad.append([0.5 * (next_x - prev_x), 0.5 * (next_y - prev_y), 0.5 * (next_z - prev_z)])
        dev = deviator(grad)
        if p < lx:
            for k in range(6):
                dev_own[k, p] = dev[k][:ly, :lz]
        label = whole_plane(4, p)
        halves = []
        for half in (slice(0, lz), slice(lz, lanes)):
            masks = [label[:, half] == r for r in range(regions - 1)]
            halves.append([lookup(tables, entry, masks) for entry in (SHEAR, SCALE, RATIO)])
        shear_cells, scale_cells, ratio_cells = [jnp.concatenate(pair, axis=1) for pair in zip(*halves)]
        energy = shear_cells * contract(dev)
        energy_next = jnp.maximum(whole_plane(3, p), energy)
        softening = soften(energy, energy_next, scale_cells, ratio_cells)
        field[0, p] = softening * energy
    for j, shift in enumerate(SHIFTS):
        for p in range(planes):
            value = field[j, p]
            next_y, prev_y, next_z, prev_z = beside(value)
            next_x, prev_x = field[j, next_plane(p)], field[j, prev_plane(p)]
            image = (value - next_x) + (value - prev_x)
            image += (value - next_y) + (value - prev_y)
            image += (value - next_z) + (value - prev_z)
            field[j + 1, p] = image - shift * value if shift else image

    grams[...] = jnp.zeros(grams.shape, jnp.float32)
    sums = [jnp.zeros((ly, lz), jnp.float32)] * len(PAIRS)
    for p in range(planes if geo.full else lx):
        for b in range(geo.by if geo.full else 1):
            own = [field[j, p, b * ly : (b + 1) * ly, :lz] for j in range(ITERS + 1)]
            sums = [total + own[i] * own[j] for total, (i, j) in zip(sums, PAIRS)]
    for k, total in enumerate(sums):
        grams[k : k + 1, :] = jnp.sum(total, axis=0, keepdims=True)
    for i in range(lx):
        for j in range(ITERS + 1):
            basis[j, i] = field[j, i, :ly, :lz]


def visco_kernel(geo, where, *refs):
    tables, dev_own, visco, halos, blocks = refs[0], refs[1], refs[2], refs[3:5], refs[5:-3]
    stress, visco_next, energy_next = refs[-3:]
    lx, ly, lz = geo.lx, geo.ly, geo.lz
    spots, _ = places(geo)
    row, lane = iota((ly, lz), 0), iota((ly, lz), 1)
    index_x, index_y, index_z = (lax.axis_index(name) for name in ("gx", "gy", "gz"))
    regions, terms = tables.shape[1], visco.shape[0]
    odd = (index_x & 1) == 1

    def own(at, code_y=0):
        array, place = where[0, code_y % geo.by]
        return blocks[array][place, at]

    def along_x(step, at):
        target = geo.beside(0, step, index_x)
        if not geo.full:
            array, place = where[target, 0]
            return blocks[array][place, at]
        value = None
        for code in {geo.beside(0, step, index) for index in range(geo.gx)}:
            array, place = where[code, 0]
            found = blocks[array][place, at]
            value = found if value is None else jnp.where(target == code, found, value)
        return value

    for i in range(lx):
        grad = []
        for a in range(3):
            at = (WIDE + a) * lx + i
            value = own(at)
            next_x = own(at + 1) if i + 1 < lx else along_x(1, at + 1 - lx)
            prev_x = own(at - 1) if i else along_x(-1, at + lx - 1)
            first = jnp.where(index_y == geo.gy - 1, 0.0, own(at, 1))
            last = jnp.where(index_y == 0, 0.0, own(at, -1))
            next_y = pltpu.roll(jnp.where(row == 0, first, value), ly - 1, 0)
            prev_y = pltpu.roll(jnp.where(row == ly - 1, last, value), 1, 0)
            tile, centre = spots[at]
            left, right = z_edges(geo, halos, 0, 0, tile)
            if geo.split:
                left, right = jnp.where(odd, right, left), jnp.where(odd, left, right)
            right = jnp.where(index_z == geo.gz - 1, 0.0, pltpu.roll(right, lz - 1 - centre, 1))
            left = jnp.where(index_z == 0, 0.0, pltpu.roll(left, lz + 1 - centre, 1))
            next_z = jnp.where(lane == lz - 1, right, pltpu.roll(value, lz - 1, 1))
            prev_z = jnp.where(lane == 0, left, pltpu.roll(value, 1, 1))
            grad.append([0.5 * (next_x - prev_x), 0.5 * (next_y - prev_y), 0.5 * (next_z - prev_z)])
        dev_old = deviator(grad)
        dev_new = [dev_own[k, i] for k in range(6)]
        label = own(4 * lx + i)
        masks = [label == r for r in range(regions - 1)]
        shear_cells, ratio_cells, scale_cells = [lookup(tables, entry, masks) for entry in (SHEAR, RATIO, SCALE)]
        energy = shear_cells * contract(dev_new)
        energy_after = jnp.maximum(own(3 * lx + i), energy)
        energy_next[i] = energy_after
        softening = soften(energy, energy_after, scale_cells, ratio_cells)
        jump = [2.0 * shear_cells * (dev_new[k] - dev_old[k]) for k in range(6)]
        totals, long_term = [0.0] * 6, 1.0
        for term in range(terms):
            modulus = lookup(tables, MODULI + term, masks)
            time = lookup(tables, MODULI + terms + term, masks)
            decay = jnp.exp(-1.0 / time)
            weight = modulus * (1.0 - decay) * time
            long_term = long_term - modulus
            for k in range(6):
                value = decay * visco[term, k, i] + weight * jump[k]
                visco_next[term, k, i] = value
                totals[k] = totals[k] + value
        for k in range(6):
            stress[k, i] = softening * (long_term * 2.0 * shear_cells * dev_new[k] + totals[k])


def solve_kernel(geo, basis, *refs):
    grams, damage, residual = refs[:-2], refs[-2], refs[-1]
    total = functools.reduce(jnp.add, [part[...] for part in grams])
    column = jnp.sum(total, axis=1, keepdims=True)
    gram = {}
    for k, (i, j) in enumerate(PAIRS):
        gram[i, j] = gram[j, i] = column[k : k + 1]

    def image_of(p):
        out = [(1.0 + LENGTH_SQUARED * SHIFTS[j]) * p[j] for j in range(len(p))]
        out.append(LENGTH_SQUARED * p[-1])
        for j in range(1, len(p)):
            out[j] = out[j] + LENGTH_SQUARED * p[j - 1]
        return out

    def product(u, v):
        value = None
        for i in range(len(u)):
            inner = None
            for j in range(len(v)):
                inner = gram[i, j] * v[j] if inner is None else inner + gram[i, j] * v[j]
            value = u[i] * inner if value is None else value + u[i] * inner
        return value

    one = jnp.ones((1, 1), jnp.float32)
    field, rest, direction = [], [one], [one]
    norm_now = gram[0, 0]
    for iteration in range(ITERS):
        image = image_of(direction)
        alpha = norm_now / product(image, direction)
        field = [x + alpha * d for x, d in zip(field, direction)] + [alpha * direction[-1]]
        rest = [r - alpha * w for r, w in zip(rest, image)] + [-alpha * image[-1]]
        if iteration + 1 < ITERS:
            norm_next = product(rest, rest)
            beta = norm_next / norm_now
            direction = [r + beta * d for r, d in zip(rest, direction)] + [rest[-1]]
            norm_now = norm_next
    for i in range(geo.lx):
        vectors = [basis[j, i] for j in range(ITERS + 1)]
        damage[i] = functools.reduce(jnp.add, [c * t for c, t in zip(field, vectors)])
        residual[i] = functools.reduce(jnp.add, [c * t for c, t in zip(rest, vectors)])


def shaped(*shape):
    return jax.ShapeDtypeStruct(shape, jnp.float32)


def call(kernel, outs, arrays, scratch=(), flops=0, parameters=(), moved=None):
    if moved is None:
        moved = 4 * sum(int(np.prod(a.shape)) for a in list(arrays) + list(outs))
    smem, vmem = pl.BlockSpec(memory_space=pltpu.SMEM), pl.BlockSpec(memory_space=pltpu.VMEM)
    return pl.pallas_call(
        kernel,
        out_shape=outs,
        in_specs=[smem] * len(parameters) + [vmem] * len(arrays),
        out_specs=[vmem] * len(outs),
        scratch_shapes=list(scratch),
        compiler_params=pltpu.CompilerParams(vmem_limit_bytes=32 * MB),
        cost_estimate=pl.CostEstimate(flops=flops, bytes_accessed=moved, transcendentals=0),
    )(*parameters, *arrays)


def moved(shard, axis, target):
    return lax.ppermute(shard, axis, [(i, target(i)) for i in range(lax.axis_size(axis))])


def ring(shard, axis, hops):
    count = lax.axis_size(axis)
    steps = list(range(hops + 1)) + list(range(-hops, 0))
    return jnp.stack([moved(shard, axis, lambda i: (i - step) % count) if step else shard for step in steps])


def assemble_kernel(*refs):
    parts, blocks = refs[:-1], refs[-1]
    size = parts[0].shape[0]
    for n, part in enumerate(parts):
        blocks[n * size : (n + 1) * size] = part[...]


def slabs_kernel(geo, *refs):
    arrays, slabs = refs[:-1], refs[-1]
    place = 0
    for array in arrays:
        for n in range(array.shape[0]):
            slabs[place] = array[n, FIELDS * geo.lx :]
            place += 1


def gathered(payload, geo):
    if not geo.full:
        blocks = ring(ring(payload, "gy", geo.hops_y), "gx", geo.hops_x)
        blocks = blocks.reshape((geo.bx * geo.by,) + payload.shape)
        where = {(x, y): (0, x * geo.by + y) for x in range(geo.bx) for y in range(geo.by)}
        slabs = blocks[:, FIELDS * geo.lx :]
        return [moved(slabs, "gz", lambda i: (i + step) % geo.gz) for step in (1, -1)] + [blocks], where
    codes = [(0, 0)] + [(x, y) for x in range(0, geo.gx, 2) for y in range(geo.gy) if x or y][::-1]
    parts = [payload]
    for x, y in codes[1:]:
        parts.append(moved(payload, ("gx", "gy"), lambda i: (i // geo.gy ^ x) * geo.gy + (i % geo.gy ^ y)))
    size, plane = payload.shape[0], payload.shape[1:]
    (blocks,) = call(assemble_kernel, [shaped(len(parts) * size, *plane)], parts)
    where = {code: (0, place) for place, code in enumerate(codes)}
    arrays = [blocks.reshape((len(parts),) + payload.shape)]
    if geo.split:
        where.update({(x + 1, y): (1, place) for place, (x, y) in enumerate(codes)})
        arrays.append(moved(arrays[0], "gx", lambda i: i ^ 1))
    tiles = size - FIELDS * geo.lx
    (slabs,) = call(functools.partial(slabs_kernel, geo), [shaped(len(arrays) * len(parts), tiles, *plane)], arrays)
    if not geo.split:
        return [moved(slabs, "gz", lambda i: (i + step) % geo.gz) for step in (1, -1)] + arrays, where
    ring_of_gz = []
    for i in range(geo.gx * geo.gz):
        x, z = divmod(i, geo.gz)
        ahead = z + 1 - 2 * (x % 2)
        ring_of_gz.append((i, x * geo.gz + ahead if 0 <= ahead < geo.gz else (x ^ 1) * geo.gz + z))
    first = lax.ppermute(slabs, ("gx", "gz"), ring_of_gz)
    second = lax.ppermute(slabs, ("gx", "gz"), [(b, a) for a, b in ring_of_gz])
    return [first, second] + arrays, where


def summed(terms, axis):
    count = lax.axis_size(axis)
    if count not in (1, 2, 4):
        return [lax.psum(terms, axis)]
    return [terms] + [moved(terms, axis, lambda i: (i + step) % count) for step in range(1, count)]


def on_device(
    displacement,
    displacement_old,
    visco_state,
    energy_max,
    region,
    dirichlet,
    prony_moduli,
    prony_times,
    shear_modulus,
    mullins_ratio,
    mullins_scale,
):
    geo = geometry(energy_max.shape)
    lx, ly, lz = energy_max.shape
    _, tiles = places(geo)
    regions, terms = prony_moduli.shape
    (zeros,) = call(first_kernel, [shaped(ly, lz)], [], flops=1 << 34, moved=0)
    (payload,) = call(
        functools.partial(pack_kernel, geo),
        [shaped(FIELDS * lx + tiles, ly, lz)],
        [zeros, displacement, displacement_old, energy_max, region, dirichlet],
    )
    (tables,) = call(
        tables_kernel,
        [shaped(MODULI + 2 * terms, regions, lz)],
        [],
        parameters=[prony_moduli, prony_times, shear_modulus, mullins_ratio, mullins_scale],
        flops=1 << 24,
    )
    blocks, where = gathered(payload, geo)
    planes, rows = geo.bx * lx, geo.by * ly
    basis, dev_own, grams = call(
        functools.partial(basis_kernel, geo, where),
        [shaped(ITERS + 1, lx, ly, lz), shaped(6, lx, ly, lz), shaped(-(-len(PAIRS) // 8) * 8, lz)],
        [tables, *blocks],
        [
            pltpu.VMEM((3, planes, rows, 2 * lz), jnp.float32),
            pltpu.VMEM((ITERS + 1, planes, rows, 2 * lz), jnp.float32),
        ],
        flops=planes * rows * lz * 500,
    )
    if geo.full:
        sums = summed(grams, "gz")
    else:
        sums = [lax.psum(grams, ("gx", "gy", "gz"))]
    stress, visco_next, energy_next = call(
        functools.partial(visco_kernel, geo, where),
        [shaped(6, lx, ly, lz), shaped(*visco_state.shape), shaped(lx, ly, lz)],
        [tables, dev_own, visco_state, *blocks],
        flops=lx * ly * lz * 500,
    )
    damage_field, residual = call(
        functools.partial(solve_kernel, geo),
        [shaped(lx, ly, lz), shaped(lx, ly, lz)],
        [basis, *sums],
    )
    return (stress, visco_next, energy_next, damage_field, residual)


def solution(mesh):
    in_specs = (
        P(None, "gx", "gy", "gz"),
        P(None, "gx", "gy", "gz"),
        P(None, None, "gx", "gy", "gz"),
        P("gx", "gy", "gz"),
        P("gx", "gy", "gz"),
        P("gx", "gy", "gz"),
        P(),
        P(),
        P(),
        P(),
        P(),
    )
    out_specs = (
        P(None, "gx", "gy", "gz"),
        P(None, None, "gx", "gy", "gz"),
        P("gx", "gy", "gz"),
        P("gx", "gy", "gz"),
        P("gx", "gy", "gz"),
    )
    return jax.shard_map(
        on_device, mesh=mesh, in_specs=in_specs, out_specs=out_specs, check_vma=False
    )
```
